32 devices in a mesh: img: 4 (over y, x), ch: 8 (over z, core).
Axes of the slice: x: 2, y: 2, z: 4, core: 2. Of those that a mesh axis runs over, the one named last changes fastest.
Arguments:
- images_in: bfloat16 [256, 49, 2048], P('img'), may hold values from -6 to 6
- labels: int32 [256], P(('img', 'ch')), may hold values from 0 to 999
- loss_wt: int32 [256], P(('img', 'ch')), may hold values from 1 to 32
- placement: int32 [4, 64], P('img'), may hold values from 0 to 63, each once within a row
- w_one: float32 [2048, 512], P(None, 'ch'), may hold values from -0.125 to 0.125
- mom_one: float32 [2048, 512], P(None, 'ch'), may hold values from -0.0029296875 to 0.0029296875
- avg_one: float32 [2048, 512], P(None, 'ch'), may hold values from -0.125 to 0.125
- mask_one: int32 [2048, 512], P(None, 'ch'), may hold values 0 or 1
- rank_one: int32 [2048, 512], P(None, 'ch'), may hold values from 0 to 99
- first_norm_params: float32 [2, 512], P(None, 'ch'), may hold values from 0.5 to 1.5
- mom_bn_one: float32 [2, 512], P(None, 'ch'), may hold values from -0.001953125 to 0.001953125
- avg_bn_one: float32 [2, 512], P(None, 'ch'), may hold values from 0.5 to 1.5
- w_two: float32 [2359296], P(('img', 'ch')), may hold values from -0.09375 to 0.09375
- mom_two: float32 [2359296], P(('img', 'ch')), may hold values from -0.01171875 to 0.01171875
- avg_two: float32 [2359296], P(('img', 'ch')), may hold values from -0.09375 to 0.09375
- mask_two: int32 [2359296], P(('img', 'ch')), may hold values 0 or 1
- rank_two: int32 [2359296], P(('img', 'ch')), may hold values from 0 to 99
- second_norm_params: float32 [2, 512], replicated, may hold values from 0.5 to 1.5
- mom_bn_two: float32 [2, 512], replicated, may hold values from -0.01953125 to 0.01953125
- avg_bn_two: float32 [2, 512], replicated, may hold values from 0.5 to 1.5
- w_head: float32 [512000], P(('img', 'ch')), may hold values from -0.75 to 0.75
- mom_head: float32 [512000], P(('img', 'ch')), may hold values from -0.0029296875 to 0.0029296875
- avg_head: float32 [512000], P(('img', 'ch')), may hold values from -0.75 to 0.75
Outputs:
- loss: float32 [], replicated
- new_w_one: float32 [2048, 512], P(None, 'ch')
- new_mom_one: float32 [2048, 512], P(None, 'ch')
- new_avg_one: float32 [2048, 512], P(None, 'ch')
- new_mask_one: int32 [2048, 512], P(None, 'ch')
- copy_w_one: bfloat16 [2048, 512], P(None, 'ch')
- new_bn_one: float32 [2, 512], P(None, 'ch')
- new_mom_bn_one: float32 [2, 512], P(None, 'ch')
- new_avg_bn_one: float32 [2, 512], P(None, 'ch')
- new_w_two: float32 [2359296], P(('img', 'ch'))
- new_mom_two: float32 [2359296], P(('img', 'ch'))
- new_avg_two: float32 [2359296], P(('img', 'ch'))
- new_mask_two: int32 [2359296], P(('img', 'ch'))
- copy_w_two: bfloat16 [2359296], P(('img', 'ch'))
- new_bn_two: float32 [2, 512], replicated
- new_mom_bn_two: float32 [2, 512], replicated
- new_avg_bn_two: float32 [2, 512], replicated
- new_w_head: float32 [512000], P(('img', 'ch'))
- new_mom_head: float32 [512000], P(('img', 'ch'))
- new_avg_head: float32 [512000], P(('img', 'ch'))
- copy_w_head: bfloat16 [512000], P(('img', 'ch'))
The draws below stay inside these ranges and needn't reach their ends.
Inputs may be any that keep to these rules, and one draw needn't show every extreme that they name: `placement`: each row is a permutation of 0 to 63.
All inputs are finite; a program needn't handle non-finite values. No bound on the sum of `mask_one` or of `mask_two` on one device may be relied on, other than what follows from the above.
Results may differ from the reference program's by a relative error of at most 0.013.
Values may be sent and summed in bfloat16 or wider, within the bound.
A program may use at most 512 MiB of HBM per device.

```python
import math
import jax
import jax.numpy as jnp
import numpy as np
from jax import lax

CIN = 2048
CMID = 512
CLS = 1000
SIDE = 7
PIX = 49
DROP = 10
GROW = 10
RANKS = 100
IMG_GRP = 64
IMAGES = 256
N_IMG = 4


def touch_ends(array, stream_key, least, high):
    shape = array.shape
    place = [jax.random.randint(jax.random.fold_in(stream_key, axis), (), 0, shape[axis]) for axis in range(len(shape))]
    array = array.at[tuple(place)].set(least)
    longest = shape.index(max(shape))
    place[longest] = (place[longest] + 1) % shape[longest]
    return array.at[tuple(place)].set(high)


def levels(rng, dims, shards, low, high):
    def one(axis_at, blocks):
        steps = jax.random.uniform(jax.random.fold_in(jax.random.fold_in(rng, 6), axis_at), (blocks,), jnp.float32, low / len(shards), high / len(shards))
        return jnp.repeat(jnp.exp(steps), dims[axis_at] // blocks).reshape((-1,) + (1,) * (len(dims) - axis_at - 1))

    factor_of = one(*shards[0])
    for cut in shards[1:]:
        factor_of = factor_of * one(*cut)
    return factor_of


def rank_table(amount, skew):
    weights = [(1 << 20) // math.isqrt(rank ** skew) + 1 for rank in range(1, amount + 1)]
    deviation = 1 + sum(weights) // (1 << 30)
    return np.cumsum(np.array([max(1, weight // deviation) for weight in weights]))


def skewed_ids(key, shape, count, slope):
    listing = rank_table(count, slope)
    lot = jax.random.randint(jax.random.fold_in(key, 1), shape, 0, int(listing[count - 1]))
    standing = jnp.searchsorted(jnp.asarray(listing, jnp.int32), lot, side="right")
    return jax.random.permutation(jax.random.fold_in(key, 2), count)[standing].astype(jnp.int32)


def centred(own_key, extent, width, reach, pieces=(), kind=jnp.bfloat16):
    values = width * jax.random.normal(own_key, extent, jnp.float32)
    if pieces:
        values = values * levels(own_key, extent, pieces, -0.22, 0.18)
    return jnp.clip(values, -reach, reach).astype(kind)


def setup_inputs(seed: int = 0) -> dict:
    keys = jax.random.split(jax.random.key(seed), 24)
    images_in = centred(keys[0], (IMAGES, PIX, CIN), 1.0, 6.0, ((0, 4),))
    labels = touch_ends(skewed_ids(keys[1], (IMAGES,), CLS, 1), jax.random.fold_in(keys[1], 3), 0, CLS - 1).astype(jnp.int32)
    loss_wt = touch_ends(jax.random.randint(keys[2], (IMAGES,), 1, 33), jax.random.fold_in(keys[2], 1), 1, 32).astype(jnp.int32)
    placement = jax.vmap(lambda own: jax.random.permutation(own, IMG_GRP))(jax.random.split(keys[3], N_IMG)).reshape((N_IMG, IMG_GRP)).astype(jnp.int32)
    w_one = centred(keys[4], (CIN, CMID), CIN ** -0.5, 0.125, ((1, 8),), jnp.float32)
    mom_one = centred(keys[5], (CIN, CMID), (0.008 / IMAGES ** 0.5), 0.0029296875, ((1, 8),), jnp.float32)
    avg_one = centred(keys[6], (CIN, CMID), CIN ** -0.5, 0.125, ((1, 8),), jnp.float32)
    mask_one = touch_ends((jax.random.randint(keys[7], (CIN, CMID), 0, 2) < 1).astype(jnp.int32), jax.random.fold_in(keys[7], 1), 0, 1)
    rank_one = touch_ends(jax.random.randint(keys[8], (CIN, CMID), 0, RANKS), jax.random.fold_in(keys[8], 1), 0, RANKS - 1).astype(jnp.int32)
    first_norm_params = jnp.clip(0.5 + 1.0 * jax.random.uniform(keys[9], (2, CMID), jnp.float32) ** levels(keys[9], (2, CMID), ((1, 8),), -0.2, 0.2), 0.5, 1.5)
    mom_bn_one = centred(keys[10], (2, CMID), (0.006 / IMAGES ** 0.5), 0.001953125, ((1, 8),), jnp.float32)
    avg_bn_one = jnp.clip(0.5 + 1.0 * jax.random.uniform(keys[11], (2, CMID), jnp.float32) ** levels(keys[11], (2, CMID), ((1, 8),), -0.2, 0.2), 0.5, 1.5)
    w_two = centred(keys[12], (9 * CMID * CMID,), (9 * CMID) ** -0.5, 0.09375, ((0, 32),), jnp.float32)
    mom_two = centred(keys[13], (9 * CMID * CMID,), (0.03 / IMAGES ** 0.5), 0.01171875, ((0, 32),), jnp.float32)
    avg_two = centred(keys[14], (9 * CMID * CMID,), (9 * CMID) ** -0.5, 0.09375, ((0, 32),), jnp.float32)
    mask_two = touch_ends((jax.random.randint(keys[15], (9 * CMID * CMID,), 0, 2) < 1).astype(jnp.int32), jax.random.fold_in(keys[15], 1), 0, 1)
    rank_two = touch_ends(jax.random.randint(keys[16], (9 * CMID * CMID,), 0, RANKS), jax.random.fold_in(keys[16], 1), 0, RANKS - 1).astype(jnp.int32)
    second_norm_params = jnp.clip(jax.random.uniform(keys[17], (2, CMID), jnp.float32, 0.5, 1.5), 0.5, 1.5)
    mom_bn_two = centred(keys[18], (2, CMID), (0.05 / IMAGES ** 0.5), 0.01953125, (), jnp.float32)
    avg_bn_two = jnp.clip(jax.random.uniform(keys[19], (2, CMID), jnp.float32, 0.5, 1.5), 0.5, 1.5)
    w_head = centred(keys[20], (CMID * CLS,), 0.12, 0.75, ((0, 32),), jnp.float32)
    mom_head = centred(keys[21], (CMID * CLS,), (0.5 / CLS), 0.0029296875, ((0, 32),), jnp.float32)
    avg_head = centred(keys[22], (CMID * CLS,), 0.12, 0.75, ((0, 32),), jnp.float32)
    return dict(images_in=images_in, labels=labels, loss_wt=loss_wt, placement=placement, w_one=w_one, mom_one=mom_one, avg_one=avg_one, mask_one=mask_one, rank_one=rank_one, first_norm_params=first_norm_params, mom_bn_one=mom_bn_one, avg_bn_one=avg_bn_one, w_two=w_two, mom_two=mom_two, avg_two=avg_two, mask_two=mask_two, rank_two=rank_two, second_norm_params=second_norm_params, mom_bn_two=mom_bn_two, avg_bn_two=avg_bn_two, w_head=w_head, mom_head=mom_head, avg_head=avg_head)


@jax.custom_vjp
def reduced_precision(v):
    return lax.optimization_barrier(v.astype(jnp.bfloat16)).astype(jnp.float32)

@jax.custom_vjp
def reduced_precision_backward(v):
    return v

def low_keep(v):
    return (reduced_precision(v), None)

def low_pass(kept, grad):
    return (grad,)

def back_keep(v):
    return (v, None)

def back_low(kept, grad):
    return (reduced_precision(grad),)
reduced_precision.defvjp(low_keep, low_pass)
reduced_precision_backward.defvjp(back_keep, back_low)
EPS = 1e-05
MOMENTUM = 0.5
HIGH = lax.Precision.HIGHEST

def standardize_features(z):
    mean = lax.optimization_barrier(jnp.mean(z, axis=0))
    var = lax.optimization_barrier(jnp.mean(z * z, axis=0)) - mean * mean
    return (z - mean) * lax.rsqrt(var + EPS)

def forward(params, feats, mask_one, mask_two, labels, weights, total):
    w_one, first_norm_params, w_two, second_norm_params, w_head = params
    element_count = labels.shape[0]
    first_conv_output = reduced_precision_backward(jnp.dot(feats, reduced_precision(w_one * mask_one), precision=HIGH))
    first_standardized_input = standardize_features(first_conv_output)
    first_activation_map = reduced_precision_backward(reduced_precision(jax.nn.silu(first_norm_params[0] * first_standardized_input + first_norm_params[1])))
    kernel = reduced_precision(w_two * mask_two).reshape(3, 3, CMID, CMID)
    second_conv_output = lax.conv_general_dilated(first_activation_map.reshape(element_count, SIDE, SIDE, CMID), kernel, (1, 1), 'SAME', dimension_numbers=('NHWC', 'HWIO', 'NHWC'), precision=HIGH)
    second_conv_output = reduced_precision_backward(second_conv_output.reshape(element_count * PIX, CMID))
    second_standardized_input = standardize_features(second_conv_output)
    second_activation_map = jax.nn.silu(second_norm_params[0] * second_standardized_input + second_norm_params[1])
    pooled = lax.optimization_barrier(jnp.mean(second_activation_map.reshape(element_count, PIX, CMID), axis=1))
    logits = reduced_precision_backward(jnp.dot(reduced_precision(pooled), reduced_precision(w_head).reshape(CMID, CLS), precision=HIGH))
    lse = jax.nn.logsumexp(logits, axis=1)
    picked = lax.optimization_barrier(jnp.sum(jnp.where(labels[:, None] == jnp.arange(CLS)[None, :], logits, 0.0), axis=1))
    return jnp.sum(weights * (lse - picked)) / total

def advance(weight, grad, velocity, rate):
    velocity = MOMENTUM * velocity + grad
    return (weight - rate * (grad + MOMENTUM * velocity), velocity)

def dense_update(weight, grad, velocity, average, rate):
    moved, velocity = advance(weight, grad, velocity, rate)
    return (moved, velocity, 0.5 * average + 0.5 * moved)

def sparse_update(weight, grad, velocity, average, mask, rank, rate):
    moved, velocity = advance(weight, grad, velocity, rate)
    kept = (mask == 1) & (rank >= DROP)
    grown = (mask == 0) & (rank < GROW)
    new_mask = jnp.where(kept | grown, 1, 0).astype(jnp.int32)
    weight = jnp.where(kept, moved, 0.0)
    velocity = jnp.where(kept, velocity, 0.0)
    average = 0.5 * average + 0.5 * weight
    return (weight, velocity, average, new_mask, weight.astype(jnp.bfloat16))

def reference(images_in, labels, loss_wt, placement, w_one, mom_one, avg_one, mask_one, rank_one, first_norm_params, mom_bn_one, avg_bn_one, w_two, mom_two, avg_two, mask_two, rank_two, second_norm_params, mom_bn_two, avg_bn_two, w_head, mom_head, avg_head):
    source = (jnp.arange(N_IMG, dtype=jnp.int32)[:, None] * IMG_GRP + placement).reshape(-1).astype(jnp.int32)
    feats = images_in[source].astype(jnp.float32).reshape(IMAGES * PIX, CIN)
    weights = loss_wt.astype(jnp.float32)
    total = jnp.sum(weights)
    fmask_one = mask_one.astype(jnp.float32)
    fmask_two = mask_two.astype(jnp.float32)

    def loss_of(a, b, c, d, e):
        return forward((a, b, c, d, e), feats, fmask_one, fmask_two, labels, weights, total)
    loss, pullback = jax.vjp(loss_of, w_one, first_norm_params, w_two, second_norm_params, w_head)
    g_one, g_bn_one, g_two, g_bn_two, g_head = pullback(jnp.ones_like(loss))
    root = math.sqrt(IMAGES)
    one = sparse_update(w_one, g_one, mom_one, avg_one, mask_one, rank_one, 1.3 * root)
    bno = dense_update(first_norm_params, g_bn_one, mom_bn_one, avg_bn_one, 8.0 * root)
    two = sparse_update(w_two, g_two, mom_two, avg_two, mask_two, rank_two, 0.25 * root)
    bnt = dense_update(second_norm_params, g_bn_two, mom_bn_two, avg_bn_two, root)
    head = dense_update(w_head, g_head, mom_head, avg_head, 40.0)
    return (loss, one[0], one[1], one[2], one[3], one[4], bno[0], bno[1], bno[2], two[0], two[1], two[2], two[3], two[4], bnt[0], bnt[1], bnt[2], head[0], head[1], head[2], head[0].astype(jnp.bfloat16))
```

```python
import math

import jax
import jax.numpy as jnp
from jax import lax
from jax.sharding import PartitionSpec as P

SIDE = 7
PIX = 49
DROP = 10
GROW = 10


EPS = 1e-05
MOMENTUM = 0.5


def advance(weight, grad, velocity, rate):
    velocity = MOMENTUM * velocity + grad
    return (weight - rate * (grad + MOMENTUM * velocity), velocity)


def dense_update(weight, grad, velocity, average, rate):
    moved, velocity = advance(weight, grad, velocity, rate)
    return (moved, velocity, 0.5 * average + 0.5 * moved)


def sparse_update(weight, grad, velocity, average, mask, rank, rate):
    moved, velocity = advance(weight, grad, velocity, rate)
    kept = (mask == 1) & (rank >= DROP)
    grown = (mask == 0) & (rank < GROW)
    new_mask = jnp.where(kept | grown, 1, 0).astype(jnp.int32)
    weight = jnp.where(kept, moved, 0.0)
    velocity = jnp.where(kept, velocity, 0.0)
    average = 0.5 * average + 0.5 * weight
    return (weight, velocity, average, new_mask, weight.astype(jnp.bfloat16))


def silu_slope(value):
    sigma = jax.nn.sigmoid(value)
    return sigma * (1.0 + value * (1.0 - sigma))


def apply_batch_norm(z, sums, squares, element_count):
    mean = sums / element_count
    inverse_deviation = lax.rsqrt(squares / element_count - mean * mean + EPS)
    return ((z - mean) * inverse_deviation, inverse_deviation)


def batch_norm_backward(
    norm_gain,
    inverse_deviation,
    output_gradient,
    standardized_input,
    bias_gradient_sum,
    gain_gradient_sum,
    element_count,
):
    return (
        norm_gain
        * inverse_deviation
        * (
            output_gradient
            - bias_gradient_sum / element_count
            - standardized_input * gain_gradient_sum / element_count
        )
    )


def contract_rows(left, right):
    return jnp.einsum("pk,pc->kc", left, right, preferred_element_type=jnp.float32)


def shards(
    images_in,
    labels,
    loss_wt,
    placement,
    w_one,
    mom_one,
    avg_one,
    mask_one,
    rank_one,
    first_norm_params,
    mom_bn_one,
    avg_bn_one,
    w_two,
    mom_two,
    avg_two,
    mask_two,
    rank_two,
    second_norm_params,
    mom_bn_two,
    avg_bn_two,
    w_head,
    mom_head,
    avg_head,
):
    n_img = lax.axis_size("img")
    n_ch = lax.axis_size("ch")
    group = images_in.shape[0]
    element_count = labels.shape[0]
    width = second_norm_params.shape[1]
    classes = w_head.shape[0] * n_img * n_ch // width
    images = element_count * n_img * n_ch
    slot_info = jnp.stack([labels.astype(jnp.float32), loss_wt.astype(jnp.float32)])
    slot_info = lax.all_gather(slot_info, "ch", axis=1, tiled=True)
    own = lax.axis_index("ch") * element_count + jnp.arange(element_count, dtype=jnp.int32)
    fills = placement[0][None, :] == own[:, None]
    labels_f, weights = jnp.sum(jnp.where(fills[None], slot_info[:, None, :], 0.0), axis=2)
    labels = labels_f.astype(jnp.int32)
    kernel_part = (w_two * mask_two.astype(jnp.float32)).astype(jnp.bfloat16)
    kernel = lax.all_gather(kernel_part, ("img", "ch"), axis=0, tiled=True)
    head = lax.all_gather(w_head.astype(jnp.bfloat16), ("img", "ch"), axis=0, tiled=True)
    kernel = kernel.reshape(9 * width, width)
    head = head.reshape(width, classes)
    rows = images_in.transpose(1, 0, 2).reshape(PIX * group, images_in.shape[2])
    filt_one = (w_one * mask_one.astype(jnp.float32)).astype(jnp.bfloat16)
    first_conv_output = jnp.dot(rows, filt_one, preferred_element_type=jnp.float32)
    first_feature_sum, first_squares_sum, total = lax.psum(
        (
            jnp.sum(first_conv_output, axis=0),
            jnp.sum(first_conv_output * first_conv_output, axis=0),
            jnp.sum(slot_info[1]),
        ),
        "img",
    )
    first_element_count = group * PIX * n_img
    first_standardized_input, first_inverse_deviation = apply_batch_norm(
        first_conv_output, first_feature_sum, first_squares_sum, first_element_count
    )
    first_norm_output = first_norm_params[0] * first_standardized_input + first_norm_params[1]
    act = jax.nn.silu(first_norm_output).astype(jnp.bfloat16).reshape(PIX, group, -1)
    act_in = lax.all_to_all(act, "ch", split_axis=1, concat_axis=2, tiled=True)
    padded = jnp.pad(
        act_in.reshape(SIDE, SIDE, element_count, width), ((1, 1), (1, 1), (0, 0), (0, 0))
    )
    patches = jnp.concatenate(
        [
            padded[tap // 3 : tap // 3 + SIDE, tap % 3 : tap % 3 + SIDE].reshape(
                PIX * element_count, width
            )
            for tap in range(9)
        ],
        axis=1,
    )
    second_conv_output = jnp.dot(patches, kernel, preferred_element_type=jnp.float32)
    second_feature_sum, second_squares_sum = lax.psum(
        (
            jnp.sum(second_conv_output, axis=0),
            jnp.sum(second_conv_output * second_conv_output, axis=0),
        ),
        ("img", "ch"),
    )
    second_element_count = images * PIX
    second_standardized_input, second_inverse_deviation = apply_batch_norm(
        second_conv_output, second_feature_sum, second_squares_sum, second_element_count
    )
    second_norm_output = second_norm_params[0] * second_standardized_input + second_norm_params[1]
    pooled = jnp.mean(jax.nn.silu(second_norm_output).reshape(PIX, element_count, width), axis=0)
    pooled_low = pooled.astype(jnp.bfloat16)
    logits = jnp.dot(pooled_low, head, preferred_element_type=jnp.float32)
    top = jnp.max(logits, axis=1, keepdims=True)
    expd = jnp.exp(logits - top)
    denom = jnp.sum(expd, axis=1, keepdims=True)
    lse = top[:, 0] + jnp.log(denom[:, 0])
    onehot = labels[:, None] == jnp.arange(classes, dtype=jnp.int32)[None, :]
    picked = jnp.sum(jnp.where(onehot, logits, 0.0), axis=1)
    share = weights / total
    partial_loss_value = jnp.sum(share * (lse - picked))
    d_logits = (share[:, None] * (expd / denom - onehot.astype(jnp.float32))).astype(jnp.bfloat16)
    g_head = contract_rows(pooled_low, d_logits)
    d_pooled = jnp.einsum("ic,kc->ik", d_logits, head, preferred_element_type=jnp.float32)
    d_act = jnp.broadcast_to(d_pooled[None] / PIX, (PIX, element_count, width)).reshape(
        PIX * element_count, width
    )
    second_output_gradient = d_act * silu_slope(second_norm_output)
    second_shift_bias, second_norm_gain, loss = lax.psum(
        (
            jnp.sum(second_output_gradient, axis=0),
            jnp.sum(second_output_gradient * second_standardized_input, axis=0),
            partial_loss_value,
        ),
        ("img", "ch"),
    )
    second_preact_gradient = batch_norm_backward(
        second_norm_params[0],
        second_inverse_deviation,
        second_output_gradient,
        second_standardized_input,
        second_shift_bias,
        second_norm_gain,
        second_element_count,
    ).astype(jnp.bfloat16)
    d_patches = jnp.einsum(
        "pc,kc->pk", second_preact_gradient, kernel, preferred_element_type=jnp.float32
    )
    d_pad = 0.0
    for tap in range(9):
        piece = d_patches[:, tap * width : (tap + 1) * width].reshape(
            SIDE, SIDE, element_count, width
        )
        up, left = tap // 3, tap % 3
        d_pad = d_pad + jnp.pad(piece, ((up, 2 - up), (left, 2 - left), (0, 0), (0, 0)))
    d_act_in = d_pad[1:-1, 1:-1].astype(jnp.bfloat16).reshape(PIX, element_count, width)
    d_act_one = lax.all_to_all(d_act_in, "ch", split_axis=2, concat_axis=1, tiled=True)
    g_kernel = contract_rows(patches, second_preact_gradient)
    d_act_one = d_act_one.reshape(PIX * group, -1).astype(jnp.float32)
    first_output_gradient = d_act_one * silu_slope(first_norm_output)
    first_shift_bias, first_norm_gain = lax.psum(
        (
            jnp.sum(first_output_gradient, axis=0),
            jnp.sum(first_output_gradient * first_standardized_input, axis=0),
        ),
        "img",
    )
    first_preact_gradient = batch_norm_backward(
        first_norm_params[0],
        first_inverse_deviation,
        first_output_gradient,
        first_standardized_input,
        first_shift_bias,
        first_norm_gain,
        first_element_count,
    ).astype(jnp.bfloat16)
    g_filt = lax.psum(
        contract_rows(rows, first_preact_gradient).astype(jnp.bfloat16), "img"
    ).astype(jnp.float32)
    g_one = g_filt * mask_one.astype(jnp.float32)
    part_two = lax.psum_scatter(
        g_kernel.reshape(-1), ("img", "ch"), tiled=True
    )
    part_head = lax.psum_scatter(
        g_head.reshape(-1), ("img", "ch"), tiled=True
    )
    g_two = part_two * mask_two.astype(jnp.float32)
    root = math.sqrt(images)
    one = sparse_update(w_one, g_one, mom_one, avg_one, mask_one, rank_one, 1.3 * root)
    bno = dense_update(
        first_norm_params,
        jnp.stack([first_norm_gain, first_shift_bias]),
        mom_bn_one,
        avg_bn_one,
        8.0 * root,
    )
    two = sparse_update(w_two, g_two, mom_two, avg_two, mask_two, rank_two, 0.25 * root)
    bnt = dense_update(
        second_norm_params,
        jnp.stack([second_norm_gain, second_shift_bias]),
        mom_bn_two,
        avg_bn_two,
        root,
    )
    top_head = dense_update(w_head, part_head, mom_head, avg_head, 40.0)
    return (
        loss,
        one[0],
        one[1],
        one[2],
        one[3],
        one[4],
        bno[0],
        bno[1],
        bno[2],
        two[0],
        two[1],
        two[2],
        two[3],
        two[4],
        bnt[0],
        bnt[1],
        bnt[2],
        top_head[0],
        top_head[1],
        top_head[2],
        top_head[0].astype(jnp.bfloat16),
    )


def solution(mesh):
    in_specs = (
        P("img", None, None),
        P(("img", "ch")),
        P(("img", "ch")),
        P("img", None),
        P(None, "ch"),
        P(None, "ch"),
        P(None, "ch"),
        P(None, "ch"),
        P(None, "ch"),
        P(None, "ch"),
        P(None, "ch"),
        P(None, "ch"),
        P(("img", "ch")),
        P(("img", "ch")),
        P(("img", "ch")),
        P(("img", "ch")),
        P(("img", "ch")),
        P(),
        P(),
        P(),
        P(("img", "ch")),
        P(("img", "ch")),
        P(("img", "ch")),
    )
    out_specs = (
        P(),
        P(None, "ch"),
        P(None, "ch"),
        P(None, "ch"),
        P(None, "ch"),
        P(None, "ch"),
        P(None, "ch"),
        P(None, "ch"),
        P(None, "ch"),
        P(("img", "ch")),
        P(("img", "ch")),
        P(("img", "ch")),
        P(("img", "ch")),
        P(("img", "ch")),
        P(),
        P(),
        P(),
        P(("img", "ch")),
        P(("img", "ch")),
        P(("img", "ch")),
        P(("img", "ch")),
    )
    return jax.shard_map(shards, mesh=mesh, in_specs=in_specs, out_specs=out_specs, check_vma=False)
```

```python
import functools
import itertools
import math

import jax
import jax.numpy as jnp
from jax import lax
from jax.experimental import pallas as pl
from jax.experimental.pallas import tpu as pltpu
from jax.sharding import PartitionSpec as P

SIDE = 7
PIX = 49
DROP = 10
GROW = 10


EPS = 1e-05
MOMENTUM = 0.5


def advance(weight, grad, velocity, rate):
    velocity = MOMENTUM * velocity + grad
    return (weight - rate * (grad + MOMENTUM * velocity), velocity)


def dense_update(weight, grad, velocity, average, rate):
    moved, velocity = advance(weight, grad, velocity, rate)
    return (moved, velocity, 0.5 * average + 0.5 * moved)


def sparse_update(weight, grad, velocity, average, mask, rank, rate):
    moved, velocity = advance(weight, grad, velocity, rate)
    kept = (mask == 1) & (rank >= DROP)
    grown = (mask == 0) & (rank < GROW)
    new_mask = jnp.where(kept | grown, 1, 0).astype(jnp.int32)
    weight = jnp.where(kept, moved, 0.0)
    velocity = jnp.where(kept, velocity, 0.0)
    average = 0.5 * average + 0.5 * weight
    return (weight, velocity, average, new_mask, weight.astype(jnp.bfloat16))


def silu_slope(value):
    sigma = jax.nn.sigmoid(value)
    return sigma * (1.0 + value * (1.0 - sigma))


def apply_batch_norm(z, sums, squares, element_count):
    mean = sums / element_count
    inverse_deviation = lax.rsqrt(squares / element_count - mean * mean + EPS)
    return ((z - mean) * inverse_deviation, inverse_deviation)


def batch_norm_backward(
    norm_gain,
    inverse_deviation,
    output_gradient,
    standardized_input,
    bias_gradient_sum,
    gain_gradient_sum,
    element_count,
):
    return (
        norm_gain
        * inverse_deviation
        * (
            output_gradient
            - bias_gradient_sum / element_count
            - standardized_input * gain_gradient_sum / element_count
        )
    )


def contract_rows(left, right):
    return jnp.einsum("pk,pc->kc", left, right, preferred_element_type=jnp.float32)


def shards(
    images_in,
    labels,
    loss_wt,
    placement,
    w_one,
    mom_one,
    avg_one,
    mask_one,
    rank_one,
    first_norm_params,
    mom_bn_one,
    avg_bn_one,
    w_two,
    mom_two,
    avg_two,
    mask_two,
    rank_two,
    second_norm_params,
    mom_bn_two,
    avg_bn_two,
    w_head,
    mom_head,
    avg_head,
):
    n_img = lax.axis_size("img")
    n_ch = lax.axis_size("ch")
    group = images_in.shape[0]
    element_count = labels.shape[0]
    width = second_norm_params.shape[1]
    classes = w_head.shape[0] * n_img * n_ch // width
    images = element_count * n_img * n_ch
    slot_info = jnp.stack([labels.astype(jnp.float32), loss_wt.astype(jnp.float32)])
    slot_info = lax.all_gather(slot_info, "ch", axis=1, tiled=True)
    own = lax.axis_index("ch") * element_count + jnp.arange(element_count, dtype=jnp.int32)
    fills = placement[0][None, :] == own[:, None]
    labels_f, weights = jnp.sum(jnp.where(fills[None], slot_info[:, None, :], 0.0), axis=2)
    labels = labels_f.astype(jnp.int32)
    kernel_part = (w_two * mask_two.astype(jnp.float32)).astype(jnp.bfloat16)
    kernel = lax.all_gather(kernel_part, ("img", "ch"), axis=0, tiled=True)
    head = lax.all_gather(w_head.astype(jnp.bfloat16), ("img", "ch"), axis=0, tiled=True)
    kernel = kernel.reshape(9 * width, width)
    head = head.reshape(width, classes)
    rows = images_in.transpose(1, 0, 2).reshape(PIX * group, images_in.shape[2])
    filt_one = (w_one * mask_one.astype(jnp.float32)).astype(jnp.bfloat16)
    first_conv_output = jnp.dot(rows, filt_one, preferred_element_type=jnp.float32)
    first_feature_sum, first_squares_sum, total = lax.psum(
        (
            jnp.sum(first_conv_output, axis=0),
            jnp.sum(first_conv_output * first_conv_output, axis=0),
            jnp.sum(slot_info[1]),
        ),
        "img",
    )
    first_element_count = group * PIX * n_img
    first_standardized_input, first_inverse_deviation = apply_batch_norm(
        first_conv_output, first_feature_sum, first_squares_sum, first_element_count
    )
    first_norm_output = first_norm_params[0] * first_standardized_input + first_norm_params[1]
    act = jax.nn.silu(first_norm_output).astype(jnp.bfloat16).reshape(PIX, group, -1)
    act_in = lax.all_to_all(act, "ch", split_axis=1, concat_axis=2, tiled=True)
    padded = jnp.pad(
        act_in.reshape(SIDE, SIDE, element_count, width), ((1, 1), (1, 1), (0, 0), (0, 0))
    )
    patches = jnp.concatenate(
        [
            padded[tap // 3 : tap // 3 + SIDE, tap % 3 : tap % 3 + SIDE].reshape(
                PIX * element_count, width
            )
            for tap in range(9)
        ],
        axis=1,
    )
    second_conv_output = jnp.dot(patches, kernel, preferred_element_type=jnp.float32)
    second_feature_sum, second_squares_sum = lax.psum(
        (
            jnp.sum(second_conv_output, axis=0),
            jnp.sum(second_conv_output * second_conv_output, axis=0),
        ),
        ("img", "ch"),
    )
    second_element_count = images * PIX
    second_standardized_input, second_inverse_deviation = apply_batch_norm(
        second_conv_output, second_feature_sum, second_squares_sum, second_element_count
    )
    second_norm_output = second_norm_params[0] * second_standardized_input + second_norm_params[1]
    pooled = jnp.mean(jax.nn.silu(second_norm_output).reshape(PIX, element_count, width), axis=0)
    pooled_low = pooled.astype(jnp.bfloat16)
    logits = jnp.dot(pooled_low, head, preferred_element_type=jnp.float32)
    top = jnp.max(logits, axis=1, keepdims=True)
    expd = jnp.exp(logits - top)
    denom = jnp.sum(expd, axis=1, keepdims=True)
    lse = top[:, 0] + jnp.log(denom[:, 0])
    onehot = labels[:, None] == jnp.arange(classes, dtype=jnp.int32)[None, :]
    picked = jnp.sum(jnp.where(onehot, logits, 0.0), axis=1)
    share = weights / total
    partial_loss_value = jnp.sum(share * (lse - picked))
    d_logits = (share[:, None] * (expd / denom - onehot.astype(jnp.float32))).astype(jnp.bfloat16)
    g_head = contract_rows(pooled_low, d_logits)
    d_pooled = jnp.einsum("ic,kc->ik", d_logits, head, preferred_element_type=jnp.float32)
    d_act = jnp.broadcast_to(d_pooled[None] / PIX, (PIX, element_count, width)).reshape(
        PIX * element_count, width
    )
    second_output_gradient = d_act * silu_slope(second_norm_output)
    second_shift_bias, second_norm_gain, loss = lax.psum(
        (
            jnp.sum(second_output_gradient, axis=0),
            jnp.sum(second_output_gradient * second_standardized_input, axis=0),
            partial_loss_value,
        ),
        ("img", "ch"),
    )
    second_preact_gradient = batch_norm_backward(
        second_norm_params[0],
        second_inverse_deviation,
        second_output_gradient,
        second_standardized_input,
        second_shift_bias,
        second_norm_gain,
        second_element_count,
    ).astype(jnp.bfloat16)
    d_patches = jnp.einsum(
        "pc,kc->pk", second_preact_gradient, kernel, preferred_element_type=jnp.float32
    )
    d_pad = 0.0
    for tap in range(9):
        piece = d_patches[:, tap * width : (tap + 1) * width].reshape(
            SIDE, SIDE, element_count, width
        )
        up, left = tap // 3, tap % 3
        d_pad = d_pad + jnp.pad(piece, ((up, 2 - up), (left, 2 - left), (0, 0), (0, 0)))
    d_act_in = d_pad[1:-1, 1:-1].astype(jnp.bfloat16).reshape(PIX, element_count, width)
    d_act_one = lax.all_to_all(d_act_in, "ch", split_axis=2, concat_axis=1, tiled=True)
    g_kernel = contract_rows(patches, second_preact_gradient)
    d_act_one = d_act_one.reshape(PIX * group, -1).astype(jnp.float32)
    first_output_gradient = d_act_one * silu_slope(first_norm_output)
    first_shift_bias, first_norm_gain = lax.psum(
        (
            jnp.sum(first_output_gradient, axis=0),
            jnp.sum(first_output_gradient * first_standardized_input, axis=0),
        ),
        "img",
    )
    first_preact_gradient = batch_norm_backward(
        first_norm_params[0],
        first_inverse_deviation,
        first_output_gradient,
        first_standardized_input,
        first_shift_bias,
        first_norm_gain,
        first_element_count,
    ).astype(jnp.bfloat16)
    g_filt = lax.psum(
        contract_rows(rows, first_preact_gradient).astype(jnp.bfloat16), "img"
    ).astype(jnp.float32)
    g_one = g_filt * mask_one.astype(jnp.float32)
    part_two = lax.psum_scatter(
        g_kernel.reshape(-1), ("img", "ch"), tiled=True
    )
    part_head = lax.psum_scatter(
        g_head.reshape(-1), ("img", "ch"), tiled=True
    )
    g_two = part_two * mask_two.astype(jnp.float32)
    root = math.sqrt(images)
    one = sparse_update(w_one, g_one, mom_one, avg_one, mask_one, rank_one, 1.3 * root)
    bno = dense_update(
        first_norm_params,
        jnp.stack([first_norm_gain, first_shift_bias]),
        mom_bn_one,
        avg_bn_one,
        8.0 * root,
    )
    two = sparse_update(w_two, g_two, mom_two, avg_two, mask_two, rank_two, 0.25 * root)
    bnt = dense_update(
        second_norm_params,
        jnp.stack([second_norm_gain, second_shift_bias]),
        mom_bn_two,
        avg_bn_two,
        root,
    )
    top_head = dense_update(w_head, part_head, mom_head, avg_head, 40.0)
    return (
        loss,
        one[0],
        one[1],
        one[2],
        one[3],
        one[4],
        bno[0],
        bno[1],
        bno[2],
        two[0],
        two[1],
        two[2],
        two[3],
        two[4],
        bnt[0],
        bnt[1],
        bnt[2],
        top_head[0],
        top_head[1],
        top_head[2],
        top_head[0].astype(jnp.bfloat16),
    )


F32, BF16 = jnp.float32, jnp.bfloat16
MESH = pl.DeviceIdType.MESH
TAPS = 9
UPPER = (SIDE + 1) // 2
PITCH = SIDE + 1
FRONT = 2 * PITCH


def silu_pair(value):
    sigma = 1.0 / (1.0 + jnp.exp(-value))
    return value * sigma, sigma * (1.0 + value * (1.0 - sigma))


def matmul_nt(left, right):
    return lax.dot_general(left, right, (((1,), (1,)), ((), ())), preferred_element_type=F32)


def matmul_tn(left, right):
    return lax.dot_general(left, right, (((0,), (0,)), ((), ())), preferred_element_type=F32)


def rank_one(row, other):
    first = other.astype(BF16)
    rest = other - first.astype(F32)
    second = rest.astype(BF16)
    third = (rest - second.astype(F32)).astype(BF16)
    place = lax.broadcasted_iota(jnp.int32, (16, other.shape[1]), 0)
    parts = jnp.where(place == 0, first.astype(F32), 0.0)
    parts = jnp.where(place == 1, second.astype(F32), parts)
    parts = jnp.where(place == 2, third.astype(F32), parts)
    rows = jnp.broadcast_to(row, (16, row.shape[1])).astype(BF16)
    return matmul_tn(rows, parts.astype(BF16))


def step_kernel(
    sizes,
    images,
    place,
    labels,
    loss_wt,
    w_one,
    mask_one,
    norm_one,
    w_two,
    mask_two,
    head_part,
    norm_two,
    g_one,
    g_two,
    g_head,
    g_bn_one,
    g_bn_two,
    loss,
    feats,
    filt,
    kern,
    head,
    act_in,
    act_out,
    z_one,
    z_two,
    slope,
    d_pad,
    act_t,
    d_act,
    d_send,
    d_recv,
    d_one,
    early,
    info,
    tile_sib,
    tile_plane,
    wide_plane,
    wide_z,
    wide_sib,
    logit,
    gh_half,
    gk,
    gh,
    rk_one,
    rh_one,
    rk_two,
    rh_two,
    rk_z,
    rh_z,
    last_send,
    last_recv,
    edge_rows,
    ranked,
    grad_t,
    g_acc,
    go_send,
    go_recv,
    ga_send,
    ga_recv,
    image_sem,
    local_sem,
    send,
    recv,
):
    group, per_chip, classes, images_in_all = sizes
    width = norm_two.shape[1]
    half = width // 2
    own_ch = w_one.shape[0]
    chip_ch = 2 * own_ch
    block = w_two.shape[0] * 128 // width
    chunk = 2 * block
    rows_a = SIDE * group
    rows_c = PITCH * per_chip
    count_all = float(images_in_all * PIX)

    i, c = lax.axis_index("img"), lax.axis_index("ch")
    z, k = lax.div(c, 2), lax.rem(c, 2)
    sib = c + 1 - 2 * k
    xn, yn, dg = i + 1 - 2 * lax.rem(i, 2), lax.rem(i + 2, 4), 3 - i
    lines = (xn, yn, dg)
    h0 = (SIDE - UPPER) * k

    def chip(dz):
        return lax.rem(z + dz, 4)

    def zdev(dz):
        return 2 * chip(dz) + k

    next_send, next_recv = itertools.count(), itertools.count()
    sent = []

    def new_recv(n=1):
        first = next(next_recv)
        for _ in range(n - 1):
            next(next_recv)
        return first

    def push(src, dst, device, to):
        copy = pltpu.make_async_remote_copy(
            src_ref=src,
            dst_ref=dst,
            send_sem=send.at[next(next_send)],
            recv_sem=recv.at[to],
            device_id=device,
            device_id_type=MESH,
        )
        copy.start()
        sent.append(copy)
        return copy

    def arrived(dst, at):
        pltpu.make_async_remote_copy(
            src_ref=dst,
            dst_ref=dst,
            send_sem=send.at[0],
            recv_sem=recv.at[at],
            device_id=(i, sib),
            device_id_type=MESH,
        ).wait_recv()

    def image_copy(r):
        return pltpu.make_async_copy(
            images.at[pl.ds(SIDE * (h0 + r), SIDE)], feats.at[pl.ds(SIDE * r, SIDE)], image_sem.at[r]
        )

    for r in range(UPPER):
        image_copy(r).start()

    act_in[0] = jnp.zeros(act_in.shape[1:], BF16)
    for r in range(SIDE + 1, act_in.shape[0]):
        act_in[r] = jnp.zeros(act_in.shape[1:], BF16)
    for r in range(1, SIDE + 1):
        act_in[r, 0] = jnp.zeros(act_in.shape[2:], BF16)
    chunk_at = pl.multiple_of(chunk * (i * 4 + z), 32)
    block_at = pl.multiple_of(chunk_at + block * k, 16)
    parts = [
        w_two[pl.ds(j, block, stride=4), :] * mask_two[pl.ds(j, block, stride=4), :].astype(F32)
        for j in range(4)
    ]
    low = jnp.concatenate(parts[:2], axis=1).astype(BF16)
    high = jnp.concatenate(parts[2:], axis=1).astype(BF16)
    kern[pl.ds(block_at, block), :] = jnp.where(k == 0, low.astype(F32), high.astype(F32)).astype(BF16)
    gk[pl.ds(0, block), :] = jnp.where(k == 0, high.astype(F32), low.astype(F32)).astype(BF16)
    own_at = pl.multiple_of(own_ch * k, 16)
    filt[pl.ds(own_at, own_ch), :] = (w_one[...] * mask_one[...].astype(F32)).astype(BF16)
    head[i, z, k] = head_part[...]
    lane = lax.broadcasted_iota(jnp.int32, (1, 128), 1)
    norms = norm_one[...]
    nothing = jnp.zeros_like(norms)
    placed = jnp.where(
        k == 0, jnp.concatenate([norms, nothing], axis=1), jnp.concatenate([nothing, norms], axis=1)
    )
    label_row, weight_row = jnp.zeros((1, 128), F32), jnp.zeros((1, 128), F32)
    for j in range(labels.shape[0]):
        here = lane == labels.shape[0] * c + j
        label_row = jnp.where(here, labels[j].astype(F32), label_row)
        weight_row = jnp.where(here, loss_wt[j].astype(F32), weight_row)
    early[0] = jnp.concatenate(
        [placed, label_row, weight_row, jnp.zeros((4, 128), F32)], axis=0
    )

    barrier = pltpu.get_barrier_semaphore()
    others = [(i, sib)] + [(o, c) for o in lines] + [(i, zdev(dz)) for dz in (1, 2, 3)]
    for device in others:
        pl.semaphore_signal(barrier, inc=1, device_id=device, device_id_type=MESH)
    pl.semaphore_wait(barrier, len(others))

    k_sib, f_sib, e_sib = new_recv(), new_recv(), new_recv()
    push(gk.at[pl.ds(0, block)], kern.at[pl.ds(block_at, block)], (i, sib), k_sib)
    push(filt.at[pl.ds(own_at, own_ch)], filt.at[pl.ds(own_at, own_ch)], (i, sib), f_sib)
    push(early.at[0], early.at[1], (i, sib), e_sib)

    k_recv, h_recv = new_recv(16), new_recv(16)

    def kern_at(line, dz):
        return kern.at[pl.ds(pl.multiple_of(chunk * (line * 4 + chip(dz)), 32), chunk)]

    def head_at(line, dz):
        return head.at[line, chip(dz), k]

    def number(line, dz):
        return line * 4 + chip(dz)

    def forward(line, dz, device):
        push(kern_at(line, dz), kern_at(line, dz), device, k_recv + number(line, dz))
        push(head_at(line, dz), head_at(line, dz), device, h_recv + number(line, dz))

    def landed(line, dz):
        arrived(kern_at(line, dz), k_recv + number(line, dz))
        arrived(head_at(line, dz), h_recv + number(line, dz))

    other_block_at = pl.multiple_of(chunk_at + block * (1 - k), 16)
    arrived(kern.at[pl.ds(other_block_at, block)], k_sib)
    for dz in (1, 2, 3):
        forward(i, 0, (i, zdev(dz)))
    forward(i, 0, (xn, c))
    forward(i, 0, (yn, c))
    arrived(early.at[1], e_sib)
    both = early[0] + early[1]
    info[z] = both
    i_recv = new_recv(4)
    for dz in (1, 2, 3):
        push(info.at[z], info.at[z], (i, zdev(dz)), i_recv + z)
    other_at = pl.multiple_of(own_ch * (1 - k), 16)
    arrived(filt.at[pl.ds(other_at, own_ch)], f_sib)

    def first_conv(r, carry):
        sums, squares = carry
        image_copy(r).wait()
        rows = feats[pl.ds(SIDE * r, SIDE)].reshape(rows_a, feats.shape[2])
        out = matmul_nt(rows, filt[...])
        z_one[pl.ds(pl.multiple_of(rows_a * r, 64), rows_a), :] = out
        counted = jnp.where((r == 0) & (k == 1), 0.0, 1.0)
        return (
            sums + counted * jnp.sum(out, axis=0, keepdims=True),
            squares + counted * jnp.sum(out * out, axis=0, keepdims=True),
        )

    zero_row = jnp.zeros((1, chip_ch), F32)
    sums, squares = lax.fori_loop(0, UPPER, first_conv, (zero_row, zero_row))

    for dz in (1, 2, 3):
        arrived(info.at[chip(dz)], i_recv + chip(dz))
    slots = info[0] + info[1] + info[2] + info[3]
    lane_in = lane < group
    group_weight = jnp.sum(jnp.where(lane_in, slots[3:4], 0.0), axis=1, keepdims=True)

    def small_sum(turn, rows):
        tile_sib[turn, 0] = rows
        at = new_recv()
        push(tile_sib.at[turn, 0], tile_sib.at[turn, 1], (i, sib), at)
        arrived(tile_sib.at[turn, 1], at)
        tile_plane[turn, i] = tile_sib[turn, 0] + tile_sib[turn, 1]
        at = new_recv(4)
        for line in lines:
            push(tile_plane.at[turn, i], tile_plane.at[turn, i], (line, c), at + i)

        def finish():
            for line in lines:
                arrived(tile_plane.at[turn, line], at + line)
            return (
                tile_plane[turn, 0] + tile_plane[turn, 1] + tile_plane[turn, 2] + tile_plane[turn, 3]
            )

        return finish

    half_weight = jnp.broadcast_to(0.5 * group_weight, (1, 128))
    finish = small_sum(
        0, jnp.concatenate([sums, squares, half_weight, jnp.zeros((5, 128), F32)], axis=0)
    )
    for dz in (1, 2, 3):
        landed(i, dz)
        forward(i, dz, (xn, c))
        forward(i, dz, (yn, c))
    totals = finish()
    total = totals[2:3, 0:1]
    mean_one = totals[0:1] / count_all
    inv_one = lax.rsqrt(totals[1:2] / count_all - mean_one * mean_one + EPS)
    gain_one, bias_one = both[0:1], both[1:2]

    def first_act(r, carry):
        at = pl.ds(pl.multiple_of(rows_a * r, 64), rows_a)
        hat = (z_one[at, :] - mean_one) * inv_one
        value, grade = silu_pair(gain_one * hat + bias_one)
        act_out[r] = value.astype(BF16).reshape(SIDE, group, chip_ch)
        return carry

    lax.fori_loop(0, UPPER, first_act, 0)

    a_recv = new_recv(4)
    into = act_in.at[
        pl.ds(1 + h0, UPPER), pl.ds(1, SIDE), :, pl.ds(pl.multiple_of(chip_ch * z, 128), chip_ch)
    ]

    def images_of(ref, dz):
        return ref.at[:, :, pl.ds(pl.multiple_of(per_chip * chip(dz), 16), per_chip), :]

    out_copies = [push(images_of(act_out, dz), into, (i, zdev(dz)), a_recv + z) for dz in (1, 2, 3)]
    keep = pltpu.make_async_copy(images_of(act_out, 0), into, local_sem.at[0])
    keep.start()

    for dz in (0, 1):
        landed(xn, dz)
        forward(xn, dz, (yn, c))
    for dz in (2, 3):
        landed(yn, dz)
        forward(yn, dz, (xn, c))

    keep.wait()
    for dz in (1, 2, 3):
        arrived(
            act_in.at[
                pl.ds(1 + h0, UPPER),
                pl.ds(1, SIDE),
                :,
                pl.ds(pl.multiple_of(chip_ch * chip(dz), 128), chip_ch),
            ],
            a_recv + chip(dz),
        )
    a_sib = new_recv()
    mine = act_in.at[pl.ds(1 + UPPER * k, SIDE - UPPER), pl.ds(1, SIDE)]
    push(mine, mine, (i, sib), a_sib)

    for dz in (0, 1):
        landed(yn, dz)
    for dz in (2, 3):
        landed(xn, dz)
    for dz in (0, 1, 2, 3):
        landed(dg, dz)
    hd_sib = new_recv()
    theirs = head.at[pl.ds(2 * (1 - k), 2), :, k]
    push(theirs, theirs, (i, sib), hd_sib)
    arrived(act_in.at[pl.ds(1 + UPPER * (1 - k), SIDE - UPPER), pl.ds(1, SIDE)], a_sib)

    def tap_of(t):
        return t // 3, t % 3

    def second_conv(h, carry):
        sums, squares = carry
        out = jnp.zeros((rows_c, half), F32)
        for t in range(TAPS):
            up, left = tap_of(t)
            wide = act_in[pl.ds(h + up, 2)].reshape(2 * PITCH, per_chip, width)
            rows = wide[left : left + PITCH].reshape(rows_c, width)
            out = out + jnp.dot(
                rows, kern[pl.ds(width * t, width), :], preferred_element_type=F32
            )
        z_two[h] = out.reshape(PITCH, per_chip, half)
        real = out[: SIDE * per_chip]
        return (
            sums + jnp.sum(real, axis=0, keepdims=True),
            squares + jnp.sum(real * real, axis=0, keepdims=True),
        )

    zero_half = jnp.zeros((1, half), F32)
    sums, squares = lax.fori_loop(0, SIDE, second_conv, (zero_half, zero_half))

    def act_sum(h, carry):
        rows = act_in[h + 1].reshape(rows_c, width).astype(F32)
        return carry + jnp.sum(rows, axis=0, keepdims=True)

    act_sums = lax.fori_loop(0, SIDE, act_sum, jnp.zeros((1, width), F32))

    def wide_sum(turn, rows, between=None, size=8):
        wide_plane[turn, i, pl.ds(0, size)] = rows
        at = new_recv(4)
        for line in lines:
            push(
                wide_plane.at[turn, i, pl.ds(0, size)],
                wide_plane.at[turn, i, pl.ds(0, size)],
                (line, c),
                at + i,
            )
        if between is not None:
            between()
        for line in lines:
            arrived(wide_plane.at[turn, line, pl.ds(0, size)], at + line)
        wide_z[turn, z, pl.ds(0, size)] = (
            wide_plane[turn, 0, pl.ds(0, size)]
            + wide_plane[turn, 1, pl.ds(0, size)]
            + wide_plane[turn, 2, pl.ds(0, size)]
            + wide_plane[turn, 3, pl.ds(0, size)]
        )
        at_z = new_recv(4)
        for dz in (1, 2, 3):
            push(
                wide_z.at[turn, z, pl.ds(0, size)],
                wide_z.at[turn, z, pl.ds(0, size)],
                (i, zdev(dz)),
                at_z + z,
            )

        def finish():
            for dz in (1, 2, 3):
                arrived(wide_z.at[turn, chip(dz), pl.ds(0, size)], at_z + chip(dz))
            return (
                wide_z[turn, 0, pl.ds(0, size)]
                + wide_z[turn, 1, pl.ds(0, size)]
                + wide_z[turn, 2, pl.ds(0, size)]
                + wide_z[turn, 3, pl.ds(0, size)]
            )

        return finish

    finish = wide_sum(
        0,
        jnp.concatenate(
            [sums, squares, act_sums[:, :half], act_sums[:, half:], jnp.zeros((4, half), F32)], axis=0
        ),
    )
    inner = act_in[pl.ds(1, SIDE + 1)].reshape((SIDE + 1) * PITCH, per_chip, width)
    inner = inner[1 : 1 + SIDE * PITCH].reshape(SIDE * rows_c, width)
    act_t[pl.ds(0, width), :] = inner.T
    column = lax.broadcasted_iota(jnp.int32, (16, SIDE * rows_c), 1)
    is_real = lax.rem(lax.div(column, per_chip), PITCH) < SIDE
    act_t[pl.ds(width, 16), :] = jnp.where(is_real, 1.0, 0.0).astype(BF16)
    d_pad[pl.ds(0, FRONT)] = jnp.zeros((FRONT, per_chip, half), BF16)
    d_pad[pl.ds(FRONT + SIDE * PITCH, FRONT)] = jnp.zeros((FRONT, per_chip, half), BF16)
    totals_two = finish()
    mean_two = totals_two[0:1] / count_all
    inv_two = lax.rsqrt(totals_two[1:2] / count_all - mean_two * mean_two + EPS)
    centre = jnp.concatenate([totals_two[2:3], totals_two[3:4]], axis=1) / count_all
    centre = centre.astype(BF16).astype(F32)
    norms_two = jnp.where(k == 0, norm_two[:, :half], norm_two[:, half:])
    gain_two, bias_two = norms_two[0:1], norms_two[1:2]

    def second_act(h, pooled):
        hat = (z_two[h] - mean_two) * inv_two
        z_two[h] = hat
        value, grade = silu_pair(gain_two * hat + bias_two)
        slope[h] = grade
        return pooled + jnp.sum(value[:SIDE], axis=0)

    pooled = lax.fori_loop(0, SIDE, second_act, jnp.zeros((per_chip, half), F32)) / PIX
    pooled_low = pooled.astype(BF16)

    arrived(head.at[pl.ds(2 * k, 2), :, 1 - k], hd_sib)
    head_half = head[pl.ds(2 * k, 2)].reshape(half, head.shape[4])
    logit[0] = jnp.dot(pooled_low, head_half, preferred_element_type=F32)
    at = new_recv()
    push(logit.at[0], logit.at[1], (i, sib), at)
    image_id = per_chip * z + lax.broadcasted_iota(jnp.int32, (per_chip, group), 0)
    fills = place[...] == image_id
    label = jnp.sum(jnp.where(fills, slots[2:3, :group], 0.0), axis=1, keepdims=True).astype(jnp.int32)
    weight = jnp.sum(jnp.where(fills, slots[3:4, :group], 0.0), axis=1, keepdims=True)
    share = weight / total
    arrived(logit.at[1], at)
    logits = logit[0] + logit[1]
    klass = lax.broadcasted_iota(jnp.int32, logits.shape, 1)
    inside = klass < classes
    top = jnp.max(jnp.where(inside, logits, -jnp.inf), axis=1, keepdims=True)
    expd = jnp.where(inside, jnp.exp(jnp.where(inside, logits - top, 0.0)), 0.0)
    denom = jnp.sum(expd, axis=1, keepdims=True)
    onehot = klass == label
    picked = jnp.sum(jnp.where(onehot, logits, 0.0), axis=1, keepdims=True)
    partial = jnp.sum(share * (top + jnp.log(denom) - picked), axis=0, keepdims=True)
    d_logits = (share * (expd / denom - jnp.where(onehot, 1.0, 0.0))).astype(BF16)
    d_pooled = matmul_nt(d_logits, head_half) / PIX

    def second_back(h, carry):
        sums, products = carry
        d_y = d_pooled[None] * slope[h]
        slope[h] = d_y
        d_y = d_y[:SIDE].reshape(SIDE * per_chip, half)
        hat = z_two[h][:SIDE].reshape(SIDE * per_chip, half)
        return (
            sums + jnp.sum(d_y, axis=0, keepdims=True),
            products + jnp.sum(d_y * hat, axis=0, keepdims=True),
        )

    d_bias, d_gain = lax.fori_loop(0, SIDE, second_back, (zero_half, zero_half))

    gh_swap = new_recv()

    def head_gradient():
        gh_half[...] = matmul_tn(pooled_low, d_logits).astype(BF16).reshape(gh_half.shape)
        push(gh_half.at[:, :, 1 - k], gh.at[pl.ds(2 * k, 2)], (i, sib), gh_swap)

    finish = wide_sum(
        1,
        jnp.concatenate(
            [d_gain, d_bias, jnp.broadcast_to(partial, (1, half)), jnp.zeros((5, half), F32)], axis=0
        ),
        head_gradient,
    )
    totals_back = finish()
    loss[...] = totals_back[2:3, :128]
    wide_sib[0] = totals_back
    bn_at = new_recv()
    push(wide_sib.at[0], wide_sib.at[1], (i, sib), bn_at)
    scale = gain_two * inv_two
    shift_two, lean_two = totals_back[1:2] / count_all, totals_back[0:1] / count_all

    def second_grad(h, carry):
        grad = scale * (slope[h] - shift_two - z_two[h] * lean_two)
        pixel = lax.broadcasted_iota(jnp.int32, grad.shape, 0)
        grad = jnp.where(pixel < SIDE, grad, 0.0)
        d_pad[pl.ds(FRONT + PITCH * h, PITCH)] = grad.astype(BF16)
        return carry

    lax.fori_loop(0, SIDE, second_grad, 0)

    def back_conv(h, carry):
        out = jnp.zeros((rows_c, width), F32)
        for t in range(TAPS):
            up, left = tap_of(t)
            rows = d_pad[pl.ds(PITCH * h + FRONT + PITCH + 1 - PITCH * up - left, PITCH)]
            out = out + matmul_nt(rows.reshape(rows_c, half), kern[pl.ds(width * t, width), :])
        d_act[h] = out.reshape(PITCH, per_chip, width)
        return carry

    lax.fori_loop(0, SIDE, back_conv, 0)
    s0 = (SIDE - UPPER) * (1 - k)
    for r in range(UPPER):
        d_send[r] = d_act[s0 + r][:SIDE].astype(BF16)
    d_at = new_recv()
    push(d_send, d_recv, (i, sib), d_at)

    def kernel_gradient(t, carry):
        rows = d_pad[pl.ds(FRONT + PITCH + 1 - PITCH * lax.div(t, 3) - lax.rem(t, 3), SIDE * PITCH)]
        out = jnp.dot(
            act_t[...], rows.reshape(SIDE * rows_c, half), preferred_element_type=F32
        )
        edge = out[width : width + 1]
        edge_rows[pl.ds(t, 1)] = edge
        gk[pl.ds(pl.multiple_of(width * t, 32), width), :] = (
            out[:width] - rank_one(centre, edge)
        ).astype(BF16)
        return carry

    arrived(d_recv, d_at)
    for r in range(UPPER):
        d_send_r = d_act[h0 + r][:SIDE] + d_recv[r].astype(F32)
        d_recv[r] = d_send_r.astype(BF16)
    b_recv = new_recv(4)
    back_into = images_of(d_one, 0)

    def channels_of(dz):
        return d_recv.at[:, :, :, pl.ds(pl.multiple_of(chip_ch * chip(dz), 128), chip_ch)]

    for dz in (1, 2, 3):
        push(channels_of(dz), back_into, (i, zdev(dz)), b_recv + z)
    keep = pltpu.make_async_copy(channels_of(0), back_into, local_sem.at[1])
    keep.start()

    sent.pop(0).wait_send()
    edge_rows[...] = jnp.zeros(edge_rows.shape, F32)
    lax.fori_loop(0, TAPS, kernel_gradient, 0)
    arrived(gh.at[pl.ds(2 * (1 - k), 2)], gh_swap)
    gh[pl.ds(2 * k, 2)] = jnp.where(
        k == 0, gh_half[:, :, 0].astype(F32), gh_half[:, :, 1].astype(F32)
    ).astype(BF16)

    def gk_at(line, dz):
        return gk.at[pl.ds(pl.multiple_of(chunk * (line * 4 + chip(dz)), 32), chunk)]

    def gh_at(line, dz):
        return gh.at[line, chip(dz)]

    order = (1, 2, 3, 0)
    ways = {1: (xn, yn), 2: (yn, xn), 3: (xn, yn), 0: (yn, xn)}
    one_at = {dz: new_recv(4) for dz in order}
    two_at = {dz: new_recv(2) for dz in order}
    z_at = new_recv(8)

    def start_one(dz):
        first, second = ways[dz]
        push(gk_at(dg, dz), rk_one.at[dz, 1], (first, c), one_at[dz] + 1)
        push(gh_at(dg, dz), rh_one.at[dz, 1], (first, c), one_at[dz] + 3)
        push(gk_at(first, dz), rk_one.at[dz, 0], (first, c), one_at[dz])
        push(gh_at(first, dz), rh_one.at[dz, 0], (first, c), one_at[dz] + 2)

    def start_two(dz):
        first, second = ways[dz]
        arrived(rk_one.at[dz, 1], one_at[dz] + 1)
        arrived(rh_one.at[dz, 1], one_at[dz] + 3)
        into_k, into_h = gk_at(second, dz), gh_at(second, dz)
        into_k[...] = (into_k[...].astype(F32) + rk_one[dz, 1].astype(F32)).astype(BF16)
        into_h[...] = (into_h[...].astype(F32) + rh_one[dz, 1].astype(F32)).astype(BF16)
        push(into_k, rk_two.at[dz], (second, c), two_at[dz])
        push(into_h, rh_two.at[dz], (second, c), two_at[dz] + 1)

    def plane_done(dz):
        arrived(rk_one.at[dz, 0], one_at[dz])
        arrived(rh_one.at[dz, 0], one_at[dz] + 2)
        arrived(rk_two.at[dz], two_at[dz])
        arrived(rh_two.at[dz], two_at[dz] + 1)
        into_k, into_h = gk_at(i, dz), gh_at(i, dz)
        sum_k = into_k[...].astype(F32) + rk_one[dz, 0].astype(F32) + rk_two[dz].astype(F32)
        sum_h = into_h[...].astype(F32) + rh_one[dz, 0].astype(F32) + rh_two[dz].astype(F32)
        if dz == 0:
            return sum_k, sum_h
        into_k[...] = sum_k.astype(BF16)
        into_h[...] = sum_h.astype(BF16)
        push(into_k, rk_z.at[z], (i, zdev(dz)), z_at + z)
        push(into_h, rh_z.at[z], (i, zdev(dz)), z_at + 4 + z)
        return None

    for dz in order:
        start_one(dz)
    finish_edges = wide_sum(2, edge_rows[...], size=edge_rows.shape[0])

    keep.wait()
    for dz in (1, 2, 3):
        arrived(images_of(d_one, dz), b_recv + chip(dz))

    def first_back(r, carry):
        sums, products = carry
        at = pl.ds(pl.multiple_of(rows_a * r, 64), rows_a)
        hat = (z_one[at, :] - mean_one) * inv_one
        z_one[at, :] = hat
        _, grade = silu_pair(gain_one * hat + bias_one)
        d_y = d_one[r].reshape(rows_a, chip_ch).astype(F32) * grade
        counted = jnp.where((r == 0) & (k == 1), 0.0, 1.0)
        return (
            sums + counted * jnp.sum(d_y, axis=0, keepdims=True),
            products + counted * jnp.sum(d_y * hat, axis=0, keepdims=True),
        )

    d_bias, d_gain = lax.fori_loop(0, UPPER, first_back, (zero_row, zero_row))
    finish = small_sum(
        1, jnp.concatenate([d_gain, d_bias, jnp.zeros((6, 128), F32)], axis=0)
    )
    start_two(1)
    start_two(2)
    totals_one = finish()
    g_bn_one[...] = jnp.where(k == 0, totals_one[0:2, :own_ch], totals_one[0:2, own_ch:])
    scale_one = gain_one * inv_one
    shift_one, lean_one = totals_one[1:2] / count_all, totals_one[0:1] / count_all

    def first_grad(r, carry):
        at = pl.ds(pl.multiple_of(rows_a * r, 64), rows_a)
        hat = z_one[at, :]
        _, grade = silu_pair(gain_one * hat + bias_one)
        d_y = d_one[r].reshape(rows_a, chip_ch).astype(F32) * grade
        counted = jnp.where((r == 0) & (k == 1), 0.0, 1.0)
        grad = (counted * scale_one) * (d_y - shift_one - hat * lean_one)
        act_out[r] = grad.astype(BF16).reshape(SIDE, group, chip_ch)
        return carry

    for copy in out_copies:
        copy.wait_send()
    sent[:] = [copy for copy in sent if all(copy is not done for done in out_copies)]
    lax.fori_loop(0, UPPER, first_grad, 0)

    grad_t[...] = act_out[...].reshape(UPPER * rows_a, chip_ch).T

    def first_weights(n, carry):
        at = pl.ds(pl.multiple_of(256 * n, 256), 256)
        rows = feats[:, :, at].reshape(UPPER * rows_a, 256)
        g_acc[:, at] = jnp.dot(grad_t[...], rows, preferred_element_type=F32)
        return carry

    lax.fori_loop(0, feats.shape[2] // 256, first_weights, 0)
    low, high = g_acc[:own_ch], g_acc[own_ch:]
    go_send[...] = jnp.where(k == 0, high, low).astype(BF16)
    g_at = new_recv()
    push(go_send, go_recv, (i, sib), g_at)
    g_one[...] = jnp.where(k == 0, low, high)
    plane_done(1)
    plane_done(2)
    start_two(3)
    start_two(0)
    arrived(go_recv, g_at)
    part = own_ch // 2
    ga_send[0] = (g_one[...] + go_recv[...].astype(F32)).astype(BF16)
    first_at, second_at = new_recv(2), new_recv(2)
    upper, lower = pl.ds(0, part), pl.ds(part, part)
    push(ga_send.at[0, upper], ga_recv.at[0, upper], (xn, c), first_at)
    push(ga_send.at[0, lower], ga_recv.at[0, lower], (yn, c), first_at + 1)
    arrived(ga_recv.at[0, upper], first_at)
    arrived(ga_recv.at[0, lower], first_at + 1)
    ga_send[1] = (ga_send[0].astype(F32) + ga_recv[0].astype(F32)).astype(BF16)
    push(ga_send.at[1, upper], ga_recv.at[1, upper], (yn, c), second_at)
    push(ga_send.at[1, lower], ga_recv.at[1, lower], (xn, c), second_at + 1)

    edges = finish_edges()
    plane_done(3)
    sum_k, sum_h = plane_done(0)

    arrived(ga_recv.at[1, upper], second_at)
    arrived(ga_recv.at[1, lower], second_at + 1)
    g_one[...] = ga_send[1].astype(F32) + ga_recv[1].astype(F32)

    row_at = chunk * (i * 4 + z)
    tap = lax.div(row_at, width)
    edge_rows[...] = edges
    for step in range(2):
        ranked[pl.ds(width * step, width), :] = rank_one(
            centre, edge_rows[pl.ds(lax.rem(tap + step, TAPS), 1)]
        )
    offset = pl.multiple_of(row_at - width * tap, 32)
    sum_k = sum_k + ranked[pl.ds(offset, chunk), :]
    for dz in (1, 2, 3):
        arrived(rk_z.at[chip(dz)], z_at + chip(dz))
        arrived(rh_z.at[chip(dz)], z_at + 4 + chip(dz))
        sum_k = sum_k + rk_z[chip(dz)].astype(F32)
        sum_h = sum_h + rh_z[chip(dz)].astype(F32)
    g_head[...] = sum_h
    last_send[...] = sum_k
    l_at = new_recv()
    theirs = last_send.at[pl.ds(pl.multiple_of(block * (1 - k), 16), block)]
    push(theirs, last_recv, (i, sib), l_at)
    mine = last_send[pl.ds(pl.multiple_of(block * k, 16), block), :]
    arrived(last_recv, l_at)
    other = last_recv[...]
    for j in range(4):
        lanes = slice(128 * (j % 2), 128 * (j % 2) + 128)
        g_two[pl.ds(j, block, stride=4), :] = jnp.where(
            k == j // 2, mine[:, lanes], other[:, lanes]
        )

    arrived(wide_sib.at[1], bn_at)
    own_bn, other_bn = wide_sib[0], wide_sib[1]
    g_bn_two[...] = jnp.where(
        k == 0,
        jnp.concatenate([own_bn[0:2], other_bn[0:2]], axis=1),
        jnp.concatenate([other_bn[0:2], own_bn[0:2]], axis=1),
    )
    for copy in sent:
        copy.wait_send()


def update_kernel(rates, *refs):
    take, give = refs[:20], refs[20:]
    rate_one, rate_bn_one, rate_two, rate_bn_two = rates
    w, g, m, v, mask, rank = (r[...] for r in take[:6])
    results = sparse_update(w, g * mask.astype(F32), m, v, mask, rank, rate_one)
    for ref, value in zip(give[:5], results):
        ref[...] = value
    w, g, m, v, mask, rank = (r[...] for r in take[6:12])
    results = sparse_update(w, g * mask.astype(F32), m, v, mask, rank, rate_two)
    for ref, value in zip(give[5:10], results):
        ref[...] = value
    w, g, m, v = (r[...] for r in take[12:16])
    for ref, value in zip(give[10:13], dense_update(w, g, m, v, rate_bn_one)):
        ref[...] = value
    w, g, m, v = (r[...] for r in take[16:20])
    for ref, value in zip(give[13:16], dense_update(w, g, m, v, rate_bn_two)):
        ref[...] = value


def fast_shards(
    images_in, labels, loss_wt, placement,
    w_one, mom_one, avg_one, mask_one, rank_one_in, first_norm_params, mom_bn_one, avg_bn_one,
    w_two, mom_two, avg_two, mask_two, rank_two, second_norm_params, mom_bn_two, avg_bn_two,
    w_head, mom_head, avg_head,
):
    n_img, n_ch = lax.axis_size("img"), lax.axis_size("ch")
    group, cin = images_in.shape[0], images_in.shape[2]
    per_core = labels.shape[0]
    per_chip = 2 * per_core
    width = second_norm_params.shape[1]
    half = width // 2
    own_ch = w_one.shape[1]
    chip_ch = 2 * own_ch
    classes = w_head.shape[0] * n_img * n_ch // width
    images = per_core * n_img * n_ch
    head_rows = w_head.shape[0] // classes
    lanes = -(-classes // 512) * 512
    block = w_two.shape[0] // width
    chunk = 2 * block
    flat = (w_two.shape[0] // 128, 128)
    headp = jnp.pad(
        w_head.astype(BF16).reshape(head_rows, classes), ((0, 0), (0, lanes - classes))
    )
    one = [a.T for a in (w_one, mom_one, avg_one, mask_one, rank_one_in)]
    two = [a.reshape(flat) for a in (w_two, mom_two, avg_two, mask_two, rank_two)]
    vmem = pl.BlockSpec(memory_space=pltpu.VMEM)
    smem = pl.BlockSpec(memory_space=pltpu.SMEM)
    hbm = pl.BlockSpec(memory_space=pl.ANY)
    v = pltpu.VMEM
    shape = jax.ShapeDtypeStruct
    g_one, g_two, g_head, g_bn_one, g_bn_two, loss = pl.pallas_call(
        functools.partial(step_kernel, (group, per_chip, classes, images)),
        out_shape=(
            shape((own_ch, cin), F32),
            shape(flat, F32),
            shape((head_rows, lanes), F32),
            shape((2, own_ch), F32),
            shape((2, width), F32),
            shape((1, 128), F32),
        ),
        in_specs=[hbm, vmem, smem, smem, vmem, vmem, vmem, vmem, vmem, vmem, vmem],
        out_specs=[vmem] * 6,
        scratch_shapes=[
            v((UPPER * SIDE, group, cin), BF16),
            v((chip_ch, cin), BF16),
            v((TAPS * width, half), BF16),
            v((4, 4, 2, head_rows, lanes), BF16),
            v((SIDE + 3, PITCH, per_chip, width), BF16),
            v((UPPER, SIDE, group, chip_ch), BF16),
            v((UPPER * SIDE * group, chip_ch), F32),
            v((SIDE, PITCH, per_chip, half), F32),
            v((SIDE, PITCH, per_chip, half), F32),
            v((2 * FRONT + SIDE * PITCH, per_chip, half), BF16),
            v((width + 16, SIDE * PITCH * per_chip), BF16),
            v((SIDE, PITCH, per_chip, width), F32),
            v((UPPER, SIDE, per_chip, width), BF16),
            v((UPPER, SIDE, per_chip, width), BF16),
            v((UPPER, SIDE, group, chip_ch), BF16),
            v((2, 8, 128), F32),
            v((4, 8, 128), F32),
            v((2, 2, 8, 128), F32),
            v((2, 4, 8, 128), F32),
            v((3, 4, 16, half), F32),
            v((3, 4, 16, half), F32),
            v((2, 8, half), F32),
            v((2, per_chip, lanes), F32),
            v((2, 4, 2, head_rows, lanes), BF16),
            v((TAPS * width, half), BF16),
            v((4, 4, head_rows, lanes), BF16),
            v((4, 2, chunk, half), BF16),
            v((4, 2, head_rows, lanes), BF16),
            v((4, chunk, half), BF16),
            v((4, head_rows, lanes), BF16),
            v((4, chunk, half), BF16),
            v((4, head_rows, lanes), BF16),
            v((chunk, half), F32),
            v((block, half), F32),
            v((16, half), F32),
            v((2 * width, half), F32),
            v((chip_ch, UPPER * SIDE * group), BF16),
            v((chip_ch, cin), F32),
            v((own_ch, cin), BF16),
            v((own_ch, cin), BF16),
            v((2, own_ch, cin), BF16),
            v((2, own_ch, cin), BF16),
            pltpu.SemaphoreType.DMA((UPPER,)),
            pltpu.SemaphoreType.DMA((2,)),
            pltpu.SemaphoreType.DMA((150,)),
            pltpu.SemaphoreType.DMA((150,)),
        ],
        compiler_params=pltpu.CompilerParams(
            collective_id=0, has_side_effects=True, vmem_limit_bytes=56 << 20
        ),
        name="step",
    )(
        images_in.transpose(1, 0, 2),
        placement,
        labels,
        loss_wt,
        one[0],
        one[3],
        first_norm_params,
        two[0],
        two[3],
        headp,
        second_norm_params,
    )
    root = math.sqrt(images)
    steps = 4
    one_spec = pl.BlockSpec((own_ch // steps, cin), lambda n: (n, 0))
    two_spec = pl.BlockSpec((flat[0] // steps, 128), lambda n: (n, 0))
    bno_spec = pl.BlockSpec((2, own_ch), lambda n: (0, 0))
    bnt_spec = pl.BlockSpec((2, width), lambda n: (0, 0))
    f_one, f_two = shape(one[0].shape, F32), shape(flat, F32)
    new = pl.pallas_call(
        functools.partial(update_kernel, (1.3 * root, 8.0 * root, 0.25 * root, root)),
        grid=(steps,),
        in_specs=[one_spec] * 6 + [two_spec] * 6 + [bno_spec] * 4 + [bnt_spec] * 4,
        out_specs=[one_spec] * 5 + [two_spec] * 5 + [bno_spec] * 3 + [bnt_spec] * 3,
        out_shape=[f_one] * 3 + [shape(f_one.shape, jnp.int32), shape(f_one.shape, BF16)]
        + [f_two] * 3 + [shape(flat, jnp.int32), shape(flat, BF16)]
        + [shape((2, own_ch), F32)] * 3 + [shape((2, width), F32)] * 3,
        compiler_params=pltpu.CompilerParams(vmem_limit_bytes=32 << 20),
        name="update",
    )(
        one[0], g_one, one[1], one[2], one[3], one[4],
        two[0], g_two, two[1], two[2], two[3], two[4],
        first_norm_params, g_bn_one, mom_bn_one, avg_bn_one,
        second_norm_params, g_bn_two, mom_bn_two, avg_bn_two,
    )
    g_head = g_head[:, :classes].reshape(-1)
    top_head = dense_update(w_head, g_head, mom_head, avg_head, 40.0)
    return (
        loss[0, 0],
        *(a.T for a in new[:5]),
        *new[10:13],
        *(a.reshape(-1) for a in new[5:10]),
        *new[13:16],
        *top_head,
        top_head[0].astype(BF16),
    )


def solution(mesh):
    in_specs = (
        P("img", None, None),
        P(("img", "ch")),
        P(("img", "ch")),
        P("img", None),
        P(None, "ch"),
        P(None, "ch"),
        P(None, "ch"),
        P(None, "ch"),
        P(None, "ch"),
        P(None, "ch"),
        P(None, "ch"),
        P(None, "ch"),
        P(("img", "ch")),
        P(("img", "ch")),
        P(("img", "ch")),
        P(("img", "ch")),
        P(("img", "ch")),
        P(),
        P(),
        P(),
        P(("img", "ch")),
        P(("img", "ch")),
        P(("img", "ch")),
    )
    out_specs = (
        P(),
        P(None, "ch"),
        P(None, "ch"),
        P(None, "ch"),
        P(None, "ch"),
        P(None, "ch"),
        P(None, "ch"),
        P(None, "ch"),
        P(None, "ch"),
        P(("img", "ch")),
        P(("img", "ch")),
        P(("img", "ch")),
        P(("img", "ch")),
        P(("img", "ch")),
        P(),
        P(),
        P(),
        P(("img", "ch")),
        P(("img", "ch")),
        P(("img", "ch")),
        P(("img", "ch")),
    )
    fast = mesh.shape["img"] == 4 and mesh.shape["ch"] == 8
    return jax.shard_map(fast_shards if fast else shards, mesh=mesh, in_specs=in_specs, out_specs=out_specs, check_vma=False)
```

```python
import functools
import itertools
import math

import jax
import jax.numpy as jnp
from jax import lax
from jax.experimental import pallas as pl
from jax.experimental.pallas import tpu as pltpu
from jax.sharding import PartitionSpec as P

SIDE = 7
PIX = 49
DROP = 10
GROW = 10


EPS = 1e-05
MOMENTUM = 0.5


def advance(weight, grad, velocity, rate):
    velocity = MOMENTUM * velocity + grad
    return (weight - rate * (grad + MOMENTUM * velocity), velocity)


def dense_update(weight, grad, velocity, average, rate):
    moved, velocity = advance(weight, grad, velocity, rate)
    return (moved, velocity, 0.5 * average + 0.5 * moved)


def sparse_update(weight, grad, velocity, average, mask, rank, rate):
    moved, velocity = advance(weight, grad, velocity, rate)
    kept = (mask == 1) & (rank >= DROP)
    grown = (mask == 0) & (rank < GROW)
    new_mask = jnp.where(kept | grown, 1, 0).astype(jnp.int32)
    weight = jnp.where(kept, moved, 0.0)
    velocity = jnp.where(kept, velocity, 0.0)
    average = 0.5 * average + 0.5 * weight
    return (weight, velocity, average, new_mask, weight.astype(jnp.bfloat16))


def silu_slope(value):
    sigma = jax.nn.sigmoid(value)
    return sigma * (1.0 + value * (1.0 - sigma))


def apply_batch_norm(z, sums, squares, element_count):
    mean = sums / element_count
    inverse_deviation = lax.rsqrt(squares / element_count - mean * mean + EPS)
    return ((z - mean) * inverse_deviation, inverse_deviation)


def batch_norm_backward(
    norm_gain,
    inverse_deviation,
    output_gradient,
    standardized_input,
    bias_gradient_sum,
    gain_gradient_sum,
    element_count,
):
    return (
        norm_gain
        * inverse_deviation
        * (
            output_gradient
            - bias_gradient_sum / element_count
            - standardized_input * gain_gradient_sum / element_count
        )
    )


def contract_rows(left, right):
    return jnp.einsum("pk,pc->kc", left, right, preferred_element_type=jnp.float32)


def shards(
    images_in,
    labels,
    loss_wt,
    placement,
    w_one,
    mom_one,
    avg_one,
    mask_one,
    rank_one,
    first_norm_params,
    mom_bn_one,
    avg_bn_one,
    w_two,
    mom_two,
    avg_two,
    mask_two,
    rank_two,
    second_norm_params,
    mom_bn_two,
    avg_bn_two,
    w_head,
    mom_head,
    avg_head,
):
    n_img = lax.axis_size("img")
    n_ch = lax.axis_size("ch")
    group = images_in.shape[0]
    element_count = labels.shape[0]
    width = second_norm_params.shape[1]
    classes = w_head.shape[0] * n_img * n_ch // width
    images = element_count * n_img * n_ch
    slot_info = jnp.stack([labels.astype(jnp.float32), loss_wt.astype(jnp.float32)])
    slot_info = lax.all_gather(slot_info, "ch", axis=1, tiled=True)
    own = lax.axis_index("ch") * element_count + jnp.arange(element_count, dtype=jnp.int32)
    fills = placement[0][None, :] == own[:, None]
    labels_f, weights = jnp.sum(jnp.where(fills[None], slot_info[:, None, :], 0.0), axis=2)
    labels = labels_f.astype(jnp.int32)
    kernel_part = (w_two * mask_two.astype(jnp.float32)).astype(jnp.bfloat16)
    kernel = lax.all_gather(kernel_part, ("img", "ch"), axis=0, tiled=True)
    head = lax.all_gather(w_head.astype(jnp.bfloat16), ("img", "ch"), axis=0, tiled=True)
    kernel = kernel.reshape(9 * width, width)
    head = head.reshape(width, classes)
    rows = images_in.transpose(1, 0, 2).reshape(PIX * group, images_in.shape[2])
    filt_one = (w_one * mask_one.astype(jnp.float32)).astype(jnp.bfloat16)
    first_conv_output = jnp.dot(rows, filt_one, preferred_element_type=jnp.float32)
    first_feature_sum, first_squares_sum, total = lax.psum(
        (
            jnp.sum(first_conv_output, axis=0),
            jnp.sum(first_conv_output * first_conv_output, axis=0),
            jnp.sum(slot_info[1]),
        ),
        "img",
    )
    first_element_count = group * PIX * n_img
    first_standardized_input, first_inverse_deviation = apply_batch_norm(
        first_conv_output, first_feature_sum, first_squares_sum, first_element_count
    )
    first_norm_output = first_norm_params[0] * first_standardized_input + first_norm_params[1]
    act = jax.nn.silu(first_norm_output).astype(jnp.bfloat16).reshape(PIX, group, -1)
    act_in = lax.all_to_all(act, "ch", split_axis=1, concat_axis=2, tiled=True)
    padded = jnp.pad(
        act_in.reshape(SIDE, SIDE, element_count, width), ((1, 1), (1, 1), (0, 0), (0, 0))
    )
    patches = jnp.concatenate(
        [
            padded[tap // 3 : tap // 3 + SIDE, tap % 3 : tap % 3 + SIDE].reshape(
                PIX * element_count, width
            )
            for tap in range(9)
        ],
        axis=1,
    )
    second_conv_output = jnp.dot(patches, kernel, preferred_element_type=jnp.float32)
    second_feature_sum, second_squares_sum = lax.psum(
        (
            jnp.sum(second_conv_output, axis=0),
            jnp.sum(second_conv_output * second_conv_output, axis=0),
        ),
        ("img", "ch"),
    )
    second_element_count = images * PIX
    second_standardized_input, second_inverse_deviation = apply_batch_norm(
        second_conv_output, second_feature_sum, second_squares_sum, second_element_count
    )
    second_norm_output = second_norm_params[0] * second_standardized_input + second_norm_params[1]
    pooled = jnp.mean(jax.nn.silu(second_norm_output).reshape(PIX, element_count, width), axis=0)
    pooled_low = pooled.astype(jnp.bfloat16)
    logits = jnp.dot(pooled_low, head, preferred_element_type=jnp.float32)
    top = jnp.max(logits, axis=1, keepdims=True)
    expd = jnp.exp(logits - top)
    denom = jnp.sum(expd, axis=1, keepdims=True)
    lse = top[:, 0] + jnp.log(denom[:, 0])
    onehot = labels[:, None] == jnp.arange(classes, dtype=jnp.int32)[None, :]
    picked = jnp.sum(jnp.where(onehot, logits, 0.0), axis=1)
    share = weights / total
    partial_loss_value = jnp.sum(share * (lse - picked))
    d_logits = (share[:, None] * (expd / denom - onehot.astype(jnp.float32))).astype(jnp.bfloat16)
    g_head = contract_rows(pooled_low, d_logits)
    d_pooled = jnp.einsum("ic,kc->ik", d_logits, head, preferred_element_type=jnp.float32)
    d_act = jnp.broadcast_to(d_pooled[None] / PIX, (PIX, element_count, width)).reshape(
        PIX * element_count, width
    )
    second_output_gradient = d_act * silu_slope(second_norm_output)
    second_shift_bias, second_norm_gain, loss = lax.psum(
        (
            jnp.sum(second_output_gradient, axis=0),
            jnp.sum(second_output_gradient * second_standardized_input, axis=0),
            partial_loss_value,
        ),
        ("img", "ch"),
    )
    second_preact_gradient = batch_norm_backward(
        second_norm_params[0],
        second_inverse_deviation,
        second_output_gradient,
        second_standardized_input,
        second_shift_bias,
        second_norm_gain,
        second_element_count,
    ).astype(jnp.bfloat16)
    d_patches = jnp.einsum(
        "pc,kc->pk", second_preact_gradient, kernel, preferred_element_type=jnp.float32
    )
    d_pad = 0.0
    for tap in range(9):
        piece = d_patches[:, tap * width : (tap + 1) * width].reshape(
            SIDE, SIDE, element_count, width
        )
        up, left = tap // 3, tap % 3
        d_pad = d_pad + jnp.pad(piece, ((up, 2 - up), (left, 2 - left), (0, 0), (0, 0)))
    d_act_in = d_pad[1:-1, 1:-1].astype(jnp.bfloat16).reshape(PIX, element_count, width)
    d_act_one = lax.all_to_all(d_act_in, "ch", split_axis=2, concat_axis=1, tiled=True)
    g_kernel = contract_rows(patches, second_preact_gradient)
    d_act_one = d_act_one.reshape(PIX * group, -1).astype(jnp.float32)
    first_output_gradient = d_act_one * silu_slope(first_norm_output)
    first_shift_bias, first_norm_gain = lax.psum(
        (
            jnp.sum(first_output_gradient, axis=0),
            jnp.sum(first_output_gradient * first_standardized_input, axis=0),
        ),
        "img",
    )
    first_preact_gradient = batch_norm_backward(
        first_norm_params[0],
        first_inverse_deviation,
        first_output_gradient,
        first_standardized_input,
        first_shift_bias,
        first_norm_gain,
        first_element_count,
    ).astype(jnp.bfloat16)
    g_filt = lax.psum(
        contract_rows(rows, first_preact_gradient).astype(jnp.bfloat16), "img"
    ).astype(jnp.float32)
    g_one = g_filt * mask_one.astype(jnp.float32)
    part_two = lax.psum_scatter(
        g_kernel.reshape(-1), ("img", "ch"), tiled=True
    )
    part_head = lax.psum_scatter(
        g_head.reshape(-1), ("img", "ch"), tiled=True
    )
    g_two = part_two * mask_two.astype(jnp.float32)
    root = math.sqrt(images)
    one = sparse_update(w_one, g_one, mom_one, avg_one, mask_one, rank_one, 1.3 * root)
    bno = dense_update(
        first_norm_params,
        jnp.stack([first_norm_gain, first_shift_bias]),
        mom_bn_one,
        avg_bn_one,
        8.0 * root,
    )
    two = sparse_update(w_two, g_two, mom_two, avg_two, mask_two, rank_two, 0.25 * root)
    bnt = dense_update(
        second_norm_params,
        jnp.stack([second_norm_gain, second_shift_bias]),
        mom_bn_two,
        avg_bn_two,
        root,
    )
    top_head = dense_update(w_head, part_head, mom_head, avg_head, 40.0)
    return (
        loss,
        one[0],
        one[1],
        one[2],
        one[3],
        one[4],
        bno[0],
        bno[1],
        bno[2],
        two[0],
        two[1],
        two[2],
        two[3],
        two[4],
        bnt[0],
        bnt[1],
        bnt[2],
        top_head[0],
        top_head[1],
        top_head[2],
        top_head[0].astype(jnp.bfloat16),
    )


F32, BF16 = jnp.float32, jnp.bfloat16
MESH = pl.DeviceIdType.MESH
TAPS = 9
UPPER = (SIDE + 1) // 2
PITCH = SIDE + 1
FRONT = 2 * PITCH
SEMS = 240


def silu_pair(value):
    sigma = 1.0 / (1.0 + jnp.exp(-value))
    return value * sigma, sigma * (1.0 + value * (1.0 - sigma))


def matmul_nt(left, right):
    return lax.dot_general(left, right, (((1,), (1,)), ((), ())), preferred_element_type=F32)


def matmul_tn(left, right):
    return lax.dot_general(left, right, (((0,), (0,)), ((), ())), preferred_element_type=F32)


def rank_one(row, other):
    first = other.astype(BF16)
    rest = other - first.astype(F32)
    second = rest.astype(BF16)
    third = (rest - second.astype(F32)).astype(BF16)
    place = lax.broadcasted_iota(jnp.int32, (16, other.shape[1]), 0)
    parts = jnp.where(place == 0, first.astype(F32), 0.0)
    parts = jnp.where(place == 1, second.astype(F32), parts)
    parts = jnp.where(place == 2, third.astype(F32), parts)
    rows = jnp.broadcast_to(row, (16, row.shape[1])).astype(BF16)
    return matmul_tn(rows, parts.astype(BF16))


def step_kernel(
    sizes,
    images,
    place,
    labels,
    loss_wt,
    w_one,
    mask_one,
    norm_one,
    w_two,
    mask_two,
    w_head,
    norm_two,
    g_one,
    g_two,
    g_head,
    g_bn_one,
    g_bn_two,
    loss,
    feats,
    filt,
    kern,
    head,
    act_in,
    act_out,
    z_one,
    z_two,
    slope,
    d_pad,
    act_t,
    d_act,
    d_send,
    d_recv,
    d_one,
    early,
    info,
    tiles,
    wide,
    wide_sib,
    logit,
    gh_half,
    gk,
    gh,
    rk_one,
    rh_one,
    rk_two,
    rh_two,
    rk_z,
    rh_z,
    h_sum,
    head_flat,
    last_send,
    last_recv,
    edge_rows,
    ranked,
    grad_t,
    g_acc,
    go_send,
    go_recv,
    ga_send,
    ga_recv,
    image_sem,
    local_sem,
    send,
    recv,
):
    group, per_chip, classes, images_in_all = sizes
    width = norm_two.shape[1]
    half = width // 2
    own_ch = w_one.shape[0]
    chip_ch = 2 * own_ch
    block = w_two.shape[0] * 128 // width
    chunk = 2 * block
    head_rows = head.shape[3]
    rows_a = SIDE * group
    rows_c = PITCH * per_chip
    count_all = float(images_in_all * PIX)

    i, c = lax.axis_index("img"), lax.axis_index("ch")
    z, k = lax.div(c, 2), lax.rem(c, 2)
    sib = c + 1 - 2 * k
    xn, yn, dg = i + 1 - 2 * lax.rem(i, 2), lax.rem(i + 2, 4), 3 - i
    lines = (xn, yn, dg)
    near = (z, z + 1 - 2 * lax.rem(z, 2), 2 - lax.div(z, 2), 3 - 3 * lax.div(z, 2))
    h0 = (SIDE - UPPER) * k

    def chip(dz):
        return near[dz]

    def zdev(dz):
        return 2 * chip(dz) + k

    next_send, next_recv = itertools.count(), itertools.count()
    sent = []

    def new_recv(n=1):
        first = next(next_recv)
        for _ in range(n - 1):
            next(next_recv)
        return first

    def push(src, dst, device, to):
        copy = pltpu.make_async_remote_copy(
            src_ref=src,
            dst_ref=dst,
            send_sem=send.at[next(next_send)],
            recv_sem=recv.at[to],
            device_id=device,
            device_id_type=MESH,
        )
        copy.start()
        sent.append(copy)
        return copy

    def arrived(dst, at):
        pltpu.make_async_remote_copy(
            src_ref=dst,
            dst_ref=dst,
            send_sem=send.at[0],
            recv_sem=recv.at[at],
            device_id=(i, sib),
            device_id_type=MESH,
        ).wait_recv()

    def image_copy(r):
        return pltpu.make_async_copy(
            images.at[pl.ds(SIDE * (h0 + r), SIDE)], feats.at[pl.ds(SIDE * r, SIDE)], image_sem.at[r]
        )

    for r in range(UPPER):
        image_copy(r).start()

    act_in[0] = jnp.zeros(act_in.shape[1:], BF16)
    for r in range(SIDE + 1, act_in.shape[0]):
        act_in[r] = jnp.zeros(act_in.shape[1:], BF16)
    for r in range(1, SIDE + 1):
        act_in[r, 0] = jnp.zeros(act_in.shape[2:], BF16)
    chunk_at = pl.multiple_of(chunk * (i * 4 + z), 32)
    block_at = pl.multiple_of(chunk_at + block * k, 16)
    parts = [
        w_two[pl.ds(j, block, stride=4), :] * mask_two[pl.ds(j, block, stride=4), :].astype(F32)
        for j in range(4)
    ]
    low = jnp.concatenate(parts[:2], axis=1).astype(BF16)
    high = jnp.concatenate(parts[2:], axis=1).astype(BF16)
    kern[pl.ds(block_at, block), :] = jnp.where(k == 0, low.astype(F32), high.astype(F32)).astype(BF16)
    gk[pl.ds(0, block), :] = jnp.where(k == 0, high.astype(F32), low.astype(F32)).astype(BF16)
    own_at = pl.multiple_of(own_ch * k, 16)
    filt[pl.ds(own_at, own_ch), :] = (w_one[...] * mask_one[...].astype(F32)).astype(BF16)
    lane = lax.broadcasted_iota(jnp.int32, (1, 128), 1)
    for r in range(head_rows):
        first, shift = divmod(classes * r, 128)
        taken = -(-(shift + classes) // 128)
        rows = w_head[first : first + taken, :]
        if taken < 9:
            rows = jnp.concatenate([rows, jnp.zeros((9 - taken, 128), F32)], axis=0)
        if shift:
            rows = pltpu.roll(rows, 128 - shift, 1)
            rows = jnp.where(lane < 128 - shift, rows[:8], rows[1:9])
        for j in range(8):
            head_flat[r : r + 1, 128 * j : 128 * j + 128] = rows[j : j + 1]
    head_lane = lax.broadcasted_iota(jnp.int32, (head_rows, 1024), 1)
    head[i, z, k] = jnp.where(head_lane < classes, head_flat[...], 0.0).astype(BF16)
    norms = norm_one[...]
    nothing = jnp.zeros_like(norms)
    placed = jnp.where(
        k == 0, jnp.concatenate([norms, nothing], axis=1), jnp.concatenate([nothing, norms], axis=1)
    )
    label_row, weight_row = jnp.zeros((1, 128), F32), jnp.zeros((1, 128), F32)
    for j in range(labels.shape[0]):
        here = lane == labels.shape[0] * c + j
        label_row = jnp.where(here, labels[j].astype(F32), label_row)
        weight_row = jnp.where(here, loss_wt[j].astype(F32), weight_row)
    early[0] = jnp.concatenate(
        [placed, label_row, weight_row, jnp.zeros((4, 128), F32)], axis=0
    )

    barrier = pltpu.get_barrier_semaphore()
    same_core = [(o, zdev(dz)) for o in (i, *lines) for dz in (0, 1, 2, 3)][1:]
    plane = [(i, sib)] + [(o, d) for o in lines for d in (c, sib)]
    others = same_core + [plane[0]] + [p for p in plane[1:] if p[1] is sib]
    for device in others:
        pl.semaphore_signal(barrier, inc=1, device_id=device, device_id_type=MESH)
    pl.semaphore_wait(barrier, len(others))

    k_sib, f_sib, e_sib = new_recv(), new_recv(), new_recv()
    push(gk.at[pl.ds(0, block)], kern.at[pl.ds(block_at, block)], (i, sib), k_sib)
    push(filt.at[pl.ds(own_at, own_ch)], filt.at[pl.ds(own_at, own_ch)], (i, sib), f_sib)
    push(early.at[0], early.at[1], (i, sib), e_sib)

    k_recv, h_recv = new_recv(16), new_recv(16)

    def kern_at(line, dz):
        return kern.at[pl.ds(pl.multiple_of(chunk * (line * 4 + chip(dz)), 32), chunk)]

    def head_at(line, dz):
        return head.at[line, chip(dz), k]

    def number(line, dz):
        return line * 4 + chip(dz)

    def forward(line, dz, device):
        push(kern_at(line, dz), kern_at(line, dz), device, k_recv + number(line, dz))

    def landed(line, dz):
        arrived(kern_at(line, dz), k_recv + number(line, dz))

    def head_forward(line, dz, device):
        push(head_at(line, dz), head_at(line, dz), device, h_recv + number(line, dz))

    def head_landed(line, dz):
        arrived(head_at(line, dz), h_recv + number(line, dz))

    other_block_at = pl.multiple_of(chunk_at + block * (1 - k), 16)
    arrived(kern.at[pl.ds(other_block_at, block)], k_sib)
    forward(i, 0, (xn, c))
    forward(i, 0, (yn, c))
    for dz in (1, 2, 3):
        forward(i, 0, (i, zdev(dz)))
    arrived(early.at[1], e_sib)
    both = early[0] + early[1]
    info[z] = both
    i_recv = new_recv(4)
    for dz in (1, 2, 3):
        push(info.at[z], info.at[z], (i, zdev(dz)), i_recv + z)
    other_at = pl.multiple_of(own_ch * (1 - k), 16)
    arrived(filt.at[pl.ds(other_at, own_ch)], f_sib)

    def first_conv(r, carry):
        sums, squares = carry
        image_copy(r).wait()
        rows = feats[pl.ds(SIDE * r, SIDE)].reshape(rows_a, feats.shape[2])
        out = matmul_nt(rows, filt[...])
        z_one[pl.ds(pl.multiple_of(rows_a * r, 64), rows_a), :] = out
        counted = jnp.where((r == 0) & (k == 1), 0.0, 1.0)
        return (
            sums + counted * jnp.sum(out, axis=0, keepdims=True),
            squares + counted * jnp.sum(out * out, axis=0, keepdims=True),
        )

    zero_row = jnp.zeros((1, chip_ch), F32)
    sums, squares = lax.fori_loop(0, UPPER, first_conv, (zero_row, zero_row))

    def small_sum(turn, rows):
        own = 2 * i + k
        tiles[turn, own] = rows
        at = new_recv(8)
        for device in plane:
            push(tiles.at[turn, own], tiles.at[turn, own], device, at + own)

        def finish():
            for line in (i, *lines):
                arrived(tiles.at[turn, 2 * line + 1 - k], at + 2 * line + 1 - k)
                if line is not i:
                    arrived(tiles.at[turn, 2 * line + k], at + 2 * line + k)
            result = tiles[turn, 0]
            for n in range(1, 8):
                result = result + tiles[turn, n]
            return result

        return finish

    finish = small_sum(0, jnp.concatenate([sums, squares, jnp.zeros((6, 128), F32)], axis=0))
    landed(i, 1)
    forward(i, 1, (xn, c))
    forward(i, 1, (yn, c))
    landed(xn, 0)
    forward(xn, 0, (yn, c))
    totals = finish()
    mean_one = totals[0:1] / count_all
    inv_one = lax.rsqrt(totals[1:2] / count_all - mean_one * mean_one + EPS)
    gain_one, bias_one = both[0:1], both[1:2]

    def first_act(r):
        at = slice(rows_a * r, rows_a * r + rows_a)
        hat = (z_one[at, :] - mean_one) * inv_one
        value, grade = silu_pair(gain_one * hat + bias_one)
        act_out[r] = value.astype(BF16).reshape(SIDE, group, chip_ch)

    a_recv = new_recv(4 * UPPER)

    def into(r, chip_id):
        return act_in.at[
            1 + h0 + r, pl.ds(1, SIDE), :, pl.ds(pl.multiple_of(chip_ch * chip_id, 128), chip_ch)
        ]

    def images_of(ref, dz):
        return ref.at[:, :, pl.ds(pl.multiple_of(per_chip * chip(dz), 16), per_chip), :]

    def images_in_row(ref, r, dz):
        return ref.at[r, :, pl.ds(pl.multiple_of(per_chip * chip(dz), 16), per_chip), :]

    out_copies, kept = [], []
    for r in range(UPPER):
        first_act(r)
        for dz in (3, 2, 1):
            out_copies.append(
                push(images_in_row(act_out, r, dz), into(r, z), (i, zdev(dz)), a_recv + 4 * r + z)
            )
        kept.append(
            pltpu.make_async_copy(images_in_row(act_out, r, 0), into(r, z), local_sem.at[r])
        )
        kept[-1].start()
    landed(i, 2)
    forward(i, 2, (xn, c))
    forward(i, 2, (yn, c))
    landed(xn, 1)
    forward(xn, 1, (yn, c))
    landed(i, 3)
    forward(i, 3, (xn, c))
    forward(i, 3, (yn, c))
    landed(yn, 2)
    forward(yn, 2, (xn, c))
    landed(yn, 3)
    forward(yn, 3, (xn, c))
    head_forward(i, 0, (xn, c))
    head_forward(i, 0, (yn, c))
    for dz in (1, 2, 3):
        head_forward(i, 0, (i, zdev(dz)))

    for copy in kept:
        copy.wait()
    for r in range(UPPER):
        for dz in (1, 2, 3):
            arrived(into(r, chip(dz)), a_recv + 4 * r + chip(dz))
    a_sib = new_recv()
    mine = act_in.at[pl.ds(1 + UPPER * k, SIDE - UPPER), pl.ds(1, SIDE)]
    push(mine, mine, (i, sib), a_sib)
    for line, dz in ((yn, 0), (yn, 1), (xn, 2), (xn, 3), (dg, 0), (dg, 1), (dg, 2), (dg, 3)):
        landed(line, dz)
    arrived(act_in.at[pl.ds(1 + UPPER * (1 - k), SIDE - UPPER), pl.ds(1, SIDE)], a_sib)

    def tap_of(t):
        return t // 3, t % 3

    def second_conv(h, carry):
        sums, squares = carry
        out = jnp.zeros((rows_c, half), F32)
        for t in range(TAPS):
            up, left = tap_of(t)
            wide = act_in[pl.ds(h + up, 2)].reshape(2 * PITCH, per_chip, width)
            rows = wide[left : left + PITCH].reshape(rows_c, width)
            out = out + jnp.dot(
                rows, kern[pl.ds(width * t, width), :], preferred_element_type=F32
            )
        z_two[h] = out.reshape(PITCH, per_chip, half)
        real = out[: SIDE * per_chip]
        return (
            sums + jnp.sum(real, axis=0, keepdims=True),
            squares + jnp.sum(real * real, axis=0, keepdims=True),
        )

    zero_half = jnp.zeros((1, half), F32)
    sums, squares = lax.fori_loop(0, SIDE, second_conv, (zero_half, zero_half))

    def act_sum(h, carry):
        rows = act_in[h + 1].reshape(rows_c, width).astype(F32)
        return carry + jnp.sum(rows, axis=0, keepdims=True)

    act_sums = lax.fori_loop(0, SIDE, act_sum, jnp.zeros((1, width), F32))

    def wide_sum(turn, rows):
        own, size = 4 * i + z, rows.shape[0]
        wide[turn, own, pl.ds(0, size)] = rows
        at = new_recv(16)

        def tile(number):
            return wide.at[turn, number, pl.ds(0, size)]

        for device in same_core[::-1]:
            push(tile(own), tile(own), device, at + own)

        def finish():
            for line in (i, *lines):
                for dz in (0, 1, 2, 3):
                    if not (line is i and dz == 0):
                        arrived(tile(4 * line + chip(dz)), at + 4 * line + chip(dz))
            result = wide[turn, 0, pl.ds(0, size)]
            for n in range(1, 16):
                result = result + wide[turn, n, pl.ds(0, size)]
            return result

        return finish

    chip_weight = jnp.sum(both[3:4], axis=1, keepdims=True)
    finish = wide_sum(
        0,
        jnp.concatenate(
            [
                sums,
                squares,
                act_sums[:, :half],
                act_sums[:, half:],
                jnp.broadcast_to(chip_weight, (1, half)),
                jnp.zeros((3, half), F32),
            ],
            axis=0,
        ),
    )
    for dz in (1, 2, 3):
        head_landed(i, dz)
        head_forward(i, dz, (xn, c))
        head_forward(i, dz, (yn, c))
    inner = act_in[pl.ds(1, SIDE + 1)].reshape((SIDE + 1) * PITCH, per_chip, width)
    inner = inner[1 : 1 + SIDE * PITCH].reshape(SIDE * rows_c, width)
    act_t[pl.ds(0, width), :] = inner.T
    column = lax.broadcasted_iota(jnp.int32, (16, SIDE * rows_c), 1)
    is_real = lax.rem(lax.div(column, per_chip), PITCH) < SIDE
    act_t[pl.ds(width, 16), :] = jnp.where(is_real, 1.0, 0.0).astype(BF16)
    d_pad[pl.ds(0, FRONT)] = jnp.zeros((FRONT, per_chip, half), BF16)
    d_pad[pl.ds(FRONT + SIDE * PITCH, FRONT)] = jnp.zeros((FRONT, per_chip, half), BF16)
    for dz in (0, 1):
        head_landed(xn, dz)
        head_forward(xn, dz, (yn, c))
    for dz in (2, 3):
        head_landed(yn, dz)
        head_forward(yn, dz, (xn, c))
    totals_two = finish()
    total = totals_two[4:5, 0:1]
    mean_two = totals_two[0:1] / count_all
    inv_two = lax.rsqrt(totals_two[1:2] / count_all - mean_two * mean_two + EPS)
    centre = jnp.concatenate([totals_two[2:3], totals_two[3:4]], axis=1) / count_all
    centre = centre.astype(BF16).astype(F32)
    norms_two = jnp.where(k == 0, norm_two[:, :half], norm_two[:, half:])
    gain_two, bias_two = norms_two[0:1], norms_two[1:2]

    def second_act(h, pooled):
        hat = (z_two[h] - mean_two) * inv_two
        z_two[h] = hat
        value, grade = silu_pair(gain_two * hat + bias_two)
        slope[h] = grade
        return pooled + jnp.sum(value[:SIDE], axis=0)

    pooled = lax.fori_loop(0, SIDE, second_act, jnp.zeros((per_chip, half), F32)) / PIX
    pooled_low = pooled.astype(BF16)

    for line, dz in ((yn, 0), (yn, 1), (xn, 2), (xn, 3), (dg, 0), (dg, 1), (dg, 2), (dg, 3)):
        head_landed(line, dz)
    hd_sib = new_recv()
    theirs = head.at[pl.ds(2 * (1 - k), 2), :, k]
    push(theirs, theirs, (i, sib), hd_sib)
    for dz in (1, 2, 3):
        arrived(info.at[chip(dz)], i_recv + chip(dz))
    slots = info[0] + info[1] + info[2] + info[3]
    arrived(head.at[pl.ds(2 * k, 2), :, 1 - k], hd_sib)
    head_half = head[pl.ds(2 * k, 2)].reshape(half, head.shape[4])
    logit[0] = jnp.dot(pooled_low, head_half, preferred_element_type=F32)
    at = new_recv()
    push(logit.at[0], logit.at[1], (i, sib), at)
    image_id = per_chip * z + lax.broadcasted_iota(jnp.int32, (per_chip, group), 0)
    fills = place[...] == image_id
    label = jnp.sum(jnp.where(fills, slots[2:3, :group], 0.0), axis=1, keepdims=True).astype(jnp.int32)
    weight = jnp.sum(jnp.where(fills, slots[3:4, :group], 0.0), axis=1, keepdims=True)
    share = weight / total
    arrived(logit.at[1], at)
    logits = logit[0] + logit[1]
    klass = lax.broadcasted_iota(jnp.int32, logits.shape, 1)
    inside = klass < classes
    top = jnp.max(jnp.where(inside, logits, -jnp.inf), axis=1, keepdims=True)
    expd = jnp.where(inside, jnp.exp(jnp.where(inside, logits - top, 0.0)), 0.0)
    denom = jnp.sum(expd, axis=1, keepdims=True)
    onehot = klass == label
    picked = jnp.sum(jnp.where(onehot, logits, 0.0), axis=1, keepdims=True)
    partial = jnp.sum(share * (top + jnp.log(denom) - picked), axis=0, keepdims=True)
    d_logits = (share * (expd / denom - jnp.where(onehot, 1.0, 0.0))).astype(BF16)
    d_pooled = matmul_nt(d_logits, head_half) / PIX

    def second_back(h, carry):
        sums, products = carry
        d_y = d_pooled[None] * slope[h]
        slope[h] = d_y
        d_y = d_y[:SIDE].reshape(SIDE * per_chip, half)
        hat = z_two[h][:SIDE].reshape(SIDE * per_chip, half)
        return (
            sums + jnp.sum(d_y, axis=0, keepdims=True),
            products + jnp.sum(d_y * hat, axis=0, keepdims=True),
        )

    d_bias, d_gain = lax.fori_loop(0, SIDE, second_back, (zero_half, zero_half))

    finish = wide_sum(
        1,
        jnp.concatenate(
            [d_gain, d_bias, jnp.broadcast_to(partial, (1, half)), jnp.zeros((5, half), F32)], axis=0
        ),
    )
    gh_swap = new_recv()
    gh_half[...] = matmul_tn(pooled_low, d_logits).astype(BF16).reshape(gh_half.shape)
    push(gh_half.at[:, :, 1 - k], gh.at[pl.ds(2 * k, 2)], (i, sib), gh_swap)
    gh[pl.ds(2 * k, 2)] = jnp.where(
        k == 0, gh_half[:, :, 0].astype(F32), gh_half[:, :, 1].astype(F32)
    ).astype(BF16)
    arrived(gh.at[pl.ds(2 * (1 - k), 2)], gh_swap)
    h_one, h_two, h_z = new_recv(4), new_recv(2), new_recv(4)
    for way, first in enumerate((xn, yn)):
        part = pl.ds(2 * way, 2)
        push(gh.at[dg, part], rh_one.at[way, 1], (first, c), h_one + 2 * way + 1)
        push(gh.at[first, part], rh_one.at[way, 0], (first, c), h_one + 2 * way)
    totals_back = finish()
    loss[...] = totals_back[2:3, :128]
    wide_sib[0] = totals_back
    bn_at = new_recv()
    push(wide_sib.at[0], wide_sib.at[1], (i, sib), bn_at)
    scale = gain_two * inv_two
    shift_two, lean_two = totals_back[1:2] / count_all, totals_back[0:1] / count_all

    def second_grad(h, carry):
        grad = scale * (slope[h] - shift_two - z_two[h] * lean_two)
        pixel = lax.broadcasted_iota(jnp.int32, grad.shape, 0)
        grad = jnp.where(pixel < SIDE, grad, 0.0)
        d_pad[pl.ds(FRONT + PITCH * h, PITCH)] = grad.astype(BF16)
        return carry

    lax.fori_loop(0, SIDE, second_grad, 0)

    def back_conv(h):
        out = jnp.zeros((rows_c, width), F32)
        for t in range(TAPS):
            up, left = tap_of(t)
            rows = d_pad[pl.ds(PITCH * h + FRONT + PITCH + 1 - PITCH * up - left, PITCH)]
            out = out + matmul_nt(rows.reshape(rows_c, half), kern[pl.ds(width * t, width), :])
        return out.reshape(PITCH, per_chip, width)

    s0 = (SIDE - UPPER) * (1 - k)

    def back_theirs(r, carry):
        out = back_conv(s0 + r)
        d_act[s0 + r] = out
        d_send[r] = out[:SIDE].astype(BF16)
        return carry

    def back_mine(r, carry):
        d_act[UPPER * k + r] = back_conv(UPPER * k + r)
        return carry

    lax.fori_loop(0, UPPER, back_theirs, 0)
    d_at = new_recv()
    push(d_send, d_recv, (i, sib), d_at)
    for way, second in enumerate((yn, xn)):
        part = pl.ds(2 * way, 2)
        arrived(rh_one.at[way, 1], h_one + 2 * way + 1)
        gh[second, part] = (gh[second, part].astype(F32) + rh_one[way, 1].astype(F32)).astype(BF16)
        push(gh.at[second, part], rh_two.at[way], (second, c), h_two + way)
    lax.fori_loop(0, SIDE - UPPER, back_mine, 0)

    def kernel_gradient(t, carry):
        rows = d_pad[pl.ds(FRONT + PITCH + 1 - PITCH * lax.div(t, 3) - lax.rem(t, 3), SIDE * PITCH)]
        out = jnp.dot(
            act_t[...], rows.reshape(SIDE * rows_c, half), preferred_element_type=F32
        )
        edge = out[width : width + 1]
        edge_rows[pl.ds(t, 1)] = edge
        gk[pl.ds(pl.multiple_of(width * t, 32), width), :] = (
            out[:width] - rank_one(centre, edge)
        ).astype(BF16)
        return carry

    arrived(d_recv, d_at)
    for r in range(UPPER):
        d_send_r = d_act[h0 + r][:SIDE] + d_recv[r].astype(F32)
        d_recv[r] = d_send_r.astype(BF16)
    b_recv = new_recv(4)
    back_into = images_of(d_one, 0)

    def channels_of(dz):
        return d_recv.at[:, :, :, pl.ds(pl.multiple_of(chip_ch * chip(dz), 128), chip_ch)]

    for dz in (1, 2, 3):
        push(channels_of(dz), back_into, (i, zdev(dz)), b_recv + z)
    keep = pltpu.make_async_copy(channels_of(0), back_into, local_sem.at[UPPER])
    keep.start()

    sent.pop(0).wait_send()
    edge_rows[...] = jnp.zeros(edge_rows.shape, F32)
    lax.fori_loop(0, TAPS, kernel_gradient, 0)
    def gk_at(line, dz):
        return gk.at[pl.ds(pl.multiple_of(chunk * (line * 4 + chip(dz)), 32), chunk)]

    ways = {1: (xn, yn), 2: (yn, xn), 3: (xn, yn), 0: (yn, xn)}
    one_at = {dz: new_recv(2) for dz in (3, 2, 1, 0)}
    two_at = {dz: new_recv() for dz in (3, 2, 1, 0)}
    z_at = new_recv(4)

    def start_one(dz):
        first, second = ways[dz]
        push(gk_at(dg, dz), rk_one.at[dz, 1], (first, c), one_at[dz] + 1)
        push(gk_at(first, dz), rk_one.at[dz, 0], (first, c), one_at[dz])

    def start_two(dz):
        first, second = ways[dz]
        arrived(rk_one.at[dz, 1], one_at[dz] + 1)
        into_k = gk_at(second, dz)
        into_k[...] = (into_k[...].astype(F32) + rk_one[dz, 1].astype(F32)).astype(BF16)
        push(into_k, rk_two.at[dz], (second, c), two_at[dz])

    def plane_done(dz):
        arrived(rk_one.at[dz, 0], one_at[dz])
        arrived(rk_two.at[dz], two_at[dz])
        into_k = gk_at(i, dz)
        sum_k = into_k[...].astype(F32) + rk_one[dz, 0].astype(F32) + rk_two[dz].astype(F32)
        if dz == 0:
            return sum_k
        into_k[...] = sum_k.astype(BF16)
        push(into_k, rk_z.at[z], (i, zdev(dz)), z_at + z)
        return None

    start_one(3)
    start_one(2)
    for way in (0, 1):
        part = pl.ds(2 * way, 2)
        arrived(rh_one.at[way, 0], h_one + 2 * way)
        arrived(rh_two.at[way], h_two + way)
        sum_h = gh[i, part].astype(F32) + rh_one[way, 0].astype(F32) + rh_two[way].astype(F32)
        h_sum[part] = sum_h
        gh[i, part] = sum_h.astype(BF16)
    for dz in (3, 2, 1):
        push(gh.at[i, chip(dz)], rh_z.at[z], (i, zdev(dz)), h_z + z)

    keep.wait()
    for dz in (1, 2, 3):
        arrived(images_of(d_one, dz), b_recv + chip(dz))

    def first_back(r, carry):
        sums, products = carry
        at = pl.ds(pl.multiple_of(rows_a * r, 64), rows_a)
        hat = (z_one[at, :] - mean_one) * inv_one
        z_one[at, :] = hat
        _, grade = silu_pair(gain_one * hat + bias_one)
        d_y = d_one[r].reshape(rows_a, chip_ch).astype(F32) * grade
        counted = jnp.where((r == 0) & (k == 1), 0.0, 1.0)
        return (
            sums + counted * jnp.sum(d_y, axis=0, keepdims=True),
            products + counted * jnp.sum(d_y * hat, axis=0, keepdims=True),
        )

    d_bias, d_gain = lax.fori_loop(0, UPPER, first_back, (zero_row, zero_row))
    finish = small_sum(
        1, jnp.concatenate([d_gain, d_bias, jnp.zeros((6, 128), F32)], axis=0)
    )
    start_two(3)
    start_two(2)
    start_one(1)
    start_one(0)
    finish_edges = wide_sum(2, edge_rows[...])
    totals_one = finish()
    g_bn_one[...] = jnp.where(k == 0, totals_one[0:2, :own_ch], totals_one[0:2, own_ch:])
    scale_one = gain_one * inv_one
    shift_one, lean_one = totals_one[1:2] / count_all, totals_one[0:1] / count_all

    def first_grad(r, carry):
        at = pl.ds(pl.multiple_of(rows_a * r, 64), rows_a)
        hat = z_one[at, :]
        _, grade = silu_pair(gain_one * hat + bias_one)
        d_y = d_one[r].reshape(rows_a, chip_ch).astype(F32) * grade
        counted = jnp.where((r == 0) & (k == 1), 0.0, 1.0)
        grad = (counted * scale_one) * (d_y - shift_one - hat * lean_one)
        act_out[r] = grad.astype(BF16).reshape(SIDE, group, chip_ch)
        return carry

    for copy in out_copies:
        copy.wait_send()
    sent[:] = [copy for copy in sent if all(copy is not done for done in out_copies)]
    lax.fori_loop(0, UPPER, first_grad, 0)

    grad_t[...] = act_out[...].reshape(UPPER * rows_a, chip_ch).T

    def first_weights(n, carry):
        at = pl.ds(pl.multiple_of(256 * n, 256), 256)
        rows = feats[:, :, at].reshape(UPPER * rows_a, 256)
        g_acc[:, at] = jnp.dot(grad_t[...], rows, preferred_element_type=F32)
        return carry

    lax.fori_loop(0, feats.shape[2] // 256, first_weights, 0)
    low, high = g_acc[:own_ch], g_acc[own_ch:]
    go_send[...] = jnp.where(k == 0, high, low).astype(BF16)
    g_at = new_recv()
    push(go_send, go_recv, (i, sib), g_at)
    g_one[...] = jnp.where(k == 0, low, high)
    plane_done(3)
    plane_done(2)
    arrived(go_recv, g_at)
    part = own_ch // 2
    ga_send[0] = (g_one[...] + go_recv[...].astype(F32)).astype(BF16)
    first_at, second_at = new_recv(2), new_recv(2)
    upper, lower = pl.ds(0, part), pl.ds(part, part)
    push(ga_send.at[0, upper], ga_recv.at[0, upper], (xn, c), first_at)
    push(ga_send.at[0, lower], ga_recv.at[0, lower], (yn, c), first_at + 1)
    start_two(1)
    start_two(0)
    arrived(ga_recv.at[0, upper], first_at)
    arrived(ga_recv.at[0, lower], first_at + 1)
    ga_send[1] = (ga_send[0].astype(F32) + ga_recv[0].astype(F32)).astype(BF16)
    push(ga_send.at[1, upper], ga_recv.at[1, upper], (yn, c), second_at)
    push(ga_send.at[1, lower], ga_recv.at[1, lower], (xn, c), second_at + 1)

    edges = finish_edges()
    plane_done(1)
    sum_k = plane_done(0)

    arrived(ga_recv.at[1, upper], second_at)
    arrived(ga_recv.at[1, lower], second_at + 1)
    g_one[...] = ga_send[1].astype(F32) + ga_recv[1].astype(F32)

    row_at = chunk * (i * 4 + z)
    tap = lax.div(row_at, width)
    edge_rows[...] = edges
    for step in range(2):
        ranked[pl.ds(width * step, width), :] = rank_one(
            centre, edge_rows[pl.ds(lax.rem(tap + step, TAPS), 1)]
        )
    offset = pl.multiple_of(row_at - width * tap, 32)
    sum_k = sum_k + ranked[pl.ds(offset, chunk), :]
    sum_h = h_sum[z]
    for dz in (1, 2, 3):
        arrived(rk_z.at[chip(dz)], z_at + chip(dz))
        arrived(rh_z.at[chip(dz)], h_z + chip(dz))
        sum_k = sum_k + rk_z[chip(dz)].astype(F32)
        sum_h = sum_h + rh_z[chip(dz)].astype(F32)
    head_flat[...] = sum_h
    g_head[...] = jnp.zeros(g_head.shape, F32)
    for r in range(head_rows):
        first, shift = divmod(classes * r, 128)
        rows = jnp.concatenate(
            [head_flat[r : r + 1, 128 * j : 128 * j + 128] for j in range(8)], axis=0
        )
        if shift:
            rows = pltpu.roll(rows, shift, 1)
        count = min(8, g_head.shape[0] - first)
        g_head[first : first + count, :] += jnp.where(lane >= shift, rows, 0.0)[:count]
        count = min(8, g_head.shape[0] - first - 1)
        if shift:
            g_head[first + 1 : first + 1 + count, :] += jnp.where(lane < shift, rows, 0.0)[:count]
    last_send[...] = sum_k
    l_at = new_recv()
    theirs = last_send.at[pl.ds(pl.multiple_of(block * (1 - k), 16), block)]
    push(theirs, last_recv, (i, sib), l_at)
    mine = last_send[pl.ds(pl.multiple_of(block * k, 16), block), :]
    arrived(last_recv, l_at)
    other = last_recv[...]
    for j in range(4):
        lanes = slice(128 * (j % 2), 128 * (j % 2) + 128)
        g_two[pl.ds(j, block, stride=4), :] = jnp.where(
            k == j // 2, mine[:, lanes], other[:, lanes]
        )

    arrived(wide_sib.at[1], bn_at)
    own_bn, other_bn = wide_sib[0], wide_sib[1]
    g_bn_two[...] = jnp.where(
        k == 0,
        jnp.concatenate([own_bn[0:2], other_bn[0:2]], axis=1),
        jnp.concatenate([other_bn[0:2], own_bn[0:2]], axis=1),
    )
    for copy in sent:
        copy.wait_send()


def update_kernel(rates, *refs):
    take, give = refs[:24], refs[24:]
    rate_one, rate_bn_one, rate_two, rate_bn_two, rate_head = rates
    w, g, m, v, mask, rank = (r[...] for r in take[:6])
    results = sparse_update(w, g * mask.astype(F32), m, v, mask, rank, rate_one)
    for ref, value in zip(give[:5], results):
        ref[...] = value
    w, g, m, v, mask, rank = (r[...] for r in take[6:12])
    results = sparse_update(w, g * mask.astype(F32), m, v, mask, rank, rate_two)
    for ref, value in zip(give[5:10], results):
        ref[...] = value

    @pl.when(pl.program_id(0) == 0)
    def _():
        for n, rate in enumerate((rate_bn_one, rate_bn_two, rate_head)):
            w, g, m, v = (r[...] for r in take[12 + 4 * n : 16 + 4 * n])
            results = dense_update(w, g, m, v, rate)
            for ref, value in zip(give[10 + 3 * n : 13 + 3 * n], results):
                ref[...] = value
        give[19][...] = results[0].astype(BF16)


def fast_shards(
    images_in, labels, loss_wt, placement,
    w_one, mom_one, avg_one, mask_one, rank_one_in, first_norm_params, mom_bn_one, avg_bn_one,
    w_two, mom_two, avg_two, mask_two, rank_two, second_norm_params, mom_bn_two, avg_bn_two,
    w_head, mom_head, avg_head,
):
    n_img, n_ch = lax.axis_size("img"), lax.axis_size("ch")
    group, cin = images_in.shape[0], images_in.shape[2]
    per_core = labels.shape[0]
    per_chip = 2 * per_core
    width = second_norm_params.shape[1]
    half = width // 2
    own_ch = w_one.shape[1]
    chip_ch = 2 * own_ch
    classes = w_head.shape[0] * n_img * n_ch // width
    images = per_core * n_img * n_ch
    head_rows = w_head.shape[0] // classes
    lanes = -(-classes // 512) * 512
    block = w_two.shape[0] // width
    chunk = 2 * block
    flat = (w_two.shape[0] // 128, 128)
    top = [a.reshape(-1, 128) for a in (w_head, mom_head, avg_head)]
    one = [a.T for a in (w_one, mom_one, avg_one, mask_one, rank_one_in)]
    two = [a.reshape(flat) for a in (w_two, mom_two, avg_two, mask_two, rank_two)]
    vmem = pl.BlockSpec(memory_space=pltpu.VMEM)
    smem = pl.BlockSpec(memory_space=pltpu.SMEM)
    hbm = pl.BlockSpec(memory_space=pl.ANY)
    v = pltpu.VMEM
    shape = jax.ShapeDtypeStruct
    g_one, g_two, g_head, g_bn_one, g_bn_two, loss = pl.pallas_call(
        functools.partial(step_kernel, (group, per_chip, classes, images)),
        out_shape=(
            shape((own_ch, cin), F32),
            shape(flat, F32),
            shape(top[0].shape, F32),
            shape((2, own_ch), F32),
            shape((2, width), F32),
            shape((1, 128), F32),
        ),
        in_specs=[hbm, vmem, smem, smem, vmem, vmem, vmem, vmem, vmem, vmem, vmem],
        out_specs=[vmem] * 6,
        scratch_shapes=[
            v((UPPER * SIDE, group, cin), BF16),
            v((chip_ch, cin), BF16),
            v((TAPS * width, half), BF16),
            v((4, 4, 2, head_rows, lanes), BF16),
            v((SIDE + 3, PITCH, per_chip, width), BF16),
            v((UPPER, SIDE, group, chip_ch), BF16),
            v((UPPER * SIDE * group, chip_ch), F32),
            v((SIDE, PITCH, per_chip, half), F32),
            v((SIDE, PITCH, per_chip, half), F32),
            v((2 * FRONT + SIDE * PITCH, per_chip, half), BF16),
            v((width + 16, SIDE * PITCH * per_chip), BF16),
            v((SIDE, PITCH, per_chip, width), F32),
            v((UPPER, SIDE, per_chip, width), BF16),
            v((UPPER, SIDE, per_chip, width), BF16),
            v((UPPER, SIDE, group, chip_ch), BF16),
            v((2, 8, 128), F32),
            v((4, 8, 128), F32),
            v((2, 8, 8, 128), F32),
            v((3, 16, 16, half), F32),
            v((2, 8, half), F32),
            v((2, per_chip, lanes), F32),
            v((2, 4, 2, head_rows, lanes), BF16),
            v((TAPS * width, half), BF16),
            v((4, 4, head_rows, lanes), BF16),
            v((4, 2, chunk, half), BF16),
            v((2, 2, 2, head_rows, lanes), BF16),
            v((4, chunk, half), BF16),
            v((2, 2, head_rows, lanes), BF16),
            v((4, chunk, half), BF16),
            v((4, head_rows, lanes), BF16),
            v((4, head_rows, lanes), F32),
            v((head_rows, lanes), F32),
            v((chunk, half), F32),
            v((block, half), F32),
            v((16, half), F32),
            v((2 * width, half), F32),
            v((chip_ch, UPPER * SIDE * group), BF16),
            v((chip_ch, cin), F32),
            v((own_ch, cin), BF16),
            v((own_ch, cin), BF16),
            v((2, own_ch, cin), BF16),
            v((2, own_ch, cin), BF16),
            pltpu.SemaphoreType.DMA((UPPER,)),
            pltpu.SemaphoreType.DMA((UPPER + 1,)),
            pltpu.SemaphoreType.DMA((SEMS,)),
            pltpu.SemaphoreType.DMA((SEMS,)),
        ],
        compiler_params=pltpu.CompilerParams(
            collective_id=0, has_side_effects=True, vmem_limit_bytes=56 << 20
        ),
        name="step",
    )(
        images_in.transpose(1, 0, 2),
        placement,
        labels,
        loss_wt,
        one[0],
        one[3],
        first_norm_params,
        two[0],
        two[3],
        top[0],
        second_norm_params,
    )
    root = math.sqrt(images)
    steps = 4
    one_spec = pl.BlockSpec((own_ch // steps, cin), lambda n: (n, 0))
    two_spec = pl.BlockSpec((flat[0] // steps, 128), lambda n: (n, 0))
    bno_spec = pl.BlockSpec((2, own_ch), lambda n: (0, 0))
    bnt_spec = pl.BlockSpec((2, width), lambda n: (0, 0))
    top_spec = pl.BlockSpec(top[0].shape, lambda n: (0, 0))
    f_one, f_two = shape(one[0].shape, F32), shape(flat, F32)
    new = pl.pallas_call(
        functools.partial(update_kernel, (1.3 * root, 8.0 * root, 0.25 * root, root, 40.0)),
        grid=(steps,),
        in_specs=[one_spec] * 6 + [two_spec] * 6 + [bno_spec] * 4 + [bnt_spec] * 4 + [top_spec] * 4,
        out_specs=[one_spec] * 5 + [two_spec] * 5 + [bno_spec] * 3 + [bnt_spec] * 3 + [top_spec] * 4,
        out_shape=[f_one] * 3 + [shape(f_one.shape, jnp.int32), shape(f_one.shape, BF16)]
        + [f_two] * 3 + [shape(flat, jnp.int32), shape(flat, BF16)]
        + [shape((2, own_ch), F32)] * 3 + [shape((2, width), F32)] * 3
        + [shape(top[0].shape, F32)] * 3 + [shape(top[0].shape, BF16)],
        compiler_params=pltpu.CompilerParams(vmem_limit_bytes=56 << 20),
        name="update",
    )(
        one[0], g_one, one[1], one[2], one[3], one[4],
        two[0], g_two, two[1], two[2], two[3], two[4],
        first_norm_params, g_bn_one, mom_bn_one, avg_bn_one,
        second_norm_params, g_bn_two, mom_bn_two, avg_bn_two,
        top[0], g_head, top[1], top[2],
    )
    return (
        loss[0, 0],
        *(a.T for a in new[:5]),
        *new[10:13],
        *(a.reshape(-1) for a in new[5:10]),
        *new[13:16],
        *(a.reshape(-1) for a in new[16:20]),
    )


def solution(mesh):
    in_specs = (
        P("img", None, None),
        P(("img", "ch")),
        P(("img", "ch")),
        P("img", None),
        P(None, "ch"),
        P(None, "ch"),
        P(None, "ch"),
        P(None, "ch"),
        P(None, "ch"),
        P(None, "ch"),
        P(None, "ch"),
        P(None, "ch"),
        P(("img", "ch")),
        P(("img", "ch")),
        P(("img", "ch")),
        P(("img", "ch")),
        P(("img", "ch")),
        P(),
        P(),
        P(),
        P(("img", "ch")),
        P(("img", "ch")),
        P(("img", "ch")),
    )
    out_specs = (
        P(),
        P(None, "ch"),
        P(None, "ch"),
        P(None, "ch"),
        P(None, "ch"),
        P(None, "ch"),
        P(None, "ch"),
        P(None, "ch"),
        P(None, "ch"),
        P(("img", "ch")),
        P(("img", "ch")),
        P(("img", "ch")),
        P(("img", "ch")),
        P(("img", "ch")),
        P(),
        P(),
        P(),
        P(("img", "ch")),
        P(("img", "ch")),
        P(("img", "ch")),
        P(("img", "ch")),
    )
    fast = mesh.shape["img"] == 4 and mesh.shape["ch"] == 8
    return jax.shard_map(fast_shards if fast else shards, mesh=mesh, in_specs=in_specs, out_specs=out_specs, check_vma=False)
```

```python
import functools
import itertools
import math

import jax
import jax.numpy as jnp
from jax import lax
from jax.experimental import pallas as pl
from jax.experimental.pallas import tpu as pltpu
from jax.sharding import PartitionSpec as P

SIDE = 7
PIX = 49
DROP = 10
GROW = 10


EPS = 1e-05
MOMENTUM = 0.5


def advance(weight, grad, velocity, rate):
    velocity = MOMENTUM * velocity + grad
    return (weight - rate * (grad + MOMENTUM * velocity), velocity)


def dense_update(weight, grad, velocity, average, rate):
    moved, velocity = advance(weight, grad, velocity, rate)
    return (moved, velocity, 0.5 * average + 0.5 * moved)


def sparse_update(weight, grad, velocity, average, mask, rank, rate):
    moved, velocity = advance(weight, grad, velocity, rate)
    kept = (mask == 1) & (rank >= DROP)
    grown = (mask == 0) & (rank < GROW)
    new_mask = jnp.where(kept | grown, 1, 0).astype(jnp.int32)
    weight = jnp.where(kept, moved, 0.0)
    velocity = jnp.where(kept, velocity, 0.0)
    average = 0.5 * average + 0.5 * weight
    return (weight, velocity, average, new_mask, weight.astype(jnp.bfloat16))


def silu_slope(value):
    sigma = jax.nn.sigmoid(value)
    return sigma * (1.0 + value * (1.0 - sigma))


def apply_batch_norm(z, sums, squares, element_count):
    mean = sums / element_count
    inverse_deviation = lax.rsqrt(squares / element_count - mean * mean + EPS)
    return ((z - mean) * inverse_deviation, inverse_deviation)


def batch_norm_backward(
    norm_gain,
    inverse_deviation,
    output_gradient,
    standardized_input,
    bias_gradient_sum,
    gain_gradient_sum,
    element_count,
):
    return (
        norm_gain
        * inverse_deviation
        * (
            output_gradient
            - bias_gradient_sum / element_count
            - standardized_input * gain_gradient_sum / element_count
        )
    )


def contract_rows(left, right):
    return jnp.einsum("pk,pc->kc", left, right, preferred_element_type=jnp.float32)


def shards(
    images_in,
    labels,
    loss_wt,
    placement,
    w_one,
    mom_one,
    avg_one,
    mask_one,
    rank_one,
    first_norm_params,
    mom_bn_one,
    avg_bn_one,
    w_two,
    mom_two,
    avg_two,
    mask_two,
    rank_two,
    second_norm_params,
    mom_bn_two,
    avg_bn_two,
    w_head,
    mom_head,
    avg_head,
):
    n_img = lax.axis_size("img")
    n_ch = lax.axis_size("ch")
    group = images_in.shape[0]
    element_count = labels.shape[0]
    width = second_norm_params.shape[1]
    classes = w_head.shape[0] * n_img * n_ch // width
    images = element_count * n_img * n_ch
    slot_info = jnp.stack([labels.astype(jnp.float32), loss_wt.astype(jnp.float32)])
    slot_info = lax.all_gather(slot_info, "ch", axis=1, tiled=True)
    own = lax.axis_index("ch") * element_count + jnp.arange(element_count, dtype=jnp.int32)
    fills = placement[0][None, :] == own[:, None]
    labels_f, weights = jnp.sum(jnp.where(fills[None], slot_info[:, None, :], 0.0), axis=2)
    labels = labels_f.astype(jnp.int32)
    kernel_part = (w_two * mask_two.astype(jnp.float32)).astype(jnp.bfloat16)
    kernel = lax.all_gather(kernel_part, ("img", "ch"), axis=0, tiled=True)
    head = lax.all_gather(w_head.astype(jnp.bfloat16), ("img", "ch"), axis=0, tiled=True)
    kernel = kernel.reshape(9 * width, width)
    head = head.reshape(width, classes)
    rows = images_in.transpose(1, 0, 2).reshape(PIX * group, images_in.shape[2])
    filt_one = (w_one * mask_one.astype(jnp.float32)).astype(jnp.bfloat16)
    first_conv_output = jnp.dot(rows, filt_one, preferred_element_type=jnp.float32)
    first_feature_sum, first_squares_sum, total = lax.psum(
        (
            jnp.sum(first_conv_output, axis=0),
            jnp.sum(first_conv_output * first_conv_output, axis=0),
            jnp.sum(slot_info[1]),
        ),
        "img",
    )
    first_element_count = group * PIX * n_img
    first_standardized_input, first_inverse_deviation = apply_batch_norm(
        first_conv_output, first_feature_sum, first_squares_sum, first_element_count
    )
    first_norm_output = first_norm_params[0] * first_standardized_input + first_norm_params[1]
    act = jax.nn.silu(first_norm_output).astype(jnp.bfloat16).reshape(PIX, group, -1)
    act_in = lax.all_to_all(act, "ch", split_axis=1, concat_axis=2, tiled=True)
    padded = jnp.pad(
        act_in.reshape(SIDE, SIDE, element_count, width), ((1, 1), (1, 1), (0, 0), (0, 0))
    )
    patches = jnp.concatenate(
        [
            padded[tap // 3 : tap // 3 + SIDE, tap % 3 : tap % 3 + SIDE].reshape(
                PIX * element_count, width
            )
            for tap in range(9)
        ],
        axis=1,
    )
    second_conv_output = jnp.dot(patches, kernel, preferred_element_type=jnp.float32)
    second_feature_sum, second_squares_sum = lax.psum(
        (
            jnp.sum(second_conv_output, axis=0),
            jnp.sum(second_conv_output * second_conv_output, axis=0),
        ),
        ("img", "ch"),
    )
    second_element_count = images * PIX
    second_standardized_input, second_inverse_deviation = apply_batch_norm(
        second_conv_output, second_feature_sum, second_squares_sum, second_element_count
    )
    second_norm_output = second_norm_params[0] * second_standardized_input + second_norm_params[1]
    pooled = jnp.mean(jax.nn.silu(second_norm_output).reshape(PIX, element_count, width), axis=0)
    pooled_low = pooled.astype(jnp.bfloat16)
    logits = jnp.dot(pooled_low, head, preferred_element_type=jnp.float32)
    top = jnp.max(logits, axis=1, keepdims=True)
    expd = jnp.exp(logits - top)
    denom = jnp.sum(expd, axis=1, keepdims=True)
    lse = top[:, 0] + jnp.log(denom[:, 0])
    onehot = labels[:, None] == jnp.arange(classes, dtype=jnp.int32)[None, :]
    picked = jnp.sum(jnp.where(onehot, logits, 0.0), axis=1)
    share = weights / total
    partial_loss_value = jnp.sum(share * (lse - picked))
    d_logits = (share[:, None] * (expd / denom - onehot.astype(jnp.float32))).astype(jnp.bfloat16)
    g_head = contract_rows(pooled_low, d_logits)
    d_pooled = jnp.einsum("ic,kc->ik", d_logits, head, preferred_element_type=jnp.float32)
    d_act = jnp.broadcast_to(d_pooled[None] / PIX, (PIX, element_count, width)).reshape(
        PIX * element_count, width
    )
    second_output_gradient = d_act * silu_slope(second_norm_output)
    second_shift_bias, second_norm_gain, loss = lax.psum(
        (
            jnp.sum(second_output_gradient, axis=0),
            jnp.sum(second_output_gradient * second_standardized_input, axis=0),
            partial_loss_value,
        ),
        ("img", "ch"),
    )
    second_preact_gradient = batch_norm_backward(
        second_norm_params[0],
        second_inverse_deviation,
        second_output_gradient,
        second_standardized_input,
        second_shift_bias,
        second_norm_gain,
        second_element_count,
    ).astype(jnp.bfloat16)
    d_patches = jnp.einsum(
        "pc,kc->pk", second_preact_gradient, kernel, preferred_element_type=jnp.float32
    )
    d_pad = 0.0
    for tap in range(9):
        piece = d_patches[:, tap * width : (tap + 1) * width].reshape(
            SIDE, SIDE, element_count, width
        )
        up, left = tap // 3, tap % 3
        d_pad = d_pad + jnp.pad(piece, ((up, 2 - up), (left, 2 - left), (0, 0), (0, 0)))
    d_act_in = d_pad[1:-1, 1:-1].astype(jnp.bfloat16).reshape(PIX, element_count, width)
    d_act_one = lax.all_to_all(d_act_in, "ch", split_axis=2, concat_axis=1, tiled=True)
    g_kernel = contract_rows(patches, second_preact_gradient)
    d_act_one = d_act_one.reshape(PIX * group, -1).astype(jnp.float32)
    first_output_gradient = d_act_one * silu_slope(first_norm_output)
    first_shift_bias, first_norm_gain = lax.psum(
        (
            jnp.sum(first_output_gradient, axis=0),
            jnp.sum(first_output_gradient * first_standardized_input, axis=0),
        ),
        "img",
    )
    first_preact_gradient = batch_norm_backward(
        first_norm_params[0],
        first_inverse_deviation,
        first_output_gradient,
        first_standardized_input,
        first_shift_bias,
        first_norm_gain,
        first_element_count,
    ).astype(jnp.bfloat16)
    g_filt = lax.psum(
        contract_rows(rows, first_preact_gradient).astype(jnp.bfloat16), "img"
    ).astype(jnp.float32)
    g_one = g_filt * mask_one.astype(jnp.float32)
    part_two = lax.psum_scatter(
        g_kernel.reshape(-1), ("img", "ch"), tiled=True
    )
    part_head = lax.psum_scatter(
        g_head.reshape(-1), ("img", "ch"), tiled=True
    )
    g_two = part_two * mask_two.astype(jnp.float32)
    root = math.sqrt(images)
    one = sparse_update(w_one, g_one, mom_one, avg_one, mask_one, rank_one, 1.3 * root)
    bno = dense_update(
        first_norm_params,
        jnp.stack([first_norm_gain, first_shift_bias]),
        mom_bn_one,
        avg_bn_one,
        8.0 * root,
    )
    two = sparse_update(w_two, g_two, mom_two, avg_two, mask_two, rank_two, 0.25 * root)
    bnt = dense_update(
        second_norm_params,
        jnp.stack([second_norm_gain, second_shift_bias]),
        mom_bn_two,
        avg_bn_two,
        root,
    )
    top_head = dense_update(w_head, part_head, mom_head, avg_head, 40.0)
    return (
        loss,
        one[0],
        one[1],
        one[2],
        one[3],
        one[4],
        bno[0],
        bno[1],
        bno[2],
        two[0],
        two[1],
        two[2],
        two[3],
        two[4],
        bnt[0],
        bnt[1],
        bnt[2],
        top_head[0],
        top_head[1],
        top_head[2],
        top_head[0].astype(jnp.bfloat16),
    )


F32, BF16 = jnp.float32, jnp.bfloat16
MESH = pl.DeviceIdType.MESH
TAPS = 9
UPPER = (SIDE + 1) // 2
PITCH = SIDE + 1
FRONT = 2 * PITCH
SEMS = 92


def silu_pair(value):
    sigma = 1.0 / (1.0 + jnp.exp(-value))
    return value * sigma, sigma * (1.0 + value * (1.0 - sigma))


def matmul_nt(left, right):
    return lax.dot_general(left, right, (((1,), (1,)), ((), ())), preferred_element_type=F32)


def matmul_tn(left, right):
    return lax.dot_general(left, right, (((0,), (0,)), ((), ())), preferred_element_type=F32)


def rank_one(row, other):
    first = other.astype(BF16)
    rest = other - first.astype(F32)
    second = rest.astype(BF16)
    third = (rest - second.astype(F32)).astype(BF16)
    place = lax.broadcasted_iota(jnp.int32, (16, other.shape[1]), 0)
    parts = jnp.where(place == 0, first.astype(F32), 0.0)
    parts = jnp.where(place == 1, second.astype(F32), parts)
    parts = jnp.where(place == 2, third.astype(F32), parts)
    rows = jnp.broadcast_to(row, (16, row.shape[1])).astype(BF16)
    return matmul_tn(rows, parts.astype(BF16))


def step_kernel(
    sizes,
    images,
    place_in,
    labels_in,
    loss_wt_in,
    w_one_in,
    mask_one_in,
    norm_one_in,
    w_two_in,
    mask_two_in,
    w_head_in,
    norm_two_in,
    g_one,
    g_two,
    g_head,
    g_bn_one,
    g_bn_two,
    loss,
    w_one,
    mask_one,
    w_two,
    mask_two,
    w_head,
    norm_one,
    norm_two,
    place,
    labels,
    loss_wt,
    feats,
    filt,
    kern,
    head,
    act_in,
    act_out,
    z_one,
    z_two,
    slope,
    d_pad,
    act_t,
    d_act,
    d_send,
    d_recv,
    d_one,
    early,
    info,
    tiles,
    wide,
    wide_sib,
    logit,
    gh_half,
    gk,
    gh,
    rk_one,
    rh_one,
    rk_two,
    rh_two,
    rk_z,
    rh_z,
    h_sum,
    head_flat,
    last_send,
    last_recv,
    edge_rows,
    ranked,
    grad_t,
    g_acc,
    go_send,
    go_recv,
    ga_send,
    ga_recv,
    load_sem,
    image_sem,
    local_sem,
    send,
    recv,
):
    group, per_chip, classes, images_in_all = sizes
    width = norm_two.shape[1]
    half = width // 2
    own_ch = w_one.shape[0]
    chip_ch = 2 * own_ch
    block = w_two.shape[0] * 128 // width
    chunk = 2 * block
    head_rows = head.shape[3]
    rows_a = SIDE * group
    rows_c = PITCH * per_chip
    count_all = float(images_in_all * PIX)

    i, c = lax.axis_index("img"), lax.axis_index("ch")
    z, k = lax.div(c, 2), lax.rem(c, 2)
    sib = c + 1 - 2 * k
    xn, yn, dg = i + 1 - 2 * lax.rem(i, 2), lax.rem(i + 2, 4), 3 - i
    lines = (xn, yn, dg)
    near = (z, z + 1 - 2 * lax.rem(z, 2), 2 - lax.div(z, 2), 3 - 3 * lax.div(z, 2))
    h0 = (SIDE - UPPER) * k

    def chip(dz):
        return near[dz]

    def zdev(dz):
        return 2 * chip(dz) + k

    next_send, next_recv = itertools.count(), itertools.count()
    sent = []

    def new_recv(n=1):
        first = next(next_recv)
        for _ in range(n - 1):
            next(next_recv)
        return first

    def push(src, dst, device, to):
        copy = pltpu.make_async_remote_copy(
            src_ref=src,
            dst_ref=dst,
            send_sem=send.at[next(next_send)],
            recv_sem=recv.at[to],
            device_id=device,
            device_id_type=MESH,
        )
        copy.start()
        sent.append(copy)
        return copy

    def push_all(copies, size_of, to):
        at = next(next_send)
        for src, dst, device in copies:
            pltpu.make_async_remote_copy(
                src_ref=src,
                dst_ref=dst,
                send_sem=send.at[at],
                recv_sem=recv.at[to],
                device_id=device,
                device_id_type=MESH,
            ).start()
        group_copy = pltpu.make_async_remote_copy(
            src_ref=size_of,
            dst_ref=size_of,
            send_sem=send.at[at],
            recv_sem=recv.at[to],
            device_id=(i, sib),
            device_id_type=MESH,
        )
        sent.append(group_copy)
        return group_copy

    def arrived(dst, at):
        pltpu.make_async_remote_copy(
            src_ref=dst,
            dst_ref=dst,
            send_sem=send.at[0],
            recv_sem=recv.at[at],
            device_id=(i, sib),
            device_id_type=MESH,
        ).wait_recv()

    def image_copy(r):
        return pltpu.make_async_copy(
            images.at[pl.ds(SIDE * (h0 + r), SIDE)], feats.at[pl.ds(SIDE * r, SIDE)], image_sem.at[r]
        )

    barrier = pltpu.get_barrier_semaphore()
    same_core = [(o, zdev(dz)) for o in (i, *lines) for dz in (0, 1, 2, 3)][1:]
    plane = [(i, sib)] + [(o, d) for o in lines for d in (c, sib)]
    others = plane + same_core[:3]
    for device in others:
        pl.semaphore_signal(barrier, inc=1, device_id=device, device_id_type=MESH)
    loads = [
        pltpu.make_async_copy(src, dst, load_sem.at[n])
        for n, (src, dst) in enumerate(
            (
                (w_two_in, w_two),
                (mask_two_in, mask_two),
                (w_one_in, w_one),
                (mask_one_in, mask_one),
                (norm_one_in, norm_one),
                (labels_in, labels),
                (loss_wt_in, loss_wt),
                (w_head_in, w_head),
                (norm_two_in, norm_two),
                (place_in, place),
            )
        )
    ]
    for copy in loads:
        copy.start()
    for r in range(UPPER):
        image_copy(r).start()

    loads[0].wait()
    loads[1].wait()
    chunk_at = pl.multiple_of(chunk * (i * 4 + z), 32)
    block_at = pl.multiple_of(chunk_at + block * k, 16)
    parts = [
        w_two[pl.ds(j, block, stride=4), :] * mask_two[pl.ds(j, block, stride=4), :].astype(F32)
        for j in range(4)
    ]
    low = jnp.concatenate(parts[:2], axis=1).astype(BF16)
    high = jnp.concatenate(parts[2:], axis=1).astype(BF16)
    kern[pl.ds(block_at, block), :] = jnp.where(k == 0, low.astype(F32), high.astype(F32)).astype(BF16)
    gk[pl.ds(0, block), :] = jnp.where(k == 0, high.astype(F32), low.astype(F32)).astype(BF16)
    for copy in loads[2:7]:
        copy.wait()
    own_at = pl.multiple_of(own_ch * k, 16)
    filt[pl.ds(own_at, own_ch), :] = (w_one[...] * mask_one[...].astype(F32)).astype(BF16)
    lane = lax.broadcasted_iota(jnp.int32, (1, 128), 1)
    norms = norm_one[...]
    nothing = jnp.zeros_like(norms)
    placed = jnp.where(
        k == 0, jnp.concatenate([norms, nothing], axis=1), jnp.concatenate([nothing, norms], axis=1)
    )
    label_row, weight_row = jnp.zeros((1, 128), F32), jnp.zeros((1, 128), F32)
    for j in range(labels.shape[0]):
        here = lane == labels.shape[0] * c + j
        label_row = jnp.where(here, labels[j].astype(F32), label_row)
        weight_row = jnp.where(here, loss_wt[j].astype(F32), weight_row)
    early[0] = jnp.concatenate(
        [placed, label_row, weight_row, jnp.zeros((4, 128), F32)], axis=0
    )

    pl.semaphore_wait(barrier, len(others))

    k_sib, f_sib, e_sib = new_recv(), new_recv(), new_recv()
    push(gk.at[pl.ds(0, block)], kern.at[pl.ds(block_at, block)], (i, sib), k_sib)
    push(filt.at[pl.ds(own_at, own_ch)], filt.at[pl.ds(own_at, own_ch)], (i, sib), f_sib)
    push(early.at[0], early.at[1], (i, sib), e_sib)

    k_recv = new_recv(32)

    def kern_at(line, dz, u):
        at = chunk * (line * 4 + chip(dz)) + block * (k if u == 0 else 1 - k)
        return kern.at[pl.ds(pl.multiple_of(at, 16), block)]

    def forward(line, dz, u, *devices):
        for device in devices:
            at = k_recv + 2 * (line * 4 + chip(dz)) + u
            push(kern_at(line, dz, u), kern_at(line, dz, u), device, at)

    def landed(line, dz, u):
        arrived(kern_at(line, dz, u), k_recv + 2 * (line * 4 + chip(dz)) + u)

    def relay(line, dz, u, *devices):
        landed(line, dz, u)
        forward(line, dz, u, *devices)

    to_x, to_y = (xn, c), (yn, c)
    to_z = [(i, zdev(dz)) for dz in (1, 2, 3)]
    forward(i, 0, 0, to_x, to_y, *to_z)
    act_in[0] = jnp.zeros(act_in.shape[1:], BF16)
    for r in range(SIDE + 1, act_in.shape[0]):
        act_in[r] = jnp.zeros(act_in.shape[1:], BF16)
    for r in range(1, SIDE + 1):
        act_in[r, 0] = jnp.zeros(act_in.shape[2:], BF16)
    other_block_at = pl.multiple_of(chunk_at + block * (1 - k), 16)
    arrived(kern.at[pl.ds(other_block_at, block)], k_sib)
    forward(i, 0, 1, to_x, to_y, *to_z)
    arrived(early.at[1], e_sib)
    both = early[0] + early[1]
    info[z] = both
    i_recv = new_recv()
    push_all([(info.at[z], info.at[z], device) for device in to_z], info.at[pl.ds(0, 3)], i_recv)
    other_at = pl.multiple_of(own_ch * (1 - k), 16)
    arrived(filt.at[pl.ds(other_at, own_ch)], f_sib)

    def first_conv(r, carry):
        sums, squares = carry
        image_copy(r).wait()
        rows = feats[pl.ds(SIDE * r, SIDE)].reshape(rows_a, feats.shape[2])
        out = matmul_nt(rows, filt[...])
        z_one[pl.ds(pl.multiple_of(rows_a * r, 64), rows_a), :] = out
        counted = jnp.where((r == 0) & (k == 1), 0.0, 1.0)
        return (
            sums + counted * jnp.sum(out, axis=0, keepdims=True),
            squares + counted * jnp.sum(out * out, axis=0, keepdims=True),
        )

    zero_row = jnp.zeros((1, chip_ch), F32)
    sums, squares = lax.fori_loop(0, UPPER, first_conv, (zero_row, zero_row))

    def small_sum(turn, rows):
        own = 2 * i + k
        tiles[turn, own] = rows
        at = new_recv()
        tile, all_others = tiles.at[turn, own], tiles.at[turn, pl.ds(0, 7)]
        push_all([(tile, tile, device) for device in plane], all_others, at)

        def finish():
            arrived(all_others, at)
            result = tiles[turn, 0]
            for n in range(1, 8):
                result = result + tiles[turn, n]
            return result

        return finish

    finish = small_sum(0, jnp.concatenate([sums, squares, jnp.zeros((6, 128), F32)], axis=0))
    for copy in loads[7:]:
        copy.wait()
    for r in range(head_rows):
        first, shift = divmod(classes * r, 128)
        taken = -(-(shift + classes) // 128)
        rows = w_head[first : first + taken, :]
        if taken < 9:
            rows = jnp.concatenate([rows, jnp.zeros((9 - taken, 128), F32)], axis=0)
        if shift:
            rows = pltpu.roll(rows, 128 - shift, 1)
            rows = jnp.where(lane < 128 - shift, rows[:8], rows[1:9])
        for j in range(8):
            head_flat[r : r + 1, 128 * j : 128 * j + 128] = rows[j : j + 1]
    head_lane = lax.broadcasted_iota(jnp.int32, (head_rows, 1024), 1)
    head[i, z, k] = jnp.where(head_lane < classes, head_flat[...], 0.0).astype(BF16)
    relay(i, 1, 0, to_x, to_y)
    relay(xn, 0, 0, to_y)
    relay(xn, 0, 1, to_y)
    totals = finish()
    mean_one = totals[0:1] / count_all
    inv_one = lax.rsqrt(totals[1:2] / count_all - mean_one * mean_one + EPS)
    gain_one, bias_one = both[0:1], both[1:2]

    def first_act(r):
        at = slice(rows_a * r, rows_a * r + rows_a)
        hat = (z_one[at, :] - mean_one) * inv_one
        value, grade = silu_pair(gain_one * hat + bias_one)
        act_out[r] = value.astype(BF16).reshape(SIDE, group, chip_ch)

    def into(row, chip_id):
        return act_in.at[
            1 + row, pl.ds(1, SIDE), :, pl.ds(pl.multiple_of(chip_ch * chip_id, 128), chip_ch)
        ]

    def images_of(ref, dz):
        return ref.at[:, :, pl.ds(pl.multiple_of(per_chip * chip(dz), 16), per_chip), :]

    def images_in_row(ref, r, dz):
        return ref.at[r, :, pl.ds(pl.multiple_of(per_chip * chip(dz), 16), per_chip), :]

    def row_copies(r):
        return [
            (images_in_row(act_out, r + k, dz), into(UPPER * k + r, z), to_z[dz - 1])
            for dz in (3, 2, 1)
        ]

    def keep_row(r, n):
        return pltpu.make_async_copy(
            images_in_row(act_out, r, 0), into(h0 + r, z), local_sem.at[n]
        )

    relay(i, 2, 0, to_x, to_y)
    relay(xn, 1, 0, to_y)
    relay(i, 3, 0, to_x, to_y)
    relay(i, 1, 1, to_x, to_y)
    for r in range(UPPER):
        first_act(r)
    a_recv, a_more = new_recv(), new_recv()
    common = SIDE - UPPER
    out_copies = [
        push_all(
            [copy for r in range(common) for copy in row_copies(r)],
            act_out.at[pl.ds(0, 3), :, pl.ds(0, 3 * per_chip)],
            a_recv,
        )
    ]
    more_send = next(next_send)

    def more_copy(dz):
        return pltpu.make_async_remote_copy(
            src_ref=images_in_row(act_out, common, dz),
            dst_ref=into(common, z),
            send_sem=send.at[more_send],
            recv_sem=recv.at[a_more],
            device_id=to_z[dz - 1],
            device_id_type=MESH,
        )

    more_size = act_out.at[0, :, pl.ds(0, 3 * per_chip)]
    more_wait = pltpu.make_async_remote_copy(
        src_ref=more_size,
        dst_ref=more_size,
        send_sem=send.at[more_send],
        recv_sem=recv.at[a_more],
        device_id=(i, sib),
        device_id_type=MESH,
    )

    @pl.when(k == 0)
    def _():
        for dz in (3, 2, 1):
            more_copy(dz).start()
        keep_row(common, common).start()

    kept = [keep_row(r + k, r) for r in range(common)]
    for copy in kept:
        copy.start()
    relay(yn, 2, 0, to_x)
    relay(i, 2, 1, to_x, to_y)
    relay(xn, 1, 1, to_y)
    relay(yn, 3, 0, to_x)
    relay(i, 3, 1, to_x, to_y)
    relay(yn, 2, 1, to_x)
    relay(yn, 3, 1, to_x)
    hz_recv = new_recv()
    own_head, line_head = head.at[i, z, k], head.at[i, :, k]
    push_all([(own_head, own_head, device) for device in to_z], head.at[i, pl.ds(0, 3), k], hz_recv)

    for copy in kept:
        copy.wait()
    arrived(act_out.at[pl.ds(0, 3), :, pl.ds(0, 3 * per_chip)], a_recv)
    a_sib, m_sib = new_recv(), new_recv()
    mine = act_in.at[pl.ds(1 + UPPER * k, common), pl.ds(1, SIDE)]
    push(mine, mine, (i, sib), a_sib)
    m_send = next(next_send)
    middle = pltpu.make_async_remote_copy(
        src_ref=act_in.at[1 + common, pl.ds(1, SIDE)],
        dst_ref=act_in.at[1 + common, pl.ds(1, SIDE)],
        send_sem=send.at[m_send],
        recv_sem=recv.at[m_sib],
        device_id=(i, sib),
        device_id_type=MESH,
    )

    @pl.when(k == 0)
    def _():
        keep_row(common, common).wait()
        more_wait.wait_recv()
        middle.start()

    for line, dz in ((yn, 0), (yn, 1), (xn, 2), (xn, 3), (dg, 0), (dg, 1), (dg, 2), (dg, 3)):
        landed(line, dz, 0)
        landed(line, dz, 1)
    arrived(act_in.at[pl.ds(1 + UPPER * (1 - k), common), pl.ds(1, SIDE)], a_sib)

    @pl.when(k == 1)
    def _():
        middle.wait_recv()

    @pl.when(k == 0)
    def _():
        middle.wait_send()
        more_wait.wait_send()

    def tap_of(t):
        return t // 3, t % 3

    def second_conv(h, carry):
        sums, squares, act_sums = carry
        inner = act_in[h + 1].reshape(rows_c, width).astype(F32)
        out = jnp.zeros((rows_c, half), F32)
        for t in range(TAPS):
            up, left = tap_of(t)
            wide = act_in[pl.ds(h + up, 2)].reshape(2 * PITCH, per_chip, width)
            rows = wide[left : left + PITCH].reshape(rows_c, width)
            out = out + jnp.dot(
                rows, kern[pl.ds(width * t, width), :], preferred_element_type=F32
            )
        z_two[h] = out.reshape(PITCH, per_chip, half)
        real = out[: SIDE * per_chip]
        return (
            sums + jnp.sum(real, axis=0, keepdims=True),
            squares + jnp.sum(real * real, axis=0, keepdims=True),
            act_sums + jnp.sum(inner, axis=0, keepdims=True),
        )

    zero_half = jnp.zeros((1, half), F32)
    sums, squares, act_sums = lax.fori_loop(
        0, SIDE, second_conv, (zero_half, zero_half, jnp.zeros((1, width), F32))
    )

    def wide_sum(turn, rows):
        own, size = 4 * i + z, rows.shape[0]
        wide[turn, own, pl.ds(0, size)] = rows
        at = new_recv()
        tile = wide.at[turn, own, pl.ds(0, size)]
        all_others = wide.at[turn, pl.ds(0, 15), pl.ds(0, size)]
        push_all([(tile, tile, device) for device in same_core[::-1]], all_others, at)

        def finish():
            arrived(all_others, at)
            result = wide[turn, 0, pl.ds(0, size)]
            for n in range(1, 16):
                result = result + wide[turn, n, pl.ds(0, size)]
            return result

        return finish

    chip_weight = jnp.sum(both[3:4], axis=1, keepdims=True)
    finish = wide_sum(
        0,
        jnp.concatenate(
            [
                sums,
                squares,
                act_sums[:, :half],
                act_sums[:, half:],
                jnp.broadcast_to(chip_weight, (1, half)),
                jnp.zeros((3, half), F32),
            ],
            axis=0,
        ),
    )
    hx_recv, hy_recv, hxy_recv, hyx_recv = new_recv(), new_recv(), new_recv(), new_recv()
    arrived(head.at[i, pl.ds(0, 3), k], hz_recv)
    push(line_head, line_head, to_x, hx_recv)
    push(line_head, line_head, to_y, hy_recv)
    column = lax.broadcasted_iota(jnp.int32, (16, SIDE * rows_c), 1)
    is_real = lax.rem(lax.div(column, per_chip), PITCH) < SIDE
    act_t[pl.ds(width, 16), :] = jnp.where(is_real, 1.0, 0.0).astype(BF16)
    d_pad[pl.ds(0, FRONT)] = jnp.zeros((FRONT, per_chip, half), BF16)
    d_pad[pl.ds(FRONT + SIDE * PITCH, FRONT)] = jnp.zeros((FRONT, per_chip, half), BF16)
    arrived(head.at[xn, :, k], hx_recv)
    half_head = head.at[xn, pl.ds(0, 2), k]
    push(half_head, half_head, to_y, hxy_recv)
    arrived(head.at[yn, :, k], hy_recv)
    half_head = head.at[yn, pl.ds(2, 2), k]
    push(half_head, half_head, to_x, hyx_recv)
    totals_two = finish()
    total = totals_two[4:5, 0:1]
    mean_two = totals_two[0:1] / count_all
    inv_two = lax.rsqrt(totals_two[1:2] / count_all - mean_two * mean_two + EPS)
    centre = jnp.concatenate([totals_two[2:3], totals_two[3:4]], axis=1) / count_all
    centre = centre.astype(BF16).astype(F32)
    norms_two = jnp.where(k == 0, norm_two[:, :half], norm_two[:, half:])
    gain_two, bias_two = norms_two[0:1], norms_two[1:2]

    def second_act(h, pooled):
        hat = (z_two[h] - mean_two) * inv_two
        z_two[h] = hat
        value, grade = silu_pair(gain_two * hat + bias_two)
        slope[h] = grade
        return pooled + jnp.sum(value[:SIDE], axis=0)

    pooled = lax.fori_loop(0, SIDE, second_act, jnp.zeros((per_chip, half), F32)) / PIX
    pooled_low = pooled.astype(BF16)

    arrived(head.at[dg, pl.ds(0, 2), k], hxy_recv)
    arrived(head.at[dg, pl.ds(2, 2), k], hyx_recv)
    hd_sib = new_recv()
    theirs = head.at[pl.ds(2 * (1 - k), 2), :, k]
    push(theirs, theirs, (i, sib), hd_sib)
    arrived(info.at[pl.ds(0, 3)], i_recv)
    slots = info[0] + info[1] + info[2] + info[3]
    arrived(head.at[pl.ds(2 * k, 2), :, 1 - k], hd_sib)
    head_half = head[pl.ds(2 * k, 2)].reshape(half, head.shape[4])
    logit[0] = jnp.dot(pooled_low, head_half, preferred_element_type=F32)
    at = new_recv()
    push(logit.at[0], logit.at[1], (i, sib), at)
    image_id = per_chip * z + lax.broadcasted_iota(jnp.int32, (per_chip, group), 0)
    fills = place[...] == image_id
    label = jnp.sum(jnp.where(fills, slots[2:3, :group], 0.0), axis=1, keepdims=True).astype(jnp.int32)
    weight = jnp.sum(jnp.where(fills, slots[3:4, :group], 0.0), axis=1, keepdims=True)
    share = weight / total
    arrived(logit.at[1], at)
    logits = logit[0] + logit[1]
    klass = lax.broadcasted_iota(jnp.int32, logits.shape, 1)
    inside = klass < classes
    top = jnp.max(jnp.where(inside, logits, -jnp.inf), axis=1, keepdims=True)
    expd = jnp.where(inside, jnp.exp(jnp.where(inside, logits - top, 0.0)), 0.0)
    denom = jnp.sum(expd, axis=1, keepdims=True)
    onehot = klass == label
    picked = jnp.sum(jnp.where(onehot, logits, 0.0), axis=1, keepdims=True)
    partial = jnp.sum(share * (top + jnp.log(denom) - picked), axis=0, keepdims=True)
    d_logits = (share * (expd / denom - jnp.where(onehot, 1.0, 0.0))).astype(BF16)
    d_pooled = matmul_nt(d_logits, head_half) / PIX

    def second_back(h, carry):
        sums, products = carry
        d_y = d_pooled[None] * slope[h]
        slope[h] = d_y
        d_y = d_y[:SIDE].reshape(SIDE * per_chip, half)
        hat = z_two[h][:SIDE].reshape(SIDE * per_chip, half)
        return (
            sums + jnp.sum(d_y, axis=0, keepdims=True),
            products + jnp.sum(d_y * hat, axis=0, keepdims=True),
        )

    d_bias, d_gain = lax.fori_loop(0, SIDE, second_back, (zero_half, zero_half))

    finish = wide_sum(
        1,
        jnp.concatenate(
            [d_gain, d_bias, jnp.broadcast_to(partial, (1, half)), jnp.zeros((5, half), F32)], axis=0
        ),
    )
    inner = act_in[pl.ds(1, SIDE + 1)].reshape((SIDE + 1) * PITCH, per_chip, width)
    inner = inner[1 : 1 + SIDE * PITCH].reshape(SIDE * rows_c, width).astype(F32)
    row = lax.broadcasted_iota(jnp.int32, (SIDE * rows_c, 1), 0)
    inner = jnp.where(lax.rem(lax.div(row, per_chip), PITCH) < SIDE, inner - centre, 0.0)
    act_t[pl.ds(0, width), :] = inner.astype(BF16).T
    gh_swap = new_recv()
    gh_half[...] = matmul_tn(pooled_low, d_logits).astype(BF16).reshape(gh_half.shape)
    push(gh_half.at[:, :, 1 - k], gh.at[pl.ds(2 * k, 2)], (i, sib), gh_swap)
    gh[pl.ds(2 * k, 2)] = jnp.where(
        k == 0, gh_half[:, :, 0].astype(F32), gh_half[:, :, 1].astype(F32)
    ).astype(BF16)
    arrived(gh.at[pl.ds(2 * (1 - k), 2)], gh_swap)
    h_one, h_two, h_z = new_recv(4), new_recv(2), new_recv(4)
    for way, first in enumerate((xn, yn)):
        part = pl.ds(2 * way, 2)
        push(gh.at[dg, part], rh_one.at[way, 1], (first, c), h_one + 2 * way + 1)
        push(gh.at[first, part], rh_one.at[way, 0], (first, c), h_one + 2 * way)
    totals_back = finish()
    loss[...] = totals_back[2:3, :128]
    wide_sib[0] = totals_back
    bn_at = new_recv()
    push(wide_sib.at[0], wide_sib.at[1], (i, sib), bn_at)
    scale = gain_two * inv_two
    shift_two, lean_two = totals_back[1:2] / count_all, totals_back[0:1] / count_all

    def second_grad(h, carry):
        grad = scale * (slope[h] - shift_two - z_two[h] * lean_two)
        pixel = lax.broadcasted_iota(jnp.int32, grad.shape, 0)
        grad = jnp.where(pixel < SIDE, grad, 0.0)
        d_pad[pl.ds(FRONT + PITCH * h, PITCH)] = grad.astype(BF16)
        return carry

    lax.fori_loop(0, SIDE, second_grad, 0)

    def back_conv(h):
        out = jnp.zeros((rows_c, width), F32)
        for t in range(TAPS):
            up, left = tap_of(t)
            rows = d_pad[pl.ds(PITCH * h + FRONT + PITCH + 1 - PITCH * up - left, PITCH)]
            out = out + matmul_nt(rows.reshape(rows_c, half), kern[pl.ds(width * t, width), :])
        return out.reshape(PITCH, per_chip, width)

    s0 = (SIDE - UPPER) * (1 - k)

    def back_theirs(r, carry):
        out = back_conv(s0 + r)
        d_act[s0 + r] = out
        d_send[r] = out[:SIDE].astype(BF16)
        return carry

    def back_mine(r, carry):
        d_act[UPPER * k + r] = back_conv(UPPER * k + r)
        return carry

    lax.fori_loop(0, UPPER, back_theirs, 0)
    d_at = new_recv()
    push(d_send, d_recv, (i, sib), d_at)
    for way, second in enumerate((yn, xn)):
        part = pl.ds(2 * way, 2)
        arrived(rh_one.at[way, 1], h_one + 2 * way + 1)
        gh[second, part] = (gh[second, part].astype(F32) + rh_one[way, 1].astype(F32)).astype(BF16)
        push(gh.at[second, part], rh_two.at[way], (second, c), h_two + way)
    lax.fori_loop(0, SIDE - UPPER, back_mine, 0)

    def kernel_gradient(t, carry):
        rows = d_pad[pl.ds(FRONT + PITCH + 1 - PITCH * lax.div(t, 3) - lax.rem(t, 3), SIDE * PITCH)]
        out = jnp.dot(
            act_t[...], rows.reshape(SIDE * rows_c, half), preferred_element_type=F32
        )
        edge = out[width : width + 1]
        edge_rows[pl.ds(t, 1)] = edge
        gk[pl.ds(pl.multiple_of(width * t, 32), width), :] = out[:width].astype(BF16)
        return carry

    arrived(d_recv, d_at)
    for r in range(UPPER):
        d_send_r = d_act[h0 + r][:SIDE] + d_recv[r].astype(F32)
        d_recv[r] = d_send_r.astype(BF16)
    b_recv = new_recv()
    back_into = images_of(d_one, 0)

    def channels_of(dz):
        return d_recv.at[:, :, :, pl.ds(pl.multiple_of(chip_ch * chip(dz), 128), chip_ch)]

    back_size = d_one.at[:, :, pl.ds(0, 3 * per_chip)]
    push_all([(channels_of(dz), back_into, to_z[dz - 1]) for dz in (3, 2, 1)], back_size, b_recv)
    keep = pltpu.make_async_copy(channels_of(0), back_into, local_sem.at[UPPER])
    keep.start()

    sent.pop(0).wait_send()
    edge_rows[...] = jnp.zeros(edge_rows.shape, F32)
    lax.fori_loop(0, TAPS, kernel_gradient, 0)
    def gk_at(line, dz):
        return gk.at[pl.ds(pl.multiple_of(chunk * (line * 4 + chip(dz)), 32), chunk)]

    ways = {1: (xn, yn), 2: (yn, xn), 3: (xn, yn), 0: (yn, xn)}
    one_at = {dz: new_recv(2) for dz in (3, 2, 1, 0)}
    two_at = {dz: new_recv() for dz in (3, 2, 1, 0)}
    z_at = new_recv(4)

    def start_one(dz):
        first, second = ways[dz]
        push(gk_at(dg, dz), rk_one.at[dz, 1], (first, c), one_at[dz] + 1)
        push(gk_at(first, dz), rk_one.at[dz, 0], (first, c), one_at[dz])

    def start_two(dz):
        first, second = ways[dz]
        arrived(rk_one.at[dz, 1], one_at[dz] + 1)
        into_k = gk_at(second, dz)
        into_k[...] = (into_k[...].astype(F32) + rk_one[dz, 1].astype(F32)).astype(BF16)
        push(into_k, rk_two.at[dz], (second, c), two_at[dz])

    def plane_done(dz):
        arrived(rk_one.at[dz, 0], one_at[dz])
        arrived(rk_two.at[dz], two_at[dz])
        into_k = gk_at(i, dz)
        sum_k = into_k[...].astype(F32) + rk_one[dz, 0].astype(F32) + rk_two[dz].astype(F32)
        if dz == 0:
            return sum_k
        into_k[...] = sum_k.astype(BF16)
        push(into_k, rk_z.at[z], (i, zdev(dz)), z_at + z)
        return None

    start_one(3)
    start_one(2)
    for way in (0, 1):
        part = pl.ds(2 * way, 2)
        arrived(rh_one.at[way, 0], h_one + 2 * way)
        arrived(rh_two.at[way], h_two + way)
        sum_h = gh[i, part].astype(F32) + rh_one[way, 0].astype(F32) + rh_two[way].astype(F32)
        h_sum[part] = sum_h
        gh[i, part] = sum_h.astype(BF16)
    for dz in (3, 2, 1):
        push(gh.at[i, chip(dz)], rh_z.at[z], (i, zdev(dz)), h_z + z)

    keep.wait()
    arrived(back_size, b_recv)

    def first_back(r, carry):
        sums, products = carry
        at = pl.ds(pl.multiple_of(rows_a * r, 64), rows_a)
        hat = (z_one[at, :] - mean_one) * inv_one
        z_one[at, :] = hat
        _, grade = silu_pair(gain_one * hat + bias_one)
        d_y = d_one[r].reshape(rows_a, chip_ch).astype(F32) * grade
        counted = jnp.where((r == 0) & (k == 1), 0.0, 1.0)
        return (
            sums + counted * jnp.sum(d_y, axis=0, keepdims=True),
            products + counted * jnp.sum(d_y * hat, axis=0, keepdims=True),
        )

    d_bias, d_gain = lax.fori_loop(0, UPPER, first_back, (zero_row, zero_row))
    finish = small_sum(
        1, jnp.concatenate([d_gain, d_bias, jnp.zeros((6, 128), F32)], axis=0)
    )
    start_two(3)
    start_two(2)
    start_one(1)
    start_one(0)
    finish_edges = wide_sum(2, edge_rows[...])
    totals_one = finish()
    g_bn_one[...] = jnp.where(k == 0, totals_one[0:2, :own_ch], totals_one[0:2, own_ch:])
    scale_one = gain_one * inv_one
    shift_one, lean_one = totals_one[1:2] / count_all, totals_one[0:1] / count_all

    def first_grad(r, carry):
        at = pl.ds(pl.multiple_of(rows_a * r, 64), rows_a)
        hat = z_one[at, :]
        _, grade = silu_pair(gain_one * hat + bias_one)
        d_y = d_one[r].reshape(rows_a, chip_ch).astype(F32) * grade
        counted = jnp.where((r == 0) & (k == 1), 0.0, 1.0)
        grad = (counted * scale_one) * (d_y - shift_one - hat * lean_one)
        act_out[r] = grad.astype(BF16).reshape(SIDE, group, chip_ch)
        return carry

    for copy in out_copies:
        copy.wait_send()
    sent[:] = [copy for copy in sent if all(copy is not done for done in out_copies)]
    lax.fori_loop(0, UPPER, first_grad, 0)

    grad_t[...] = act_out[...].reshape(UPPER * rows_a, chip_ch).T

    def first_weights(n, carry):
        at = pl.ds(pl.multiple_of(256 * n, 256), 256)
        rows = feats[:, :, at].reshape(UPPER * rows_a, 256)
        g_acc[:, at] = jnp.dot(grad_t[...], rows, preferred_element_type=F32)
        return carry

    lax.fori_loop(0, feats.shape[2] // 256, first_weights, 0)
    low, high = g_acc[:own_ch], g_acc[own_ch:]
    go_send[...] = jnp.where(k == 0, high, low).astype(BF16)
    g_at = new_recv()
    push(go_send, go_recv, (i, sib), g_at)
    g_one[...] = jnp.where(k == 0, low, high)
    plane_done(3)
    plane_done(2)
    arrived(go_recv, g_at)
    part = own_ch // 2
    ga_send[0] = (g_one[...] + go_recv[...].astype(F32)).astype(BF16)
    first_at, second_at = new_recv(2), new_recv(2)
    upper, lower = pl.ds(0, part), pl.ds(part, part)
    push(ga_send.at[0, upper], ga_recv.at[0, upper], (xn, c), first_at)
    push(ga_send.at[0, lower], ga_recv.at[0, lower], (yn, c), first_at + 1)
    start_two(1)
    start_two(0)
    arrived(ga_recv.at[0, upper], first_at)
    arrived(ga_recv.at[0, lower], first_at + 1)
    ga_send[1] = (ga_send[0].astype(F32) + ga_recv[0].astype(F32)).astype(BF16)
    push(ga_send.at[1, upper], ga_recv.at[1, upper], (yn, c), second_at)
    push(ga_send.at[1, lower], ga_recv.at[1, lower], (xn, c), second_at + 1)

    edges = finish_edges()
    plane_done(1)
    sum_k = plane_done(0)

    arrived(ga_recv.at[1, upper], second_at)
    arrived(ga_recv.at[1, lower], second_at + 1)
    g_one[...] = ga_send[1].astype(F32) + ga_recv[1].astype(F32)

    row_at = chunk * (i * 4 + z)
    tap = lax.div(row_at, width)
    edge_rows[...] = edges
    for step in range(2):
        ranked[pl.ds(width * step, width), :] = rank_one(
            centre, edge_rows[pl.ds(lax.rem(tap + step, TAPS), 1)]
        )
    offset = pl.multiple_of(row_at - width * tap, 32)
    sum_k = sum_k + ranked[pl.ds(offset, chunk), :]
    sum_h = h_sum[z]
    for dz in (1, 2, 3):
        arrived(rk_z.at[chip(dz)], z_at + chip(dz))
        arrived(rh_z.at[chip(dz)], h_z + chip(dz))
        sum_k = sum_k + rk_z[chip(dz)].astype(F32)
        sum_h = sum_h + rh_z[chip(dz)].astype(F32)
    head_flat[...] = sum_h
    g_head[...] = jnp.zeros(g_head.shape, F32)
    for r in range(head_rows):
        first, shift = divmod(classes * r, 128)
        rows = jnp.concatenate(
            [head_flat[r : r + 1, 128 * j : 128 * j + 128] for j in range(8)], axis=0
        )
        if shift:
            rows = pltpu.roll(rows, shift, 1)
        count = min(8, g_head.shape[0] - first)
        g_head[first : first + count, :] += jnp.where(lane >= shift, rows, 0.0)[:count]
        count = min(8, g_head.shape[0] - first - 1)
        if shift:
            g_head[first + 1 : first + 1 + count, :] += jnp.where(lane < shift, rows, 0.0)[:count]
    last_send[...] = sum_k
    l_at = new_recv()
    theirs = last_send.at[pl.ds(pl.multiple_of(block * (1 - k), 16), block)]
    push(theirs, last_recv, (i, sib), l_at)
    mine = last_send[pl.ds(pl.multiple_of(block * k, 16), block), :]
    arrived(last_recv, l_at)
    other = last_recv[...]
    for j in range(4):
        lanes = slice(128 * (j % 2), 128 * (j % 2) + 128)
        g_two[pl.ds(j, block, stride=4), :] = jnp.where(
            k == j // 2, mine[:, lanes], other[:, lanes]
        )

    arrived(wide_sib.at[1], bn_at)
    own_bn, other_bn = wide_sib[0], wide_sib[1]
    g_bn_two[...] = jnp.where(
        k == 0,
        jnp.concatenate([own_bn[0:2], other_bn[0:2]], axis=1),
        jnp.concatenate([other_bn[0:2], own_bn[0:2]], axis=1),
    )
    for copy in sent:
        copy.wait_send()


def update_kernel(rates, *refs):
    take, give = refs[:24], refs[24:]
    rate_one, rate_bn_one, rate_two, rate_bn_two, rate_head = rates
    w, g, m, v, mask, rank = (r[...] for r in take[:6])
    results = sparse_update(w, g * mask.astype(F32), m, v, mask, rank, rate_one)
    for ref, value in zip(give[:5], results):
        ref[...] = value
    w, g, m, v, mask, rank = (r[...] for r in take[6:12])
    results = sparse_update(w, g * mask.astype(F32), m, v, mask, rank, rate_two)
    for ref, value in zip(give[5:10], results):
        ref[...] = value

    @pl.when(pl.program_id(0) == 0)
    def _():
        for n, rate in enumerate((rate_bn_one, rate_bn_two, rate_head)):
            w, g, m, v = (r[...] for r in take[12 + 4 * n : 16 + 4 * n])
            results = dense_update(w, g, m, v, rate)
            for ref, value in zip(give[10 + 3 * n : 13 + 3 * n], results):
                ref[...] = value
        give[19][...] = results[0].astype(BF16)


def fast_shards(
    images_in, labels, loss_wt, placement,
    w_one, mom_one, avg_one, mask_one, rank_one_in, first_norm_params, mom_bn_one, avg_bn_one,
    w_two, mom_two, avg_two, mask_two, rank_two, second_norm_params, mom_bn_two, avg_bn_two,
    w_head, mom_head, avg_head,
):
    n_img, n_ch = lax.axis_size("img"), lax.axis_size("ch")
    group, cin = images_in.shape[0], images_in.shape[2]
    per_core = labels.shape[0]
    per_chip = 2 * per_core
    width = second_norm_params.shape[1]
    half = width // 2
    own_ch = w_one.shape[1]
    chip_ch = 2 * own_ch
    classes = w_head.shape[0] * n_img * n_ch // width
    images = per_core * n_img * n_ch
    head_rows = w_head.shape[0] // classes
    lanes = -(-classes // 512) * 512
    block = w_two.shape[0] // width
    chunk = 2 * block
    flat = (w_two.shape[0] // 128, 128)
    top = [a.reshape(-1, 128) for a in (w_head, mom_head, avg_head)]
    one = [a.T for a in (w_one, mom_one, avg_one, mask_one, rank_one_in)]
    two = [a.reshape(flat) for a in (w_two, mom_two, avg_two, mask_two, rank_two)]
    vmem = pl.BlockSpec(memory_space=pltpu.VMEM)
    hbm = pl.BlockSpec(memory_space=pltpu.HBM)
    v = pltpu.VMEM
    shape = jax.ShapeDtypeStruct
    g_one, g_two, g_head, g_bn_one, g_bn_two, loss = pl.pallas_call(
        functools.partial(step_kernel, (group, per_chip, classes, images)),
        out_shape=(
            shape((own_ch, cin), F32),
            shape(flat, F32),
            shape(top[0].shape, F32),
            shape((2, own_ch), F32),
            shape((2, width), F32),
            shape((1, 128), F32),
        ),
        in_specs=[hbm] * 11,
        out_specs=[vmem] * 6,
        scratch_shapes=[
            v((own_ch, cin), F32),
            v((own_ch, cin), jnp.int32),
            v(flat, F32),
            v(flat, jnp.int32),
            v(top[0].shape, F32),
            v((2, own_ch), F32),
            v((2, width), F32),
            v((1, group), jnp.int32),
            pltpu.SMEM((per_core,), jnp.int32),
            pltpu.SMEM((per_core,), jnp.int32),
            v((UPPER * SIDE, group, cin), BF16),
            v((chip_ch, cin), BF16),
            v((TAPS * width, half), BF16),
            v((4, 4, 2, head_rows, lanes), BF16),
            v((SIDE + 3, PITCH, per_chip, width), BF16),
            v((UPPER, SIDE, group, chip_ch), BF16),
            v((UPPER * SIDE * group, chip_ch), F32),
            v((SIDE, PITCH, per_chip, half), F32),
            v((SIDE, PITCH, per_chip, half), F32),
            v((2 * FRONT + SIDE * PITCH, per_chip, half), BF16),
            v((width + 16, SIDE * PITCH * per_chip), BF16),
            v((SIDE, PITCH, per_chip, width), F32),
            v((UPPER, SIDE, per_chip, width), BF16),
            v((UPPER, SIDE, per_chip, width), BF16),
            v((UPPER, SIDE, group, chip_ch), BF16),
            v((2, 8, 128), F32),
            v((4, 8, 128), F32),
            v((2, 8, 8, 128), F32),
            v((3, 16, 16, half), F32),
            v((2, 8, half), F32),
            v((2, per_chip, lanes), F32),
            v((2, 4, 2, head_rows, lanes), BF16),
            v((TAPS * width, half), BF16),
            v((4, 4, head_rows, lanes), BF16),
            v((4, 2, chunk, half), BF16),
            v((2, 2, 2, head_rows, lanes), BF16),
            v((4, chunk, half), BF16),
            v((2, 2, head_rows, lanes), BF16),
            v((4, chunk, half), BF16),
            v((4, head_rows, lanes), BF16),
            v((4, head_rows, lanes), F32),
            v((head_rows, lanes), F32),
            v((chunk, half), F32),
            v((block, half), F32),
            v((16, half), F32),
            v((2 * width, half), F32),
            v((chip_ch, UPPER * SIDE * group), BF16),
            v((chip_ch, cin), F32),
            v((own_ch, cin), BF16),
            v((own_ch, cin), BF16),
            v((2, own_ch, cin), BF16),
            v((2, own_ch, cin), BF16),
            pltpu.SemaphoreType.DMA((10,)),
            pltpu.SemaphoreType.DMA((UPPER,)),
            pltpu.SemaphoreType.DMA((UPPER + 1,)),
            pltpu.SemaphoreType.DMA((SEMS,)),
            pltpu.SemaphoreType.DMA((SEMS,)),
        ],
        compiler_params=pltpu.CompilerParams(
            collective_id=0, has_side_effects=True, vmem_limit_bytes=56 << 20
        ),
        name="step",
    )(
        images_in.transpose(1, 0, 2),
        placement,
        labels,
        loss_wt,
        one[0],
        one[3],
        first_norm_params,
        two[0],
        two[3],
        top[0],
        second_norm_params,
    )
    root = math.sqrt(images)
    steps = 2
    one_spec = pl.BlockSpec((own_ch // steps, cin), lambda n: (n, 0))
    two_spec = pl.BlockSpec((flat[0] // steps, 128), lambda n: (n, 0))
    bno_spec = pl.BlockSpec((2, own_ch), lambda n: (0, 0))
    bnt_spec = pl.BlockSpec((2, width), lambda n: (0, 0))
    top_spec = pl.BlockSpec(top[0].shape, lambda n: (0, 0))
    f_one, f_two = shape(one[0].shape, F32), shape(flat, F32)
    new = pl.pallas_call(
        functools.partial(update_kernel, (1.3 * root, 8.0 * root, 0.25 * root, root, 40.0)),
        grid=(steps,),
        in_specs=[one_spec] * 6 + [two_spec] * 6 + [bno_spec] * 4 + [bnt_spec] * 4 + [top_spec] * 4,
        out_specs=[one_spec] * 5 + [two_spec] * 5 + [bno_spec] * 3 + [bnt_spec] * 3 + [top_spec] * 4,
        out_shape=[f_one] * 3 + [shape(f_one.shape, jnp.int32), shape(f_one.shape, BF16)]
        + [f_two] * 3 + [shape(flat, jnp.int32), shape(flat, BF16)]
        + [shape((2, own_ch), F32)] * 3 + [shape((2, width), F32)] * 3
        + [shape(top[0].shape, F32)] * 3 + [shape(top[0].shape, BF16)],
        compiler_params=pltpu.CompilerParams(vmem_limit_bytes=56 << 20),
        name="update",
    )(
        one[0], g_one, one[1], one[2], one[3], one[4],
        two[0], g_two, two[1], two[2], two[3], two[4],
        first_norm_params, g_bn_one, mom_bn_one, avg_bn_one,
        second_norm_params, g_bn_two, mom_bn_two, avg_bn_two,
        top[0], g_head, top[1], top[2],
    )
    return (
        loss[0, 0],
        *(a.T for a in new[:5]),
        *new[10:13],
        *(a.reshape(-1) for a in new[5:10]),
        *new[13:16],
        *(a.reshape(-1) for a in new[16:20]),
    )


def solution(mesh):
    in_specs = (
        P("img", None, None),
        P(("img", "ch")),
        P(("img", "ch")),
        P("img", None),
        P(None, "ch"),
        P(None, "ch"),
        P(None, "ch"),
        P(None, "ch"),
        P(None, "ch"),
        P(None, "ch"),
        P(None, "ch"),
        P(None, "ch"),
        P(("img", "ch")),
        P(("img", "ch")),
        P(("img", "ch")),
        P(("img", "ch")),
        P(("img", "ch")),
        P(),
        P(),
        P(),
        P(("img", "ch")),
        P(("img", "ch")),
        P(("img", "ch")),
    )
    out_specs = (
        P(),
        P(None, "ch"),
        P(None, "ch"),
        P(None, "ch"),
        P(None, "ch"),
        P(None, "ch"),
        P(None, "ch"),
        P(None, "ch"),
        P(None, "ch"),
        P(("img", "ch")),
        P(("img", "ch")),
        P(("img", "ch")),
        P(("img", "ch")),
        P(("img", "ch")),
        P(),
        P(),
        P(),
        P(("img", "ch")),
        P(("img", "ch")),
        P(("img", "ch")),
        P(("img", "ch")),
    )
    fast = mesh.shape["img"] == 4 and mesh.shape["ch"] == 8
    return jax.shard_map(fast_shards if fast else shards, mesh=mesh, in_specs=in_specs, out_specs=out_specs, check_vma=False)
```

```python
import functools
import itertools
import math

import jax
import jax.numpy as jnp
from jax import lax
from jax.experimental import pallas as pl
from jax.experimental.pallas import tpu as pltpu
from jax.sharding import PartitionSpec as P

SIDE = 7
PIX = 49
DROP = 10
GROW = 10


EPS = 1e-05
MOMENTUM = 0.5


def advance(weight, grad, velocity, rate):
    velocity = MOMENTUM * velocity + grad
    return (weight - rate * (grad + MOMENTUM * velocity), velocity)


def dense_update(weight, grad, velocity, average, rate):
    moved, velocity = advance(weight, grad, velocity, rate)
    return (moved, velocity, 0.5 * average + 0.5 * moved)


def sparse_update(weight, grad, velocity, average, mask, rank, rate):
    moved, velocity = advance(weight, grad, velocity, rate)
    kept = (mask == 1) & (rank >= DROP)
    grown = (mask == 0) & (rank < GROW)
    new_mask = jnp.where(kept | grown, 1, 0).astype(jnp.int32)
    weight = jnp.where(kept, moved, 0.0)
    velocity = jnp.where(kept, velocity, 0.0)
    average = 0.5 * average + 0.5 * weight
    return (weight, velocity, average, new_mask, weight.astype(jnp.bfloat16))


def silu_slope(value):
    sigma = jax.nn.sigmoid(value)
    return sigma * (1.0 + value * (1.0 - sigma))


def apply_batch_norm(z, sums, squares, element_count):
    mean = sums / element_count
    inverse_deviation = lax.rsqrt(squares / element_count - mean * mean + EPS)
    return ((z - mean) * inverse_deviation, inverse_deviation)


def batch_norm_backward(
    norm_gain,
    inverse_deviation,
    output_gradient,
    standardized_input,
    bias_gradient_sum,
    gain_gradient_sum,
    element_count,
):
    return (
        norm_gain
        * inverse_deviation
        * (
            output_gradient
            - bias_gradient_sum / element_count
            - standardized_input * gain_gradient_sum / element_count
        )
    )


def contract_rows(left, right):
    return jnp.einsum("pk,pc->kc", left, right, preferred_element_type=jnp.float32)


def shards(
    images_in,
    labels,
    loss_wt,
    placement,
    w_one,
    mom_one,
    avg_one,
    mask_one,
    rank_one,
    first_norm_params,
    mom_bn_one,
    avg_bn_one,
    w_two,
    mom_two,
    avg_two,
    mask_two,
    rank_two,
    second_norm_params,
    mom_bn_two,
    avg_bn_two,
    w_head,
    mom_head,
    avg_head,
):
    n_img = lax.axis_size("img")
    n_ch = lax.axis_size("ch")
    group = images_in.shape[0]
    element_count = labels.shape[0]
    width = second_norm_params.shape[1]
    classes = w_head.shape[0] * n_img * n_ch // width
    images = element_count * n_img * n_ch
    slot_info = jnp.stack([labels.astype(jnp.float32), loss_wt.astype(jnp.float32)])
    slot_info = lax.all_gather(slot_info, "ch", axis=1, tiled=True)
    own = lax.axis_index("ch") * element_count + jnp.arange(element_count, dtype=jnp.int32)
    fills = placement[0][None, :] == own[:, None]
    labels_f, weights = jnp.sum(jnp.where(fills[None], slot_info[:, None, :], 0.0), axis=2)
    labels = labels_f.astype(jnp.int32)
    kernel_part = (w_two * mask_two.astype(jnp.float32)).astype(jnp.bfloat16)
    kernel = lax.all_gather(kernel_part, ("img", "ch"), axis=0, tiled=True)
    head = lax.all_gather(w_head.astype(jnp.bfloat16), ("img", "ch"), axis=0, tiled=True)
    kernel = kernel.reshape(9 * width, width)
    head = head.reshape(width, classes)
    rows = images_in.transpose(1, 0, 2).reshape(PIX * group, images_in.shape[2])
    filt_one = (w_one * mask_one.astype(jnp.float32)).astype(jnp.bfloat16)
    first_conv_output = jnp.dot(rows, filt_one, preferred_element_type=jnp.float32)
    first_feature_sum, first_squares_sum, total = lax.psum(
        (
            jnp.sum(first_conv_output, axis=0),
            jnp.sum(first_conv_output * first_conv_output, axis=0),
            jnp.sum(slot_info[1]),
        ),
        "img",
    )
    first_element_count = group * PIX * n_img
    first_standardized_input, first_inverse_deviation = apply_batch_norm(
        first_conv_output, first_feature_sum, first_squares_sum, first_element_count
    )
    first_norm_output = first_norm_params[0] * first_standardized_input + first_norm_params[1]
    act = jax.nn.silu(first_norm_output).astype(jnp.bfloat16).reshape(PIX, group, -1)
    act_in = lax.all_to_all(act, "ch", split_axis=1, concat_axis=2, tiled=True)
    padded = jnp.pad(
        act_in.reshape(SIDE, SIDE, element_count, width), ((1, 1), (1, 1), (0, 0), (0, 0))
    )
    patches = jnp.concatenate(
        [
            padded[tap // 3 : tap // 3 + SIDE, tap % 3 : tap % 3 + SIDE].reshape(
                PIX * element_count, width
            )
            for tap in range(9)
        ],
        axis=1,
    )
    second_conv_output = jnp.dot(patches, kernel, preferred_element_type=jnp.float32)
    second_feature_sum, second_squares_sum = lax.psum(
        (
            jnp.sum(second_conv_output, axis=0),
            jnp.sum(second_conv_output * second_conv_output, axis=0),
        ),
        ("img", "ch"),
    )
    second_element_count = images * PIX
    second_standardized_input, second_inverse_deviation = apply_batch_norm(
        second_conv_output, second_feature_sum, second_squares_sum, second_element_count
    )
    second_norm_output = second_norm_params[0] * second_standardized_input + second_norm_params[1]
    pooled = jnp.mean(jax.nn.silu(second_norm_output).reshape(PIX, element_count, width), axis=0)
    pooled_low = pooled.astype(jnp.bfloat16)
    logits = jnp.dot(pooled_low, head, preferred_element_type=jnp.float32)
    top = jnp.max(logits, axis=1, keepdims=True)
    expd = jnp.exp(logits - top)
    denom = jnp.sum(expd, axis=1, keepdims=True)
    lse = top[:, 0] + jnp.log(denom[:, 0])
    onehot = labels[:, None] == jnp.arange(classes, dtype=jnp.int32)[None, :]
    picked = jnp.sum(jnp.where(onehot, logits, 0.0), axis=1)
    share = weights / total
    partial_loss_value = jnp.sum(share * (lse - picked))
    d_logits = (share[:, None] * (expd / denom - onehot.astype(jnp.float32))).astype(jnp.bfloat16)
    g_head = contract_rows(pooled_low, d_logits)
    d_pooled = jnp.einsum("ic,kc->ik", d_logits, head, preferred_element_type=jnp.float32)
    d_act = jnp.broadcast_to(d_pooled[None] / PIX, (PIX, element_count, width)).reshape(
        PIX * element_count, width
    )
    second_output_gradient = d_act * silu_slope(second_norm_output)
    second_shift_bias, second_norm_gain, loss = lax.psum(
        (
            jnp.sum(second_output_gradient, axis=0),
            jnp.sum(second_output_gradient * second_standardized_input, axis=0),
            partial_loss_value,
        ),
        ("img", "ch"),
    )
    second_preact_gradient = batch_norm_backward(
        second_norm_params[0],
        second_inverse_deviation,
        second_output_gradient,
        second_standardized_input,
        second_shift_bias,
        second_norm_gain,
        second_element_count,
    ).astype(jnp.bfloat16)
    d_patches = jnp.einsum(
        "pc,kc->pk", second_preact_gradient, kernel, preferred_element_type=jnp.float32
    )
    d_pad = 0.0
    for tap in range(9):
        piece = d_patches[:, tap * width : (tap + 1) * width].reshape(
            SIDE, SIDE, element_count, width
        )
        up, left = tap // 3, tap % 3
        d_pad = d_pad + jnp.pad(piece, ((up, 2 - up), (left, 2 - left), (0, 0), (0, 0)))
    d_act_in = d_pad[1:-1, 1:-1].astype(jnp.bfloat16).reshape(PIX, element_count, width)
    d_act_one = lax.all_to_all(d_act_in, "ch", split_axis=2, concat_axis=1, tiled=True)
    g_kernel = contract_rows(patches, second_preact_gradient)
    d_act_one = d_act_one.reshape(PIX * group, -1).astype(jnp.float32)
    first_output_gradient = d_act_one * silu_slope(first_norm_output)
    first_shift_bias, first_norm_gain = lax.psum(
        (
            jnp.sum(first_output_gradient, axis=0),
            jnp.sum(first_output_gradient * first_standardized_input, axis=0),
        ),
        "img",
    )
    first_preact_gradient = batch_norm_backward(
        first_norm_params[0],
        first_inverse_deviation,
        first_output_gradient,
        first_standardized_input,
        first_shift_bias,
        first_norm_gain,
        first_element_count,
    ).astype(jnp.bfloat16)
    g_filt = lax.psum(
        contract_rows(rows, first_preact_gradient).astype(jnp.bfloat16), "img"
    ).astype(jnp.float32)
    g_one = g_filt * mask_one.astype(jnp.float32)
    part_two = lax.psum_scatter(
        g_kernel.reshape(-1), ("img", "ch"), tiled=True
    )
    part_head = lax.psum_scatter(
        g_head.reshape(-1), ("img", "ch"), tiled=True
    )
    g_two = part_two * mask_two.astype(jnp.float32)
    root = math.sqrt(images)
    one = sparse_update(w_one, g_one, mom_one, avg_one, mask_one, rank_one, 1.3 * root)
    bno = dense_update(
        first_norm_params,
        jnp.stack([first_norm_gain, first_shift_bias]),
        mom_bn_one,
        avg_bn_one,
        8.0 * root,
    )
    two = sparse_update(w_two, g_two, mom_two, avg_two, mask_two, rank_two, 0.25 * root)
    bnt = dense_update(
        second_norm_params,
        jnp.stack([second_norm_gain, second_shift_bias]),
        mom_bn_two,
        avg_bn_two,
        root,
    )
    top_head = dense_update(w_head, part_head, mom_head, avg_head, 40.0)
    return (
        loss,
        one[0],
        one[1],
        one[2],
        one[3],
        one[4],
        bno[0],
        bno[1],
        bno[2],
        two[0],
        two[1],
        two[2],
        two[3],
        two[4],
        bnt[0],
        bnt[1],
        bnt[2],
        top_head[0],
        top_head[1],
        top_head[2],
        top_head[0].astype(jnp.bfloat16),
    )


F32, BF16 = jnp.float32, jnp.bfloat16
MESH = pl.DeviceIdType.MESH
TAPS = 9
UPPER = (SIDE + 1) // 2
PITCH = SIDE + 1
FRONT = 2 * PITCH
SENDS, RECEIVES = 48, 95


def silu_pair(value):
    sigma = 1.0 / (1.0 + jnp.exp(-value))
    return value * sigma, sigma * (1.0 + value * (1.0 - sigma))


def matmul_nt(left, right):
    return lax.dot_general(left, right, (((1,), (1,)), ((), ())), preferred_element_type=F32)


def matmul_tn(left, right):
    return lax.dot_general(left, right, (((0,), (0,)), ((), ())), preferred_element_type=F32)


def rank_one(row, other):
    first = other.astype(BF16)
    rest = other - first.astype(F32)
    second = rest.astype(BF16)
    third = (rest - second.astype(F32)).astype(BF16)
    place = lax.broadcasted_iota(jnp.int32, (16, other.shape[1]), 0)
    parts = jnp.where(place == 0, first.astype(F32), 0.0)
    parts = jnp.where(place == 1, second.astype(F32), parts)
    parts = jnp.where(place == 2, third.astype(F32), parts)
    rows = jnp.broadcast_to(row, (16, row.shape[1])).astype(BF16)
    return matmul_tn(rows, parts.astype(BF16))


def step_kernel(
    sizes,
    images,
    place_in,
    labels_in,
    loss_wt_in,
    w_one_in,
    mask_one_in,
    norm_one_in,
    w_two_in,
    mask_two_in,
    w_head_in,
    norm_two_in,
    g_one,
    g_two,
    g_head,
    g_bn_one,
    g_bn_two,
    loss,
    w_one,
    mask_one,
    w_two,
    mask_two,
    w_head,
    norm_one,
    norm_two,
    place,
    labels,
    loss_wt,
    feats,
    filt,
    kern,
    head,
    act_in,
    act_out,
    z_one,
    z_two,
    slope,
    d_pad,
    act_t,
    d_act,
    d_send,
    d_recv,
    d_one,
    early,
    info,
    tiles,
    wide,
    wide_sib,
    logit,
    gh_half,
    gk,
    gh,
    rk_one,
    rh_one,
    rk_two,
    rh_two,
    rk_z,
    rh_z,
    h_sum,
    head_flat,
    last_send,
    last_recv,
    edge_rows,
    ranked,
    grad_t,
    g_acc,
    go_send,
    go_recv,
    ga_send,
    ga_recv,
    kern_t,
    hat_t,
    m_two,
    load_sem,
    image_sem,
    local_sem,
    send,
    recv,
):
    group, per_chip, classes, images_in_all = sizes
    width = norm_two.shape[1]
    half = width // 2
    own_ch = w_one.shape[0]
    chip_ch = 2 * own_ch
    block = w_two.shape[0] * 128 // width
    chunk = 2 * block
    head_rows = head.shape[3]
    rows_a = SIDE * group
    rows_c = PITCH * per_chip
    count_all = float(images_in_all * PIX)

    i, c = lax.axis_index("img"), lax.axis_index("ch")
    z, k = lax.div(c, 2), lax.rem(c, 2)
    sib = c + 1 - 2 * k
    xn, yn, dg = i + 1 - 2 * lax.rem(i, 2), lax.rem(i + 2, 4), 3 - i
    lines = (xn, yn, dg)
    near = (z, z + 1 - 2 * lax.rem(z, 2), 2 - lax.div(z, 2), 3 - 3 * lax.div(z, 2))
    h0 = (SIDE - UPPER) * k

    def chip(dz):
        return near[dz]

    def zdev(dz):
        return 2 * chip(dz) + k

    next_send, next_recv = itertools.count(), itertools.count()
    sent = []

    def new_recv(n=1):
        first = next(next_recv)
        for _ in range(n - 1):
            next(next_recv)
        return first

    def push(src, dst, device, to):
        copy = pltpu.make_async_remote_copy(
            src_ref=src,
            dst_ref=dst,
            send_sem=send.at[next(next_send)],
            recv_sem=recv.at[to],
            device_id=device,
            device_id_type=MESH,
        )
        copy.start()
        sent.append(copy)
        return copy

    def push_all(copies, size_of, to):
        at = next(next_send)
        for src, dst, device in copies:
            pltpu.make_async_remote_copy(
                src_ref=src,
                dst_ref=dst,
                send_sem=send.at[at],
                recv_sem=recv.at[to],
                device_id=device,
                device_id_type=MESH,
            ).start()
        group_copy = pltpu.make_async_remote_copy(
            src_ref=size_of,
            dst_ref=size_of,
            send_sem=send.at[at],
            recv_sem=recv.at[to],
            device_id=(i, sib),
            device_id_type=MESH,
        )
        sent.append(group_copy)
        return group_copy

    def start(at, to, src, dst, device):
        pltpu.make_async_remote_copy(
            src_ref=src,
            dst_ref=dst,
            send_sem=send.at[at],
            recv_sem=recv.at[to],
            device_id=device,
            device_id_type=MESH,
        ).start()

    def size_wait(ref, at, to):
        return pltpu.make_async_remote_copy(
            src_ref=ref,
            dst_ref=ref,
            send_sem=send.at[at],
            recv_sem=recv.at[to],
            device_id=(i, sib),
            device_id_type=MESH,
        )

    def arrived(dst, at):
        pltpu.make_async_remote_copy(
            src_ref=dst,
            dst_ref=dst,
            send_sem=send.at[0],
            recv_sem=recv.at[at],
            device_id=(i, sib),
            device_id_type=MESH,
        ).wait_recv()

    def image_copy(r):
        return pltpu.make_async_copy(
            images.at[pl.ds(SIDE * (h0 + r), SIDE)], feats.at[pl.ds(SIDE * r, SIDE)], image_sem.at[r]
        )

    barrier = pltpu.get_barrier_semaphore()
    same_core = [(o, zdev(dz)) for o in (i, *lines) for dz in (0, 1, 2, 3)][1:]
    plane = [(i, sib)] + [(o, d) for o in lines for d in (c, sib)]
    others = plane + same_core[:3]
    for device in others:
        pl.semaphore_signal(barrier, inc=1, device_id=device, device_id_type=MESH)
    loads = [
        pltpu.make_async_copy(src, dst, load_sem.at[n])
        for n, (src, dst) in enumerate(
            (
                (w_two_in, w_two),
                (mask_two_in, mask_two),
                (w_one_in, w_one),
                (mask_one_in, mask_one),
                (norm_one_in, norm_one),
                (labels_in, labels),
                (loss_wt_in, loss_wt),
                (w_head_in, w_head),
                (norm_two_in, norm_two),
                (place_in, place),
            )
        )
    ]
    for copy in loads:
        copy.start()
    for r in range(UPPER):
        image_copy(r).start()

    loads[0].wait()
    loads[1].wait()
    chunk_at = pl.multiple_of(chunk * (i * 4 + z), 32)
    block_at = pl.multiple_of(chunk_at + block * k, 16)
    parts = [
        w_two[pl.ds(j, block, stride=4), :] * mask_two[pl.ds(j, block, stride=4), :].astype(F32)
        for j in range(4)
    ]
    low = jnp.concatenate(parts[:2], axis=1).astype(BF16)
    high = jnp.concatenate(parts[2:], axis=1).astype(BF16)
    kern[pl.ds(block_at, block), :] = jnp.where(k == 0, low.astype(F32), high.astype(F32)).astype(BF16)
    gk[pl.ds(0, block), :] = jnp.where(k == 0, high.astype(F32), low.astype(F32)).astype(BF16)
    for copy in loads[2:7]:
        copy.wait()
    own_at = pl.multiple_of(own_ch * k, 16)
    filt[pl.ds(own_at, own_ch), :] = (w_one[...] * mask_one[...].astype(F32)).astype(BF16)
    lane = lax.broadcasted_iota(jnp.int32, (1, 128), 1)
    norms = norm_one[...]
    nothing = jnp.zeros_like(norms)
    placed = jnp.where(
        k == 0, jnp.concatenate([norms, nothing], axis=1), jnp.concatenate([nothing, norms], axis=1)
    )
    label_row, weight_row = jnp.zeros((1, 128), F32), jnp.zeros((1, 128), F32)
    for j in range(labels.shape[0]):
        here = lane == labels.shape[0] * c + j
        label_row = jnp.where(here, labels[j].astype(F32), label_row)
        weight_row = jnp.where(here, loss_wt[j].astype(F32), weight_row)
    early[0] = jnp.concatenate(
        [placed, label_row, weight_row, jnp.zeros((4, 128), F32)], axis=0
    )

    pl.semaphore_wait(barrier, len(others))

    k_sib, f_sib, e_sib = new_recv(), new_recv(), new_recv()
    push(gk.at[pl.ds(0, block)], kern.at[pl.ds(block_at, block)], (i, sib), k_sib)
    push(filt.at[pl.ds(own_at, own_ch)], filt.at[pl.ds(own_at, own_ch)], (i, sib), f_sib)
    push(early.at[0], early.at[1], (i, sib), e_sib)

    k_recv = new_recv(32)

    def kern_at(line, dz, u):
        at = chunk * (line * 4 + chip(dz)) + block * (k if u == 0 else 1 - k)
        return kern.at[pl.ds(pl.multiple_of(at, 16), block)]

    k_send, k_count = next(next_send), itertools.count(1)

    def forward(line, dz, u, *devices):
        for device in devices:
            at = k_recv + 2 * (line * 4 + chip(dz)) + u
            start(k_send, at, kern_at(line, dz, u), kern_at(line, dz, u), device)
            next(k_count)

    def landed(line, dz, u):
        arrived(kern_at(line, dz, u), k_recv + 2 * (line * 4 + chip(dz)) + u)

    def relay(line, dz, u, *devices):
        landed(line, dz, u)
        forward(line, dz, u, *devices)

    to_x, to_y = (xn, c), (yn, c)
    to_z = [(i, zdev(dz)) for dz in (1, 2, 3)]
    forward(i, 0, 0, to_x, to_y, *to_z[::-1])
    act_in[0] = jnp.zeros(act_in.shape[1:], BF16)
    for r in range(SIDE + 1, act_in.shape[0]):
        act_in[r] = jnp.zeros(act_in.shape[1:], BF16)
    for r in range(1, SIDE + 1):
        act_in[r, 0] = jnp.zeros(act_in.shape[2:], BF16)
    other_block_at = pl.multiple_of(chunk_at + block * (1 - k), 16)
    arrived(kern.at[pl.ds(other_block_at, block)], k_sib)
    forward(i, 0, 1, to_x, to_y, *to_z[::-1])
    arrived(early.at[1], e_sib)
    both = early[0] + early[1]
    info[z] = both
    i_recv = new_recv()
    push_all([(info.at[z], info.at[z], device) for device in to_z], info.at[pl.ds(0, 3)], i_recv)
    other_at = pl.multiple_of(own_ch * (1 - k), 16)
    arrived(filt.at[pl.ds(other_at, own_ch)], f_sib)

    def first_conv(r, carry):
        sums, squares = carry
        image_copy(r).wait()
        rows = feats[pl.ds(SIDE * r, SIDE)].reshape(rows_a, feats.shape[2])
        out = matmul_nt(rows, filt[...])
        z_one[pl.ds(pl.multiple_of(rows_a * r, 64), rows_a), :] = out
        counted = jnp.where((r == 0) & (k == 1), 0.0, 1.0)
        return (
            sums + counted * jnp.sum(out, axis=0, keepdims=True),
            squares + counted * jnp.sum(out * out, axis=0, keepdims=True),
        )

    zero_row = jnp.zeros((1, chip_ch), F32)
    so_far = lax.fori_loop(0, UPPER // 2, first_conv, (zero_row, zero_row))
    relay(i, 1, 0, to_x, to_y)
    relay(xn, 0, 0, to_y)
    sums, squares = lax.fori_loop(UPPER // 2, UPPER, first_conv, so_far)

    def small_sum(turn, rows):
        own = 2 * i + k
        tiles[turn, own] = rows
        at = new_recv()
        tile, all_others = tiles.at[turn, own], tiles.at[turn, pl.ds(0, 7)]
        push_all([(tile, tile, device) for device in plane], all_others, at)

        def finish():
            arrived(all_others, at)
            result = tiles[turn, 0]
            for n in range(1, 8):
                result = result + tiles[turn, n]
            return result

        return finish

    finish = small_sum(0, jnp.concatenate([sums, squares, jnp.zeros((6, 128), F32)], axis=0))
    for copy in loads[7:]:
        copy.wait()
    for r in range(head_rows):
        first, shift = divmod(classes * r, 128)
        taken = -(-(shift + classes) // 128)
        rows = w_head[first : first + taken, :]
        if taken < 9:
            rows = jnp.concatenate([rows, jnp.zeros((9 - taken, 128), F32)], axis=0)
        if shift:
            rows = pltpu.roll(rows, 128 - shift, 1)
            rows = jnp.where(lane < 128 - shift, rows[:8], rows[1:9])
        for j in range(8):
            head_flat[r : r + 1, 128 * j : 128 * j + 128] = rows[j : j + 1]
    head_lane = lax.broadcasted_iota(jnp.int32, (head_rows, 1024), 1)
    head[i, z, k] = jnp.where(head_lane < classes, head_flat[...], 0.0).astype(BF16)
    relay(xn, 0, 1, to_y)
    relay(i, 2, 0, to_x, to_y)
    relay(i, 1, 1, to_x, to_y)
    relay(xn, 1, 0, to_y)
    totals = finish()
    mean_one = totals[0:1] / count_all
    inv_one = lax.rsqrt(totals[1:2] / count_all - mean_one * mean_one + EPS)
    gain_one, bias_one = both[0:1], both[1:2]

    def first_act(r):
        at = slice(rows_a * r, rows_a * r + rows_a)
        hat = (z_one[at, :] - mean_one) * inv_one
        value, grade = silu_pair(gain_one * hat + bias_one)
        act_out[r] = value.astype(BF16).reshape(SIDE, group, chip_ch)
        counted = jnp.where(k == 1, 0.0, 1.0) if r == 0 else 1.0
        d_one[r] = (counted * hat).astype(BF16).reshape(SIDE, group, chip_ch)

    def hat_products(first, last):
        def step(n, carry):
            at = pl.ds(pl.multiple_of(256 * n, 256), 256)
            rows = feats[:, :, at].reshape(UPPER * rows_a, 256)
            m_two[:, at] = jnp.dot(hat_t[...], rows, preferred_element_type=F32)
            return carry

        lax.fori_loop(first, last, step, 0)

    def into(row, chip_id):
        return act_in.at[
            1 + row, pl.ds(1, SIDE), :, pl.ds(pl.multiple_of(chip_ch * chip_id, 128), chip_ch)
        ]

    def images_of(ref, dz):
        return ref.at[:, :, pl.ds(pl.multiple_of(per_chip * chip(dz), 16), per_chip), :]

    def images_in_row(ref, r, dz):
        return ref.at[r, :, pl.ds(pl.multiple_of(per_chip * chip(dz), 16), per_chip), :]

    def row_copies(r):
        return [
            (images_in_row(act_out, r + k, dz), into(UPPER * k + r, z), to_z[dz - 1])
            for dz in (3, 2, 1)
        ]

    def keep_row(r, n):
        return pltpu.make_async_copy(
            images_in_row(act_out, r, 0), into(h0 + r, z), local_sem.at[n]
        )

    for r in range(UPPER):
        first_act(r)
    a_recv, a_more = new_recv(), new_recv()
    common = SIDE - UPPER
    out_copies = [
        push_all(
            [copy for r in range(common) for copy in row_copies(r)],
            act_out.at[pl.ds(0, 3), :, pl.ds(0, 3 * per_chip)],
            a_recv,
        )
    ]
    more_send = next(next_send)

    def more_copy(dz):
        return pltpu.make_async_remote_copy(
            src_ref=images_in_row(act_out, common, dz),
            dst_ref=into(common, z),
            send_sem=send.at[more_send],
            recv_sem=recv.at[a_more],
            device_id=to_z[dz - 1],
            device_id_type=MESH,
        )

    more_size = act_out.at[0, :, pl.ds(0, 3 * per_chip)]
    more_wait = pltpu.make_async_remote_copy(
        src_ref=more_size,
        dst_ref=more_size,
        send_sem=send.at[more_send],
        recv_sem=recv.at[a_more],
        device_id=(i, sib),
        device_id_type=MESH,
    )

    @pl.when(k == 0)
    def _():
        for dz in (3, 2, 1):
            more_copy(dz).start()
        keep_row(common, common).start()

    kept = [keep_row(r + k, r) for r in range(common)]
    for copy in kept:
        copy.start()
    steps = feats.shape[2] // 256
    relay(i, 3, 0, to_x, to_y)
    relay(i, 2, 1, to_x, to_y)
    relay(xn, 1, 1, to_y)
    hat_t[pl.ds(0, chip_ch), :] = d_one[...].reshape(UPPER * rows_a, chip_ch).T
    place_of = lax.broadcasted_iota(jnp.int32, (16, UPPER * rows_a), 1)
    hat_t[pl.ds(chip_ch, 16), :] = jnp.where(
        place_of < jnp.where(k == 1, rows_a, 0), 0.0, 1.0
    ).astype(BF16)
    relay(yn, 2, 0, to_x)
    hat_products(0, steps // 4)
    relay(yn, 3, 0, to_x)
    relay(i, 3, 1, to_x, to_y)
    hat_products(steps // 4, steps // 2)
    relay(yn, 2, 1, to_x)
    relay(yn, 3, 1, to_x)
    hz_recv = new_recv()
    own_head, line_head = head.at[i, z, k], head.at[i, :, k]
    push_all([(own_head, own_head, device) for device in to_z], head.at[i, pl.ds(0, 3), k], hz_recv)
    hat_products(steps // 2, steps)

    for copy in kept:
        copy.wait()
    arrived(act_out.at[pl.ds(0, 3), :, pl.ds(0, 3 * per_chip)], a_recv)
    a_sib, m_sib = new_recv(), new_recv()
    mine = act_in.at[pl.ds(1 + UPPER * k, common), pl.ds(1, SIDE)]
    push(mine, mine, (i, sib), a_sib)
    m_send = next(next_send)
    middle = pltpu.make_async_remote_copy(
        src_ref=act_in.at[1 + common, pl.ds(1, SIDE)],
        dst_ref=act_in.at[1 + common, pl.ds(1, SIDE)],
        send_sem=send.at[m_send],
        recv_sem=recv.at[m_sib],
        device_id=(i, sib),
        device_id_type=MESH,
    )

    @pl.when(k == 0)
    def _():
        keep_row(common, common).wait()
        more_wait.wait_recv()
        middle.start()

    for line, dz in ((yn, 0), (yn, 1), (xn, 2), (xn, 3), (dg, 0), (dg, 1), (dg, 2), (dg, 3)):
        landed(line, dz, 0)
        landed(line, dz, 1)
    sent.append(size_wait(kern.at[pl.ds(0, block * (next(k_count) - 1))], k_send, k_recv))
    arrived(act_in.at[pl.ds(1 + UPPER * (1 - k), common), pl.ds(1, SIDE)], a_sib)

    @pl.when(k == 1)
    def _():
        middle.wait_recv()

    @pl.when(k == 0)
    def _():
        middle.wait_send()
        more_wait.wait_send()

    hx_recv, hy_recv, hxy_recv, hyx_recv = new_recv(), new_recv(), new_recv(), new_recv()
    arrived(head.at[i, pl.ds(0, 3), k], hz_recv)
    push(line_head, line_head, to_x, hx_recv)
    push(line_head, line_head, to_y, hy_recv)

    arrived(info.at[pl.ds(0, 3)], i_recv)
    slots = info[0] + info[1] + info[2] + info[3]
    gains = jnp.concatenate([info[n, 0:1] for n in range(4)], axis=1)
    biases = jnp.concatenate([info[n, 1:2] for n in range(4)], axis=1)
    spread = math.sqrt(3.0) * gains
    centre = 2.0 / 3.0 * silu_pair(biases)[0] + 1.0 / 6.0 * (
        silu_pair(biases + spread)[0] + silu_pair(biases - spread)[0]
    )
    centre = centre.astype(BF16).astype(F32)

    def tap_of(t):
        return t // 3, t % 3

    def transpose_tap(t):
        kern_t[pl.ds(pl.multiple_of(half * t, 256), half), :] = kern[
            pl.ds(pl.multiple_of(width * t, 512), width), :
        ].T

    def second_conv(h, carry):
        sums, squares = carry
        transpose_tap(h)
        rows = []
        for t in range(TAPS):
            up, left = tap_of(t)
            wide_rows = act_in[pl.ds(h + up, 2)].reshape(2 * PITCH, per_chip, width)
            rows.append(wide_rows[left : left + PITCH].reshape(rows_c, width))
        out = jnp.dot(jnp.concatenate(rows, axis=1), kern[...], preferred_element_type=F32)
        z_two[h] = out.reshape(PITCH, per_chip, half)
        real = out[: SIDE * per_chip]
        return (
            sums + jnp.sum(real, axis=0, keepdims=True),
            squares + jnp.sum(real * real, axis=0, keepdims=True),
        )

    zero_half = jnp.zeros((1, half), F32)
    sums, squares = lax.fori_loop(0, SIDE, second_conv, (zero_half, zero_half))

    def wide_sum(turn, rows):
        own, size = 4 * i + z, rows.shape[0]
        wide[turn, own, pl.ds(0, size)] = rows
        at = new_recv()
        tile = wide.at[turn, own, pl.ds(0, size)]
        all_others = wide.at[turn, pl.ds(0, 15), pl.ds(0, size)]
        push_all([(tile, tile, device) for device in same_core[::-1]], all_others, at)

        def finish():
            arrived(all_others, at)
            result = wide[turn, 0, pl.ds(0, size)]
            for n in range(1, 16):
                result = result + wide[turn, n, pl.ds(0, size)]
            return result

        return finish

    chip_weight = jnp.sum(both[3:4], axis=1, keepdims=True)
    finish = wide_sum(
        0,
        jnp.concatenate(
            [
                sums,
                squares,
                jnp.broadcast_to(chip_weight, (1, half)),
                jnp.zeros((5, half), F32),
            ],
            axis=0,
        ),
    )
    arrived(head.at[xn, :, k], hx_recv)
    half_head = head.at[xn, pl.ds(0, 2), k]
    push(half_head, half_head, to_y, hxy_recv)
    arrived(head.at[yn, :, k], hy_recv)
    half_head = head.at[yn, pl.ds(2, 2), k]
    push(half_head, half_head, to_x, hyx_recv)
    for t in range(SIDE, TAPS):
        transpose_tap(t)
    inner = act_in[pl.ds(1, SIDE + 1)].reshape((SIDE + 1) * PITCH, per_chip, width)
    inner = inner[1 : 1 + SIDE * PITCH].reshape(SIDE * rows_c, width).astype(F32)
    row = lax.broadcasted_iota(jnp.int32, (SIDE * rows_c, 1), 0)
    inner = jnp.where(lax.rem(lax.div(row, per_chip), PITCH) < SIDE, inner - centre, 0.0)
    act_t[pl.ds(0, width), :] = inner.astype(BF16).T
    column = lax.broadcasted_iota(jnp.int32, (16, SIDE * rows_c), 1)
    is_real = lax.rem(lax.div(column, per_chip), PITCH) < SIDE
    act_t[pl.ds(width, 16), :] = jnp.where(is_real, 1.0, 0.0).astype(BF16)
    d_pad[pl.ds(0, FRONT)] = jnp.zeros((FRONT, per_chip, half), BF16)
    d_pad[pl.ds(FRONT + SIDE * PITCH, FRONT)] = jnp.zeros((FRONT, per_chip, half), BF16)
    arrived(head.at[dg, pl.ds(0, 2), k], hxy_recv)
    arrived(head.at[dg, pl.ds(2, 2), k], hyx_recv)
    hd_sib = new_recv()
    theirs = head.at[pl.ds(2 * (1 - k), 2), :, k]
    push(theirs, theirs, (i, sib), hd_sib)
    totals_two = finish()
    total = totals_two[2:3, 0:1]
    mean_two = totals_two[0:1] / count_all
    inv_two = lax.rsqrt(totals_two[1:2] / count_all - mean_two * mean_two + EPS)
    norms_two = jnp.where(k == 0, norm_two[:, :half], norm_two[:, half:])
    gain_two, bias_two = norms_two[0:1], norms_two[1:2]

    def second_act(h, pooled):
        hat = (z_two[h] - mean_two) * inv_two
        z_two[h] = hat
        value, grade = silu_pair(gain_two * hat + bias_two)
        slope[h] = grade
        return pooled + jnp.sum(value[:SIDE], axis=0)

    pooled = lax.fori_loop(0, SIDE, second_act, jnp.zeros((per_chip, half), F32)) / PIX
    pooled_low = pooled.astype(BF16)

    arrived(head.at[pl.ds(2 * k, 2), :, 1 - k], hd_sib)
    head_half = head[pl.ds(2 * k, 2)].reshape(half, head.shape[4])
    logit[0] = jnp.dot(pooled_low, head_half, preferred_element_type=F32)
    at = new_recv()
    push(logit.at[0], logit.at[1], (i, sib), at)
    image_id = per_chip * z + lax.broadcasted_iota(jnp.int32, (per_chip, group), 0)
    fills = place[...] == image_id
    label = jnp.sum(jnp.where(fills, slots[2:3, :group], 0.0), axis=1, keepdims=True).astype(jnp.int32)
    weight = jnp.sum(jnp.where(fills, slots[3:4, :group], 0.0), axis=1, keepdims=True)
    share = weight / total
    arrived(logit.at[1], at)
    logits = logit[0] + logit[1]
    klass = lax.broadcasted_iota(jnp.int32, logits.shape, 1)
    inside = klass < classes
    top = jnp.max(jnp.where(inside, logits, -jnp.inf), axis=1, keepdims=True)
    expd = jnp.where(inside, jnp.exp(jnp.where(inside, logits - top, 0.0)), 0.0)
    denom = jnp.sum(expd, axis=1, keepdims=True)
    onehot = klass == label
    picked = jnp.sum(jnp.where(onehot, logits, 0.0), axis=1, keepdims=True)
    partial = jnp.sum(share * (top + jnp.log(denom) - picked), axis=0, keepdims=True)
    d_logits = (share * (expd / denom - jnp.where(onehot, 1.0, 0.0))).astype(BF16)
    d_pooled = matmul_nt(d_logits, head_half) / PIX

    def second_back(h, carry):
        sums, products = carry
        d_y = d_pooled[None] * slope[h]
        slope[h] = d_y
        d_y = d_y[:SIDE].reshape(SIDE * per_chip, half)
        hat = z_two[h][:SIDE].reshape(SIDE * per_chip, half)
        return (
            sums + jnp.sum(d_y, axis=0, keepdims=True),
            products + jnp.sum(d_y * hat, axis=0, keepdims=True),
        )

    d_bias, d_gain = lax.fori_loop(0, SIDE, second_back, (zero_half, zero_half))

    finish = wide_sum(
        1,
        jnp.concatenate(
            [d_gain, d_bias, jnp.broadcast_to(partial, (1, half)), jnp.zeros((5, half), F32)], axis=0
        ),
    )
    gh_swap = new_recv()
    gh_half[...] = matmul_tn(pooled_low, d_logits).astype(BF16).reshape(gh_half.shape)
    push(gh_half.at[:, :, 1 - k], gh.at[pl.ds(2 * k, 2)], (i, sib), gh_swap)
    gh[pl.ds(2 * k, 2)] = jnp.where(
        k == 0, gh_half[:, :, 0].astype(F32), gh_half[:, :, 1].astype(F32)
    ).astype(BF16)
    arrived(gh.at[pl.ds(2 * (1 - k), 2)], gh_swap)
    h_one, h_two, h_z = new_recv(4), new_recv(2), new_recv(4)
    for way, first in enumerate((xn, yn)):
        part = pl.ds(2 * way, 2)
        push(gh.at[dg, part], rh_one.at[way, 1], (first, c), h_one + 2 * way + 1)
        push(gh.at[first, part], rh_one.at[way, 0], (first, c), h_one + 2 * way)
    totals_back = finish()
    loss[...] = totals_back[2:3, :128]
    wide_sib[0] = totals_back
    bn_at = new_recv()
    push(wide_sib.at[0], wide_sib.at[1], (i, sib), bn_at)
    scale = gain_two * inv_two
    shift_two, lean_two = totals_back[1:2] / count_all, totals_back[0:1] / count_all

    def second_grad(h, carry):
        grad = scale * (slope[h] - shift_two - z_two[h] * lean_two)
        pixel = lax.broadcasted_iota(jnp.int32, grad.shape, 0)
        grad = jnp.where(pixel < SIDE, grad, 0.0)
        d_pad[pl.ds(FRONT + PITCH * h, PITCH)] = grad.astype(BF16)
        return carry

    lax.fori_loop(0, SIDE, second_grad, 0)

    def kernel_gradient(t, carry):
        rows = d_pad[pl.ds(FRONT + PITCH + 1 - PITCH * lax.div(t, 3) - lax.rem(t, 3), SIDE * PITCH)]
        out = jnp.dot(
            act_t[...], rows.reshape(SIDE * rows_c, half), preferred_element_type=F32
        )
        edge = out[width : width + 1]
        edge_rows[pl.ds(t, 1)] = edge
        gk[pl.ds(pl.multiple_of(width * t, 32), width), :] = out[:width].astype(BF16)
        return carry

    sent.pop(0).wait_send()
    edge_rows[...] = jnp.zeros(edge_rows.shape, F32)
    lax.fori_loop(0, TAPS, kernel_gradient, 0)
    def gk_at(line, dz):
        return gk.at[pl.ds(pl.multiple_of(chunk * (line * 4 + chip(dz)), 32), chunk)]

    ways = {1: (xn, yn), 2: (yn, xn), 3: (xn, yn), 0: (yn, xn)}
    one_at = {dz: new_recv(2) for dz in (3, 2, 1, 0)}
    two_at = {dz: new_recv() for dz in (3, 2, 1, 0)}
    z_at = new_recv(4)
    r_send = next(next_send)
    sent.append(size_wait(gk.at[pl.ds(0, 15 * chunk)], r_send, z_at))

    def start_one(dz):
        first, second = ways[dz]
        start(r_send, one_at[dz] + 1, gk_at(dg, dz), rk_one.at[dz, 1], (first, c))
        start(r_send, one_at[dz], gk_at(first, dz), rk_one.at[dz, 0], (first, c))

    def start_two(dz):
        first, second = ways[dz]
        arrived(rk_one.at[dz, 1], one_at[dz] + 1)
        into_k = gk_at(second, dz)
        into_k[...] = (into_k[...].astype(F32) + rk_one[dz, 1].astype(F32)).astype(BF16)
        start(r_send, two_at[dz], into_k, rk_two.at[dz], (second, c))

    def plane_done(dz):
        arrived(rk_one.at[dz, 0], one_at[dz])
        arrived(rk_two.at[dz], two_at[dz])
        into_k = gk_at(i, dz)
        sum_k = into_k[...].astype(F32) + rk_one[dz, 0].astype(F32) + rk_two[dz].astype(F32)
        if dz == 0:
            return sum_k
        into_k[...] = sum_k.astype(BF16)
        start(r_send, z_at + z, into_k, rk_z.at[z], to_z[dz - 1])
        return None

    start_one(3)
    start_one(2)

    def back_conv(h):
        rows = []
        for t in range(TAPS):
            up, left = tap_of(t)
            at = PITCH * h + FRONT + PITCH + 1 - PITCH * up - left
            rows.append(d_pad[pl.ds(at, PITCH)].reshape(rows_c, half))
        out = jnp.dot(jnp.concatenate(rows, axis=1), kern_t[...], preferred_element_type=F32)
        return out.reshape(PITCH, per_chip, width)[:SIDE]

    d_at, d_send_at = new_recv(), next(next_send)

    def back_theirs(r, carry):
        out = back_conv(h0_other + r)
        d_act[h0_other + r, pl.ds(0, SIDE)] = out
        d_send[r] = out.astype(BF16)
        start(d_send_at, d_at, d_send.at[r], d_recv.at[r], (i, sib))
        return carry

    def channels_of(r, dz):
        return d_recv.at[r, :, :, pl.ds(pl.multiple_of(chip_ch * chip(dz), 128), chip_ch)]

    def back_row(r, at, to):
        d_recv[r] = (d_act[h0 + r, pl.ds(0, SIDE)] + d_recv[r].astype(F32)).astype(BF16)
        for dz in (3, 2, 1):
            start(at, to, channels_of(r, dz), images_in_row(d_one, r, 0), to_z[dz - 1])

    h0_other = (SIDE - UPPER) * (1 - k)
    lax.fori_loop(0, UPPER, back_theirs, 0)
    for way, second in enumerate((yn, xn)):
        part = pl.ds(2 * way, 2)
        arrived(rh_one.at[way, 1], h_one + 2 * way + 1)
        gh[second, part] = (gh[second, part].astype(F32) + rh_one[way, 1].astype(F32)).astype(BF16)
        push(gh.at[second, part], rh_two.at[way], (second, c), h_two + way)
    b_recv, b_more = new_recv(), new_recv()
    b_send, b_more_send = next(next_send), next(next_send)

    d_copy = size_wait(d_send, d_send_at, d_at)
    sent.append(d_copy)
    d_act[UPPER * k, pl.ds(0, SIDE)] = back_conv(UPPER * k)
    d_copy.wait_recv()

    def keep_back(r, n):
        return pltpu.make_async_copy(
            channels_of(r, 0), images_in_row(d_one, r, 0), local_sem.at[n]
        )

    @pl.when(k == 0)
    def _():
        back_row(common, b_more_send, b_more)
        keep_back(common, common).start()

    @pl.when(k == 1)
    def _():
        d_one[0] = jnp.zeros(d_one.shape[1:], BF16)

    for r in range(common):
        if r:
            d_act[UPPER * k + r, pl.ds(0, SIDE)] = back_conv(UPPER * k + r)
        back_row(r + k, b_send, b_recv)
    kept = [keep_back(r + k, r) for r in range(common)]
    for copy in kept:
        copy.start()
    back_copy = size_wait(d_one.at[pl.ds(0, 3), :, pl.ds(0, 3 * per_chip)], b_send, b_recv)
    back_more = size_wait(d_one.at[0, :, pl.ds(0, 3 * per_chip)], b_more_send, b_more)
    sent.append(back_copy)

    for way in (0, 1):
        part = pl.ds(2 * way, 2)
        arrived(rh_one.at[way, 0], h_one + 2 * way)
        arrived(rh_two.at[way], h_two + way)
        sum_h = gh[i, part].astype(F32) + rh_one[way, 0].astype(F32) + rh_two[way].astype(F32)
        h_sum[part] = sum_h
        gh[i, part] = sum_h.astype(BF16)
    for dz in (3, 2, 1):
        push(gh.at[i, chip(dz)], rh_z.at[z], (i, zdev(dz)), h_z + z)

    start_two(3)
    start_two(2)
    start_one(1)
    start_one(0)
    for copy in kept:
        copy.wait()
    back_copy.wait_recv()

    @pl.when(k == 0)
    def _():
        keep_back(common, common).wait()
        back_more.wait_recv()
        back_more.wait_send()


    def first_back(r, carry):
        sums, products = carry
        at = pl.ds(pl.multiple_of(rows_a * r, 64), rows_a)
        hat = (z_one[at, :] - mean_one) * inv_one
        z_one[at, :] = hat
        _, grade = silu_pair(gain_one * hat + bias_one)
        d_y = d_one[r].reshape(rows_a, chip_ch).astype(F32) * grade
        counted = jnp.where((r == 0) & (k == 1), 0.0, 1.0)
        return (
            sums + counted * jnp.sum(d_y, axis=0, keepdims=True),
            products + counted * jnp.sum(d_y * hat, axis=0, keepdims=True),
        )

    d_bias, d_gain = lax.fori_loop(0, UPPER, first_back, (zero_row, zero_row))
    finish = small_sum(
        1, jnp.concatenate([d_gain, d_bias, jnp.zeros((6, 128), F32)], axis=0)
    )
    finish_edges = wide_sum(2, edge_rows[...])
    start_two(1)
    start_two(0)
    plane_done(3)
    plane_done(2)
    scale_one = gain_one * inv_one
    near_count = count_all / 8
    shift_near, lean_near = d_bias / near_count, d_gain / near_count

    def first_grad(r, carry):
        at = pl.ds(pl.multiple_of(rows_a * r, 64), rows_a)
        hat = z_one[at, :]
        _, grade = silu_pair(gain_one * hat + bias_one)
        d_y = d_one[r].reshape(rows_a, chip_ch).astype(F32) * grade
        counted = jnp.where((r == 0) & (k == 1), 0.0, 1.0)
        grad = (counted * scale_one) * (d_y - shift_near - hat * lean_near)
        act_out[r] = grad.astype(BF16).reshape(SIDE, group, chip_ch)
        return carry

    for copy in out_copies:
        copy.wait_send()
    sent[:] = [copy for copy in sent if all(copy is not done for done in out_copies)]
    lax.fori_loop(0, UPPER, first_grad, 0)

    grad_t[...] = act_out[...].reshape(UPPER * rows_a, chip_ch).T

    def first_weights(n, carry):
        at = pl.ds(pl.multiple_of(256 * n, 256), 256)
        rows = feats[:, :, at].reshape(UPPER * rows_a, 256)
        g_acc[:, at] = jnp.dot(grad_t[...], rows, preferred_element_type=F32)
        return carry

    part, columns = own_ch // 2, feats.shape[2] // 2
    upper, lower = pl.ds(0, part), pl.ds(part, part)
    sides = [slice(0, columns), slice(columns, 2 * columns)]
    g_at, first_at, second_at = new_recv(2), new_recv(4), new_recv(4)
    for n, side in enumerate(sides):
        lax.fori_loop(columns // 256 * n, columns // 256 * (n + 1), first_weights, 0)
        if n == 0:
            totals_one = finish()
            g_bn_one[...] = jnp.where(k == 0, totals_one[0:2, :own_ch], totals_one[0:2, own_ch:])
            shift_rest = scale_one * (totals_one[1:2] / count_all - shift_near)
            lean_rest = scale_one * (totals_one[0:1] / count_all - lean_near)
            rest = jnp.concatenate([shift_rest, lean_rest, jnp.zeros((6, chip_ch), F32)], axis=0).T
        g_all = (
            g_acc[:, side]
            - rest[:, 0:1] * m_two[chip_ch : chip_ch + 1, side]
            - rest[:, 1:2] * m_two[:chip_ch, side]
        )
        low, high = g_all[:own_ch], g_all[own_ch:]
        go_send[n] = jnp.where(k == 0, high, low).astype(BF16)
        push(go_send.at[n], go_recv.at[n], (i, sib), g_at + n)
        g_one[:, side] = jnp.where(k == 0, low, high)
    for n, side in enumerate(sides):
        arrived(go_recv.at[n], g_at + n)
        ga_send[n] = (g_one[:, side] + go_recv[n].astype(F32)).astype(BF16)
        push(ga_send.at[n, upper], ga_recv.at[n, upper], to_x, first_at + 2 * n)
        push(ga_send.at[n, lower], ga_recv.at[n, lower], to_y, first_at + 2 * n + 1)
    for n in (0, 1):
        arrived(ga_recv.at[n, upper], first_at + 2 * n)
        arrived(ga_recv.at[n, lower], first_at + 2 * n + 1)
        ga_send[2 + n] = (ga_send[n].astype(F32) + ga_recv[n].astype(F32)).astype(BF16)
        push(ga_send.at[2 + n, upper], ga_recv.at[2 + n, upper], to_y, second_at + 2 * n)
        push(ga_send.at[2 + n, lower], ga_recv.at[2 + n, lower], to_x, second_at + 2 * n + 1)

    edges = finish_edges()
    plane_done(1)
    sum_k = plane_done(0)

    for n, side in enumerate(sides):
        arrived(ga_recv.at[2 + n, upper], second_at + 2 * n)
        arrived(ga_recv.at[2 + n, lower], second_at + 2 * n + 1)
        g_one[:, side] = ga_send[2 + n].astype(F32) + ga_recv[2 + n].astype(F32)

    row_at = chunk * (i * 4 + z)
    tap = lax.div(row_at, width)
    edge_rows[...] = edges
    for step in range(2):
        ranked[pl.ds(width * step, width), :] = rank_one(
            centre, edge_rows[pl.ds(lax.rem(tap + step, TAPS), 1)]
        )
    offset = pl.multiple_of(row_at - width * tap, 32)
    sum_k = sum_k + ranked[pl.ds(offset, chunk), :]
    sum_h = h_sum[z]
    for dz in (1, 2, 3):
        arrived(rk_z.at[chip(dz)], z_at + chip(dz))
        arrived(rh_z.at[chip(dz)], h_z + chip(dz))
        sum_k = sum_k + rk_z[chip(dz)].astype(F32)
        sum_h = sum_h + rh_z[chip(dz)].astype(F32)
    head_flat[...] = sum_h
    g_head[...] = jnp.zeros(g_head.shape, F32)
    for r in range(head_rows):
        first, shift = divmod(classes * r, 128)
        rows = jnp.concatenate(
            [head_flat[r : r + 1, 128 * j : 128 * j + 128] for j in range(8)], axis=0
        )
        if shift:
            rows = pltpu.roll(rows, shift, 1)
        count = min(8, g_head.shape[0] - first)
        g_head[first : first + count, :] += jnp.where(lane >= shift, rows, 0.0)[:count]
        count = min(8, g_head.shape[0] - first - 1)
        if shift:
            g_head[first + 1 : first + 1 + count, :] += jnp.where(lane < shift, rows, 0.0)[:count]
    last_send[...] = sum_k
    l_at = new_recv()
    theirs = last_send.at[pl.ds(pl.multiple_of(block * (1 - k), 16), block)]
    push(theirs, last_recv, (i, sib), l_at)
    mine = last_send[pl.ds(pl.multiple_of(block * k, 16), block), :]
    arrived(last_recv, l_at)
    other = last_recv[...]
    for j in range(4):
        lanes = slice(128 * (j % 2), 128 * (j % 2) + 128)
        g_two[pl.ds(j, block, stride=4), :] = jnp.where(
            k == j // 2, mine[:, lanes], other[:, lanes]
        )

    arrived(wide_sib.at[1], bn_at)
    own_bn, other_bn = wide_sib[0], wide_sib[1]
    g_bn_two[...] = jnp.where(
        k == 0,
        jnp.concatenate([own_bn[0:2], other_bn[0:2]], axis=1),
        jnp.concatenate([other_bn[0:2], own_bn[0:2]], axis=1),
    )
    for copy in sent:
        copy.wait_send()


def update_kernel(rates, *refs):
    take, give = refs[:24], refs[24:]
    rate_one, rate_bn_one, rate_two, rate_bn_two, rate_head = rates
    w, g, m, v, mask, rank = (r[...] for r in take[:6])
    results = sparse_update(w, g * mask.astype(F32), m, v, mask, rank, rate_one)
    for ref, value in zip(give[:5], results):
        ref[...] = value
    w, g, m, v, mask, rank = (r[...] for r in take[6:12])
    results = sparse_update(w, g * mask.astype(F32), m, v, mask, rank, rate_two)
    for ref, value in zip(give[5:10], results):
        ref[...] = value

    @pl.when(pl.program_id(0) == 0)
    def _():
        for n, rate in enumerate((rate_bn_one, rate_bn_two, rate_head)):
            w, g, m, v = (r[...] for r in take[12 + 4 * n : 16 + 4 * n])
            results = dense_update(w, g, m, v, rate)
            for ref, value in zip(give[10 + 3 * n : 13 + 3 * n], results):
                ref[...] = value
        give[19][...] = results[0].astype(BF16)


def fast_shards(
    images_in, labels, loss_wt, placement,
    w_one, mom_one, avg_one, mask_one, rank_one_in, first_norm_params, mom_bn_one, avg_bn_one,
    w_two, mom_two, avg_two, mask_two, rank_two, second_norm_params, mom_bn_two, avg_bn_two,
    w_head, mom_head, avg_head,
):
    n_img, n_ch = lax.axis_size("img"), lax.axis_size("ch")
    group, cin = images_in.shape[0], images_in.shape[2]
    per_core = labels.shape[0]
    per_chip = 2 * per_core
    width = second_norm_params.shape[1]
    half = width // 2
    own_ch = w_one.shape[1]
    chip_ch = 2 * own_ch
    classes = w_head.shape[0] * n_img * n_ch // width
    images = per_core * n_img * n_ch
    head_rows = w_head.shape[0] // classes
    lanes = -(-classes // 512) * 512
    block = w_two.shape[0] // width
    chunk = 2 * block
    flat = (w_two.shape[0] // 128, 128)
    top = [a.reshape(-1, 128) for a in (w_head, mom_head, avg_head)]
    one = [a.T for a in (w_one, mom_one, avg_one, mask_one, rank_one_in)]
    two = [a.reshape(flat) for a in (w_two, mom_two, avg_two, mask_two, rank_two)]
    vmem = pl.BlockSpec(memory_space=pltpu.VMEM)
    hbm = pl.BlockSpec(memory_space=pltpu.HBM)
    v = pltpu.VMEM
    shape = jax.ShapeDtypeStruct
    g_one, g_two, g_head, g_bn_one, g_bn_two, loss = pl.pallas_call(
        functools.partial(step_kernel, (group, per_chip, classes, images)),
        out_shape=(
            shape((own_ch, cin), F32),
            shape(flat, F32),
            shape(top[0].shape, F32),
            shape((2, own_ch), F32),
            shape((2, width), F32),
            shape((1, 128), F32),
        ),
        in_specs=[hbm] * 11,
        out_specs=[vmem] * 6,
        scratch_shapes=[
            v((own_ch, cin), F32),
            v((own_ch, cin), jnp.int32),
            v(flat, F32),
            v(flat, jnp.int32),
            v(top[0].shape, F32),
            v((2, own_ch), F32),
            v((2, width), F32),
            v((1, group), jnp.int32),
            pltpu.SMEM((per_core,), jnp.int32),
            pltpu.SMEM((per_core,), jnp.int32),
            v((UPPER * SIDE, group, cin), BF16),
            v((chip_ch, cin), BF16),
            v((TAPS * width, half), BF16),
            v((4, 4, 2, head_rows, lanes), BF16),
            v((SIDE + 3, PITCH, per_chip, width), BF16),
            v((UPPER, SIDE, group, chip_ch), BF16),
            v((UPPER * SIDE * group, chip_ch), F32),
            v((SIDE, PITCH, per_chip, half), F32),
            v((SIDE, PITCH, per_chip, half), F32),
            v((2 * FRONT + SIDE * PITCH, per_chip, half), BF16),
            v((width + 16, SIDE * PITCH * per_chip), BF16),
            v((SIDE, PITCH, per_chip, width), F32),
            v((UPPER, SIDE, per_chip, width), BF16),
            v((UPPER, SIDE, per_chip, width), BF16),
            v((UPPER, SIDE, group, chip_ch), BF16),
            v((2, 8, 128), F32),
            v((4, 8, 128), F32),
            v((2, 8, 8, 128), F32),
            v((3, 16, 16, half), F32),
            v((2, 8, half), F32),
            v((2, per_chip, lanes), F32),
            v((2, 4, 2, head_rows, lanes), BF16),
            v((TAPS * width, half), BF16),
            v((4, 4, head_rows, lanes), BF16),
            v((4, 2, chunk, half), BF16),
            v((2, 2, 2, head_rows, lanes), BF16),
            v((4, chunk, half), BF16),
            v((2, 2, head_rows, lanes), BF16),
            v((4, chunk, half), BF16),
            v((4, head_rows, lanes), BF16),
            v((4, head_rows, lanes), F32),
            v((head_rows, lanes), F32),
            v((chunk, half), F32),
            v((block, half), F32),
            v((16, half), F32),
            v((2 * width, half), F32),
            v((chip_ch, UPPER * SIDE * group), BF16),
            v((chip_ch, cin), F32),
            v((2, own_ch, cin // 2), BF16),
            v((2, own_ch, cin // 2), BF16),
            v((4, own_ch, cin // 2), BF16),
            v((4, own_ch, cin // 2), BF16),
            v((TAPS * half, width), BF16),
            v((chip_ch + 16, UPPER * SIDE * group), BF16),
            v((chip_ch + 16, cin), F32),
            pltpu.SemaphoreType.DMA((10,)),
            pltpu.SemaphoreType.DMA((UPPER,)),
            pltpu.SemaphoreType.DMA((UPPER + 1,)),
            pltpu.SemaphoreType.DMA((SENDS,)),
            pltpu.SemaphoreType.DMA((RECEIVES,)),
        ],
        compiler_params=pltpu.CompilerParams(
            collective_id=0, has_side_effects=True, vmem_limit_bytes=56 << 20
        ),
        name="step",
    )(
        images_in.transpose(1, 0, 2),
        placement,
        labels,
        loss_wt,
        one[0],
        one[3],
        first_norm_params,
        two[0],
        two[3],
        top[0],
        second_norm_params,
    )
    root = math.sqrt(images)
    steps = 2
    one_spec = pl.BlockSpec((own_ch // steps, cin), lambda n: (n, 0))
    two_spec = pl.BlockSpec((flat[0] // steps, 128), lambda n: (n, 0))
    bno_spec = pl.BlockSpec((2, own_ch), lambda n: (0, 0))
    bnt_spec = pl.BlockSpec((2, width), lambda n: (0, 0))
    top_spec = pl.BlockSpec(top[0].shape, lambda n: (0, 0))
    f_one, f_two = shape(one[0].shape, F32), shape(flat, F32)
    new = pl.pallas_call(
        functools.partial(update_kernel, (1.3 * root, 8.0 * root, 0.25 * root, root, 40.0)),
        grid=(steps,),
        in_specs=[one_spec] * 6 + [two_spec] * 6 + [bno_spec] * 4 + [bnt_spec] * 4 + [top_spec] * 4,
        out_specs=[one_spec] * 5 + [two_spec] * 5 + [bno_spec] * 3 + [bnt_spec] * 3 + [top_spec] * 4,
        out_shape=[f_one] * 3 + [shape(f_one.shape, jnp.int32), shape(f_one.shape, BF16)]
        + [f_two] * 3 + [shape(flat, jnp.int32), shape(flat, BF16)]
        + [shape((2, own_ch), F32)] * 3 + [shape((2, width), F32)] * 3
        + [shape(top[0].shape, F32)] * 3 + [shape(top[0].shape, BF16)],
        compiler_params=pltpu.CompilerParams(vmem_limit_bytes=56 << 20),
        name="update",
    )(
        one[0], g_one, one[1], one[2], one[3], one[4],
        two[0], g_two, two[1], two[2], two[3], two[4],
        first_norm_params, g_bn_one, mom_bn_one, avg_bn_one,
        second_norm_params, g_bn_two, mom_bn_two, avg_bn_two,
        top[0], g_head, top[1], top[2],
    )
    return (
        loss[0, 0],
        *(a.T for a in new[:5]),
        *new[10:13],
        *(a.reshape(-1) for a in new[5:10]),
        *new[13:16],
        *(a.reshape(-1) for a in new[16:20]),
    )


def solution(mesh):
    in_specs = (
        P("img", None, None),
        P(("img", "ch")),
        P(("img", "ch")),
        P("img", None),
        P(None, "ch"),
        P(None, "ch"),
        P(None, "ch"),
        P(None, "ch"),
        P(None, "ch"),
        P(None, "ch"),
        P(None, "ch"),
        P(None, "ch"),
        P(("img", "ch")),
        P(("img", "ch")),
        P(("img", "ch")),
        P(("img", "ch")),
        P(("img", "ch")),
        P(),
        P(),
        P(),
        P(("img", "ch")),
        P(("img", "ch")),
        P(("img", "ch")),
    )
    out_specs = (
        P(),
        P(None, "ch"),
        P(None, "ch"),
        P(None, "ch"),
        P(None, "ch"),
        P(None, "ch"),
        P(None, "ch"),
        P(None, "ch"),
        P(None, "ch"),
        P(("img", "ch")),
        P(("img", "ch")),
        P(("img", "ch")),
        P(("img", "ch")),
        P(("img", "ch")),
        P(),
        P(),
        P(),
        P(("img", "ch")),
        P(("img", "ch")),
        P(("img", "ch")),
        P(("img", "ch")),
    )
    fast = mesh.shape["img"] == 4 and mesh.shape["ch"] == 8
    return jax.shard_map(fast_shards if fast else shards, mesh=mesh, in_specs=in_specs, out_specs=out_specs, check_vma=False)
```

```python
import functools
import itertools
import math

import jax
import jax.numpy as jnp
from jax import lax
from jax.experimental import pallas as pl
from jax.experimental.pallas import tpu as pltpu
from jax.sharding import PartitionSpec as P

SIDE = 7
PIX = 49
DROP = 10
GROW = 10


EPS = 1e-05
MOMENTUM = 0.5


def advance(weight, grad, velocity, rate):
    velocity = MOMENTUM * velocity + grad
    return (weight - rate * (grad + MOMENTUM * velocity), velocity)


def dense_update(weight, grad, velocity, average, rate):
    moved, velocity = advance(weight, grad, velocity, rate)
    return (moved, velocity, 0.5 * average + 0.5 * moved)


def sparse_update(weight, grad, velocity, average, mask, rank, rate):
    moved, velocity = advance(weight, grad, velocity, rate)
    kept = (mask == 1) & (rank >= DROP)
    grown = (mask == 0) & (rank < GROW)
    new_mask = jnp.where(kept | grown, 1, 0).astype(jnp.int32)
    weight = jnp.where(kept, moved, 0.0)
    velocity = jnp.where(kept, velocity, 0.0)
    average = 0.5 * average + 0.5 * weight
    return (weight, velocity, average, new_mask, weight.astype(jnp.bfloat16))


def silu_slope(value):
    sigma = jax.nn.sigmoid(value)
    return sigma * (1.0 + value * (1.0 - sigma))


def apply_batch_norm(z, sums, squares, element_count):
    mean = sums / element_count
    inverse_deviation = lax.rsqrt(squares / element_count - mean * mean + EPS)
    return ((z - mean) * inverse_deviation, inverse_deviation)


def batch_norm_backward(
    norm_gain,
    inverse_deviation,
    output_gradient,
    standardized_input,
    bias_gradient_sum,
    gain_gradient_sum,
    element_count,
):
    return (
        norm_gain
        * inverse_deviation
        * (
            output_gradient
            - bias_gradient_sum / element_count
            - standardized_input * gain_gradient_sum / element_count
        )
    )


def contract_rows(left, right):
    return jnp.einsum("pk,pc->kc", left, right, preferred_element_type=jnp.float32)


def shards(
    images_in,
    labels,
    loss_wt,
    placement,
    w_one,
    mom_one,
    avg_one,
    mask_one,
    rank_one,
    first_norm_params,
    mom_bn_one,
    avg_bn_one,
    w_two,
    mom_two,
    avg_two,
    mask_two,
    rank_two,
    second_norm_params,
    mom_bn_two,
    avg_bn_two,
    w_head,
    mom_head,
    avg_head,
):
    n_img = lax.axis_size("img")
    n_ch = lax.axis_size("ch")
    group = images_in.shape[0]
    element_count = labels.shape[0]
    width = second_norm_params.shape[1]
    classes = w_head.shape[0] * n_img * n_ch // width
    images = element_count * n_img * n_ch
    slot_info = jnp.stack([labels.astype(jnp.float32), loss_wt.astype(jnp.float32)])
    slot_info = lax.all_gather(slot_info, "ch", axis=1, tiled=True)
    own = lax.axis_index("ch") * element_count + jnp.arange(element_count, dtype=jnp.int32)
    fills = placement[0][None, :] == own[:, None]
    labels_f, weights = jnp.sum(jnp.where(fills[None], slot_info[:, None, :], 0.0), axis=2)
    labels = labels_f.astype(jnp.int32)
    kernel_part = (w_two * mask_two.astype(jnp.float32)).astype(jnp.bfloat16)
    kernel = lax.all_gather(kernel_part, ("img", "ch"), axis=0, tiled=True)
    head = lax.all_gather(w_head.astype(jnp.bfloat16), ("img", "ch"), axis=0, tiled=True)
    kernel = kernel.reshape(9 * width, width)
    head = head.reshape(width, classes)
    rows = images_in.transpose(1, 0, 2).reshape(PIX * group, images_in.shape[2])
    filt_one = (w_one * mask_one.astype(jnp.float32)).astype(jnp.bfloat16)
    first_conv_output = jnp.dot(rows, filt_one, preferred_element_type=jnp.float32)
    first_feature_sum, first_squares_sum, total = lax.psum(
        (
            jnp.sum(first_conv_output, axis=0),
            jnp.sum(first_conv_output * first_conv_output, axis=0),
            jnp.sum(slot_info[1]),
        ),
        "img",
    )
    first_element_count = group * PIX * n_img
    first_standardized_input, first_inverse_deviation = apply_batch_norm(
        first_conv_output, first_feature_sum, first_squares_sum, first_element_count
    )
    first_norm_output = first_norm_params[0] * first_standardized_input + first_norm_params[1]
    act = jax.nn.silu(first_norm_output).astype(jnp.bfloat16).reshape(PIX, group, -1)
    act_in = lax.all_to_all(act, "ch", split_axis=1, concat_axis=2, tiled=True)
    padded = jnp.pad(
        act_in.reshape(SIDE, SIDE, element_count, width), ((1, 1), (1, 1), (0, 0), (0, 0))
    )
    patches = jnp.concatenate(
        [
            padded[tap // 3 : tap // 3 + SIDE, tap % 3 : tap % 3 + SIDE].reshape(
                PIX * element_count, width
            )
            for tap in range(9)
        ],
        axis=1,
    )
    second_conv_output = jnp.dot(patches, kernel, preferred_element_type=jnp.float32)
    second_feature_sum, second_squares_sum = lax.psum(
        (
            jnp.sum(second_conv_output, axis=0),
            jnp.sum(second_conv_output * second_conv_output, axis=0),
        ),
        ("img", "ch"),
    )
    second_element_count = images * PIX
    second_standardized_input, second_inverse_deviation = apply_batch_norm(
        second_conv_output, second_feature_sum, second_squares_sum, second_element_count
    )
    second_norm_output = second_norm_params[0] * second_standardized_input + second_norm_params[1]
    pooled = jnp.mean(jax.nn.silu(second_norm_output).reshape(PIX, element_count, width), axis=0)
    pooled_low = pooled.astype(jnp.bfloat16)
    logits = jnp.dot(pooled_low, head, preferred_element_type=jnp.float32)
    top = jnp.max(logits, axis=1, keepdims=True)
    expd = jnp.exp(logits - top)
    denom = jnp.sum(expd, axis=1, keepdims=True)
    lse = top[:, 0] + jnp.log(denom[:, 0])
    onehot = labels[:, None] == jnp.arange(classes, dtype=jnp.int32)[None, :]
    picked = jnp.sum(jnp.where(onehot, logits, 0.0), axis=1)
    share = weights / total
    partial_loss_value = jnp.sum(share * (lse - picked))
    d_logits = (share[:, None] * (expd / denom - onehot.astype(jnp.float32))).astype(jnp.bfloat16)
    g_head = contract_rows(pooled_low, d_logits)
    d_pooled = jnp.einsum("ic,kc->ik", d_logits, head, preferred_element_type=jnp.float32)
    d_act = jnp.broadcast_to(d_pooled[None] / PIX, (PIX, element_count, width)).reshape(
        PIX * element_count, width
    )
    second_output_gradient = d_act * silu_slope(second_norm_output)
    second_shift_bias, second_norm_gain, loss = lax.psum(
        (
            jnp.sum(second_output_gradient, axis=0),
            jnp.sum(second_output_gradient * second_standardized_input, axis=0),
            partial_loss_value,
        ),
        ("img", "ch"),
    )
    second_preact_gradient = batch_norm_backward(
        second_norm_params[0],
        second_inverse_deviation,
        second_output_gradient,
        second_standardized_input,
        second_shift_bias,
        second_norm_gain,
        second_element_count,
    ).astype(jnp.bfloat16)
    d_patches = jnp.einsum(
        "pc,kc->pk", second_preact_gradient, kernel, preferred_element_type=jnp.float32
    )
    d_pad = 0.0
    for tap in range(9):
        piece = d_patches[:, tap * width : (tap + 1) * width].reshape(
            SIDE, SIDE, element_count, width
        )
        up, left = tap // 3, tap % 3
        d_pad = d_pad + jnp.pad(piece, ((up, 2 - up), (left, 2 - left), (0, 0), (0, 0)))
    d_act_in = d_pad[1:-1, 1:-1].astype(jnp.bfloat16).reshape(PIX, element_count, width)
    d_act_one = lax.all_to_all(d_act_in, "ch", split_axis=2, concat_axis=1, tiled=True)
    g_kernel = contract_rows(patches, second_preact_gradient)
    d_act_one = d_act_one.reshape(PIX * group, -1).astype(jnp.float32)
    first_output_gradient = d_act_one * silu_slope(first_norm_output)
    first_shift_bias, first_norm_gain = lax.psum(
        (
            jnp.sum(first_output_gradient, axis=0),
            jnp.sum(first_output_gradient * first_standardized_input, axis=0),
        ),
        "img",
    )
    first_preact_gradient = batch_norm_backward(
        first_norm_params[0],
        first_inverse_deviation,
        first_output_gradient,
        first_standardized_input,
        first_shift_bias,
        first_norm_gain,
        first_element_count,
    ).astype(jnp.bfloat16)
    g_filt = lax.psum(
        contract_rows(rows, first_preact_gradient).astype(jnp.bfloat16), "img"
    ).astype(jnp.float32)
    g_one = g_filt * mask_one.astype(jnp.float32)
    part_two = lax.psum_scatter(
        g_kernel.reshape(-1), ("img", "ch"), tiled=True
    )
    part_head = lax.psum_scatter(
        g_head.reshape(-1), ("img", "ch"), tiled=True
    )
    g_two = part_two * mask_two.astype(jnp.float32)
    root = math.sqrt(images)
    one = sparse_update(w_one, g_one, mom_one, avg_one, mask_one, rank_one, 1.3 * root)
    bno = dense_update(
        first_norm_params,
        jnp.stack([first_norm_gain, first_shift_bias]),
        mom_bn_one,
        avg_bn_one,
        8.0 * root,
    )
    two = sparse_update(w_two, g_two, mom_two, avg_two, mask_two, rank_two, 0.25 * root)
    bnt = dense_update(
        second_norm_params,
        jnp.stack([second_norm_gain, second_shift_bias]),
        mom_bn_two,
        avg_bn_two,
        root,
    )
    top_head = dense_update(w_head, part_head, mom_head, avg_head, 40.0)
    return (
        loss,
        one[0],
        one[1],
        one[2],
        one[3],
        one[4],
        bno[0],
        bno[1],
        bno[2],
        two[0],
        two[1],
        two[2],
        two[3],
        two[4],
        bnt[0],
        bnt[1],
        bnt[2],
        top_head[0],
        top_head[1],
        top_head[2],
        top_head[0].astype(jnp.bfloat16),
    )


F32, BF16 = jnp.float32, jnp.bfloat16
MESH = pl.DeviceIdType.MESH
TAPS = 9
UPPER = (SIDE + 1) // 2
PITCH = SIDE + 1
FRONT = 2 * PITCH
SENDS, RECEIVES = 48, 102


def silu_pair(value):
    sigma = 1.0 / (1.0 + jnp.exp(-value))
    return value * sigma, sigma * (1.0 + value * (1.0 - sigma))


def matmul_nt(left, right):
    return lax.dot_general(left, right, (((1,), (1,)), ((), ())), preferred_element_type=F32)


def matmul_tn(left, right):
    return lax.dot_general(left, right, (((0,), (0,)), ((), ())), preferred_element_type=F32)


def rank_one(row, other):
    first = other.astype(BF16)
    rest = other - first.astype(F32)
    second = rest.astype(BF16)
    third = (rest - second.astype(F32)).astype(BF16)
    place = lax.broadcasted_iota(jnp.int32, (16, other.shape[1]), 0)
    parts = jnp.where(place == 0, first.astype(F32), 0.0)
    parts = jnp.where(place == 1, second.astype(F32), parts)
    parts = jnp.where(place == 2, third.astype(F32), parts)
    rows = jnp.broadcast_to(row, (16, row.shape[1])).astype(BF16)
    return matmul_tn(rows, parts.astype(BF16))


def step_kernel(
    sizes,
    images,
    place_in,
    labels_in,
    loss_wt_in,
    w_one_in,
    mask_one_in,
    norm_one_in,
    w_two_in,
    mask_two_in,
    w_head_in,
    norm_two_in,
    g_one,
    g_two,
    g_head,
    g_bn_one,
    g_bn_two,
    loss,
    w_one,
    mask_one,
    w_two,
    mask_two,
    w_head,
    norm_one,
    norm_two,
    place,
    labels,
    loss_wt,
    feats,
    filt,
    kern,
    head,
    act_in,
    act_out,
    z_one,
    z_two,
    slope,
    d_pad,
    act_t,
    d_act,
    d_send,
    d_recv,
    d_one,
    early,
    info,
    tiles,
    wide,
    wide_sib,
    logit,
    gh_half,
    gk,
    gh,
    rk_one,
    rh_one,
    rk_two,
    rh_two,
    rk_z,
    rh_z,
    h_sum,
    head_flat,
    last_send,
    last_recv,
    edge_rows,
    ranked,
    grad_t,
    g_acc,
    go_send,
    go_recv,
    ga_send,
    ga_recv,
    kern_t,
    hat_t,
    m_two,
    edge_plane,
    edge_z,
    load_sem,
    image_sem,
    local_sem,
    send,
    recv,
):
    group, per_chip, classes, images_in_all = sizes
    width = norm_two.shape[1]
    half = width // 2
    own_ch = w_one.shape[0]
    chip_ch = 2 * own_ch
    block = w_two.shape[0] * 128 // width
    chunk = 2 * block
    head_rows = head.shape[3]
    rows_a = SIDE * group
    rows_c = PITCH * per_chip
    count_all = float(images_in_all * PIX)

    i, c = lax.axis_index("img"), lax.axis_index("ch")
    z, k = lax.div(c, 2), lax.rem(c, 2)
    sib = c + 1 - 2 * k
    xn, yn, dg = i + 1 - 2 * lax.rem(i, 2), lax.rem(i + 2, 4), 3 - i
    lines = (xn, yn, dg)
    near = (z, z + 1 - 2 * lax.rem(z, 2), 2 - lax.div(z, 2), 3 - 3 * lax.div(z, 2))
    h0 = (SIDE - UPPER) * k

    def chip(dz):
        return near[dz]

    def zdev(dz):
        return 2 * chip(dz) + k

    next_send, next_recv = itertools.count(), itertools.count()
    sent = []

    def new_recv(n=1):
        first = next(next_recv)
        for _ in range(n - 1):
            next(next_recv)
        return first

    def push(src, dst, device, to):
        copy = pltpu.make_async_remote_copy(
            src_ref=src,
            dst_ref=dst,
            send_sem=send.at[next(next_send)],
            recv_sem=recv.at[to],
            device_id=device,
            device_id_type=MESH,
        )
        copy.start()
        sent.append(copy)
        return copy

    def push_all(copies, size_of, to):
        at = next(next_send)
        for src, dst, device in copies:
            pltpu.make_async_remote_copy(
                src_ref=src,
                dst_ref=dst,
                send_sem=send.at[at],
                recv_sem=recv.at[to],
                device_id=device,
                device_id_type=MESH,
            ).start()
        group_copy = pltpu.make_async_remote_copy(
            src_ref=size_of,
            dst_ref=size_of,
            send_sem=send.at[at],
            recv_sem=recv.at[to],
            device_id=(i, sib),
            device_id_type=MESH,
        )
        sent.append(group_copy)
        return group_copy

    def start(at, to, src, dst, device):
        pltpu.make_async_remote_copy(
            src_ref=src,
            dst_ref=dst,
            send_sem=send.at[at],
            recv_sem=recv.at[to],
            device_id=device,
            device_id_type=MESH,
        ).start()

    def size_wait(ref, at, to):
        return pltpu.make_async_remote_copy(
            src_ref=ref,
            dst_ref=ref,
            send_sem=send.at[at],
            recv_sem=recv.at[to],
            device_id=(i, sib),
            device_id_type=MESH,
        )

    def arrived(dst, at):
        pltpu.make_async_remote_copy(
            src_ref=dst,
            dst_ref=dst,
            send_sem=send.at[0],
            recv_sem=recv.at[at],
            device_id=(i, sib),
            device_id_type=MESH,
        ).wait_recv()

    def image_copy(r):
        return pltpu.make_async_copy(
            images.at[pl.ds(SIDE * (h0 + r), SIDE)], feats.at[pl.ds(SIDE * r, SIDE)], image_sem.at[r]
        )

    barrier = pltpu.get_barrier_semaphore()
    same_core = [(o, zdev(dz)) for o in (i, *lines) for dz in (0, 1, 2, 3)][1:]
    plane = [(i, sib)] + [(o, d) for o in lines for d in (c, sib)]
    others = plane + same_core[:3]
    for device in others:
        pl.semaphore_signal(barrier, inc=1, device_id=device, device_id_type=MESH)
    loads = [
        pltpu.make_async_copy(src, dst, load_sem.at[n])
        for n, (src, dst) in enumerate(
            (
                (w_two_in, w_two),
                (mask_two_in, mask_two),
                (w_one_in, w_one),
                (mask_one_in, mask_one),
                (norm_one_in, norm_one),
                (labels_in, labels),
                (loss_wt_in, loss_wt),
                (w_head_in, w_head),
                (norm_two_in, norm_two),
                (place_in, place),
            )
        )
    ]
    for copy in loads:
        copy.start()
    for r in range(UPPER):
        image_copy(r).start()

    loads[0].wait()
    loads[1].wait()
    chunk_at = pl.multiple_of(chunk * (i * 4 + z), 32)
    block_at = pl.multiple_of(chunk_at + block * k, 16)
    parts = [
        w_two[pl.ds(j, block, stride=4), :] * mask_two[pl.ds(j, block, stride=4), :].astype(F32)
        for j in range(4)
    ]
    low = jnp.concatenate(parts[:2], axis=1).astype(BF16)
    high = jnp.concatenate(parts[2:], axis=1).astype(BF16)
    kern[pl.ds(block_at, block), :] = jnp.where(k == 0, low.astype(F32), high.astype(F32)).astype(BF16)
    gk[pl.ds(0, block), :] = jnp.where(k == 0, high.astype(F32), low.astype(F32)).astype(BF16)
    for copy in loads[2:7]:
        copy.wait()
    own_at = pl.multiple_of(own_ch * k, 16)
    filt[pl.ds(own_at, own_ch), :] = (w_one[...] * mask_one[...].astype(F32)).astype(BF16)
    lane = lax.broadcasted_iota(jnp.int32, (1, 128), 1)
    norms = norm_one[...]
    nothing = jnp.zeros_like(norms)
    placed = jnp.where(
        k == 0, jnp.concatenate([norms, nothing], axis=1), jnp.concatenate([nothing, norms], axis=1)
    )
    label_row, weight_row = jnp.zeros((1, 128), F32), jnp.zeros((1, 128), F32)
    for j in range(labels.shape[0]):
        here = lane == labels.shape[0] * c + j
        label_row = jnp.where(here, labels[j].astype(F32), label_row)
        weight_row = jnp.where(here, loss_wt[j].astype(F32), weight_row)
    early[0] = jnp.concatenate(
        [placed, label_row, weight_row, jnp.zeros((4, 128), F32)], axis=0
    )

    pl.semaphore_wait(barrier, len(others))

    k_sib, f_sib, e_sib = new_recv(), new_recv(), new_recv()
    push(gk.at[pl.ds(0, block)], kern.at[pl.ds(block_at, block)], (i, sib), k_sib)
    push(filt.at[pl.ds(own_at, own_ch)], filt.at[pl.ds(own_at, own_ch)], (i, sib), f_sib)
    push(early.at[0], early.at[1], (i, sib), e_sib)

    k_recv = new_recv(32)

    def kern_at(line, dz, u):
        at = chunk * (line * 4 + chip(dz)) + block * (k if u == 0 else 1 - k)
        return kern.at[pl.ds(pl.multiple_of(at, 16), block)]

    k_send, k_count = next(next_send), itertools.count(1)

    def forward(line, dz, u, *devices):
        for device in devices:
            at = k_recv + 2 * (line * 4 + chip(dz)) + u
            start(k_send, at, kern_at(line, dz, u), kern_at(line, dz, u), device)
            next(k_count)

    def landed(line, dz, u):
        arrived(kern_at(line, dz, u), k_recv + 2 * (line * 4 + chip(dz)) + u)

    def relay(line, dz, u, *devices):
        landed(line, dz, u)
        forward(line, dz, u, *devices)

    to_x, to_y = (xn, c), (yn, c)
    to_z = [(i, zdev(dz)) for dz in (1, 2, 3)]
    forward(i, 0, 0, to_x, to_y, *to_z[::-1])
    act_in[0] = jnp.zeros(act_in.shape[1:], BF16)
    for r in range(SIDE + 1, act_in.shape[0]):
        act_in[r] = jnp.zeros(act_in.shape[1:], BF16)
    for r in range(1, SIDE + 1):
        act_in[r, 0] = jnp.zeros(act_in.shape[2:], BF16)
    other_block_at = pl.multiple_of(chunk_at + block * (1 - k), 16)
    arrived(kern.at[pl.ds(other_block_at, block)], k_sib)
    forward(i, 0, 1, to_x, to_y, *to_z[::-1])
    arrived(early.at[1], e_sib)
    both = early[0] + early[1]
    info[z] = both
    i_recv = new_recv()
    push_all([(info.at[z], info.at[z], device) for device in to_z], info.at[pl.ds(0, 3)], i_recv)
    other_at = pl.multiple_of(own_ch * (1 - k), 16)
    arrived(filt.at[pl.ds(other_at, own_ch)], f_sib)

    def first_conv(r, carry):
        sums, squares = carry
        image_copy(r).wait()
        rows = feats[pl.ds(SIDE * r, SIDE)].reshape(rows_a, feats.shape[2])
        out = matmul_nt(rows, filt[...])
        z_one[pl.ds(pl.multiple_of(rows_a * r, 64), rows_a), :] = out
        counted = jnp.where((r == 0) & (k == 1), 0.0, 1.0)
        return (
            sums + counted * jnp.sum(out, axis=0, keepdims=True),
            squares + counted * jnp.sum(out * out, axis=0, keepdims=True),
        )

    zero_row = jnp.zeros((1, chip_ch), F32)
    so_far = lax.fori_loop(0, UPPER // 2, first_conv, (zero_row, zero_row))
    relay(i, 1, 0, to_x, to_y)
    relay(xn, 0, 0, to_y)
    sums, squares = lax.fori_loop(UPPER // 2, UPPER, first_conv, so_far)

    def small_sum(turn, rows):
        own = 2 * i + k
        tiles[turn, own] = rows
        at = new_recv()
        tile, all_others = tiles.at[turn, own], tiles.at[turn, pl.ds(0, 7)]
        push_all([(tile, tile, device) for device in plane], all_others, at)

        def finish():
            arrived(all_others, at)
            result = tiles[turn, 0]
            for n in range(1, 8):
                result = result + tiles[turn, n]
            return result

        return finish

    finish = small_sum(0, jnp.concatenate([sums, squares, jnp.zeros((6, 128), F32)], axis=0))
    for copy in loads[7:]:
        copy.wait()
    for r in range(head_rows):
        first, shift = divmod(classes * r, 128)
        taken = -(-(shift + classes) // 128)
        rows = w_head[first : first + taken, :]
        if taken < 9:
            rows = jnp.concatenate([rows, jnp.zeros((9 - taken, 128), F32)], axis=0)
        if shift:
            rows = pltpu.roll(rows, 128 - shift, 1)
            rows = jnp.where(lane < 128 - shift, rows[:8], rows[1:9])
        for j in range(8):
            head_flat[r : r + 1, 128 * j : 128 * j + 128] = rows[j : j + 1]
    head_lane = lax.broadcasted_iota(jnp.int32, (head_rows, 1024), 1)
    head[i, z, k] = jnp.where(head_lane < classes, head_flat[...], 0.0).astype(BF16)
    relay(xn, 0, 1, to_y)
    relay(i, 2, 0, to_x, to_y)
    relay(i, 1, 1, to_x, to_y)
    relay(xn, 1, 0, to_y)
    totals = finish()
    mean_one = totals[0:1] / count_all
    inv_one = lax.rsqrt(totals[1:2] / count_all - mean_one * mean_one + EPS)
    gain_one, bias_one = both[0:1], both[1:2]

    def first_act(r):
        at = slice(rows_a * r, rows_a * r + rows_a)
        hat = (z_one[at, :] - mean_one) * inv_one
        value, grade = silu_pair(gain_one * hat + bias_one)
        act_out[r] = value.astype(BF16).reshape(SIDE, group, chip_ch)
        counted = jnp.where(k == 1, 0.0, 1.0) if r == 0 else 1.0
        d_one[r] = (counted * hat).astype(BF16).reshape(SIDE, group, chip_ch)

    def hat_products(first, last):
        def step(n, carry):
            at = pl.ds(pl.multiple_of(256 * n, 256), 256)
            rows = feats[:, :, at].reshape(UPPER * rows_a, 256)
            m_two[:, at] = jnp.dot(hat_t[...], rows, preferred_element_type=F32)
            return carry

        lax.fori_loop(first, last, step, 0)

    def into(row, chip_id):
        return act_in.at[
            1 + row, pl.ds(1, SIDE), :, pl.ds(pl.multiple_of(chip_ch * chip_id, 128), chip_ch)
        ]

    def images_of(ref, dz):
        return ref.at[:, :, pl.ds(pl.multiple_of(per_chip * chip(dz), 16), per_chip), :]

    def images_in_row(ref, r, dz):
        return ref.at[r, :, pl.ds(pl.multiple_of(per_chip * chip(dz), 16), per_chip), :]

    def row_copies(r):
        return [
            (images_in_row(act_out, r + k, dz), into(UPPER * k + r, z), to_z[dz - 1])
            for dz in (3, 2, 1)
        ]

    def keep_row(r, n):
        return pltpu.make_async_copy(
            images_in_row(act_out, r, 0), into(h0 + r, z), local_sem.at[n]
        )

    for r in range(UPPER):
        first_act(r)
    a_recv, a_more = new_recv(), new_recv()
    common = SIDE - UPPER
    out_copies = [
        push_all(
            [copy for r in range(common) for copy in row_copies(r)],
            act_out.at[pl.ds(0, 3), :, pl.ds(0, 3 * per_chip)],
            a_recv,
        )
    ]
    more_send = next(next_send)

    def more_copy(dz):
        return pltpu.make_async_remote_copy(
            src_ref=images_in_row(act_out, common, dz),
            dst_ref=into(common, z),
            send_sem=send.at[more_send],
            recv_sem=recv.at[a_more],
            device_id=to_z[dz - 1],
            device_id_type=MESH,
        )

    more_size = act_out.at[0, :, pl.ds(0, 3 * per_chip)]
    more_wait = pltpu.make_async_remote_copy(
        src_ref=more_size,
        dst_ref=more_size,
        send_sem=send.at[more_send],
        recv_sem=recv.at[a_more],
        device_id=(i, sib),
        device_id_type=MESH,
    )

    @pl.when(k == 0)
    def _():
        for dz in (3, 2, 1):
            more_copy(dz).start()
        keep_row(common, common).start()

    kept = [keep_row(r + k, r) for r in range(common)]
    for copy in kept:
        copy.start()
    steps = feats.shape[2] // 256
    relay(i, 3, 0, to_x, to_y)
    relay(i, 2, 1, to_x, to_y)
    relay(xn, 1, 1, to_y)
    hat_t[pl.ds(0, chip_ch), :] = d_one[...].reshape(UPPER * rows_a, chip_ch).T
    place_of = lax.broadcasted_iota(jnp.int32, (16, UPPER * rows_a), 1)
    hat_t[pl.ds(chip_ch, 16), :] = jnp.where(
        place_of < jnp.where(k == 1, rows_a, 0), 0.0, 1.0
    ).astype(BF16)
    relay(yn, 2, 0, to_x)
    hat_products(0, steps // 4)
    relay(yn, 3, 0, to_x)
    relay(i, 3, 1, to_x, to_y)
    hat_products(steps // 4, steps // 2)
    relay(yn, 2, 1, to_x)
    relay(yn, 3, 1, to_x)
    hz_recv = new_recv()
    own_head, line_head = head.at[i, z, k], head.at[i, :, k]
    push_all([(own_head, own_head, device) for device in to_z], head.at[i, pl.ds(0, 3), k], hz_recv)
    hat_products(steps // 2, steps)

    for copy in kept:
        copy.wait()
    arrived(act_out.at[pl.ds(0, 3), :, pl.ds(0, 3 * per_chip)], a_recv)
    a_sib, m_sib = new_recv(), new_recv()
    mine = act_in.at[pl.ds(1 + UPPER * k, common), pl.ds(1, SIDE)]
    push(mine, mine, (i, sib), a_sib)
    m_send = next(next_send)
    middle = pltpu.make_async_remote_copy(
        src_ref=act_in.at[1 + common, pl.ds(1, SIDE)],
        dst_ref=act_in.at[1 + common, pl.ds(1, SIDE)],
        send_sem=send.at[m_send],
        recv_sem=recv.at[m_sib],
        device_id=(i, sib),
        device_id_type=MESH,
    )

    @pl.when(k == 0)
    def _():
        keep_row(common, common).wait()
        more_wait.wait_recv()
        middle.start()

    for line, dz in ((yn, 0), (yn, 1), (xn, 2), (xn, 3), (dg, 0), (dg, 1), (dg, 2), (dg, 3)):
        landed(line, dz, 0)
        landed(line, dz, 1)
    sent.append(size_wait(kern.at[pl.ds(0, block * (next(k_count) - 1))], k_send, k_recv))
    arrived(act_in.at[pl.ds(1 + UPPER * (1 - k), common), pl.ds(1, SIDE)], a_sib)

    @pl.when(k == 1)
    def _():
        middle.wait_recv()

    @pl.when(k == 0)
    def _():
        middle.wait_send()
        more_wait.wait_send()

    hx_recv, hy_recv, hxy_recv, hyx_recv = new_recv(), new_recv(), new_recv(), new_recv()
    arrived(head.at[i, pl.ds(0, 3), k], hz_recv)
    push(line_head, line_head, to_x, hx_recv)
    push(line_head, line_head, to_y, hy_recv)

    arrived(info.at[pl.ds(0, 3)], i_recv)
    slots = info[0] + info[1] + info[2] + info[3]
    gains = jnp.concatenate([info[n, 0:1] for n in range(4)], axis=1)
    biases = jnp.concatenate([info[n, 1:2] for n in range(4)], axis=1)
    spread = math.sqrt(3.0) * gains
    centre = 2.0 / 3.0 * silu_pair(biases)[0] + 1.0 / 6.0 * (
        silu_pair(biases + spread)[0] + silu_pair(biases - spread)[0]
    )
    centre = centre.astype(BF16).astype(F32)

    def tap_of(t):
        return t // 3, t % 3

    def transpose_tap(t):
        kern_t[pl.ds(pl.multiple_of(half * t, 256), half), :] = kern[
            pl.ds(pl.multiple_of(width * t, 512), width), :
        ].T

    def second_conv(h, carry):
        sums, squares = carry
        transpose_tap(h)
        rows = []
        for t in range(TAPS):
            up, left = tap_of(t)
            wide_rows = act_in[pl.ds(h + up, 2)].reshape(2 * PITCH, per_chip, width)
            rows.append(wide_rows[left : left + PITCH].reshape(rows_c, width))
        out = jnp.dot(jnp.concatenate(rows, axis=1), kern[...], preferred_element_type=F32)
        z_two[h] = out.reshape(PITCH, per_chip, half)
        real = out[: SIDE * per_chip]
        return (
            sums + jnp.sum(real, axis=0, keepdims=True),
            squares + jnp.sum(real * real, axis=0, keepdims=True),
        )

    zero_half = jnp.zeros((1, half), F32)
    sums, squares = lax.fori_loop(0, SIDE, second_conv, (zero_half, zero_half))

    def folded(*rows):
        parts = [row[:, n : n + 128] for row in rows for n in range(0, row.shape[1], 128)]
        parts.append(jnp.zeros((8 - len(parts), 128), F32))
        return jnp.concatenate(parts, axis=0)

    def unfolded(tile, n):
        return jnp.concatenate([tile[2 * n : 2 * n + 1], tile[2 * n + 1 : 2 * n + 2]], axis=1)

    def wide_sum(turn, rows):
        own = 4 * i + z
        wide[turn, own] = rows
        at = new_recv()
        tile, all_others = wide.at[turn, own], wide.at[turn, pl.ds(0, 15)]
        push_all([(tile, tile, device) for device in same_core[::-1]], all_others, at)

        def finish():
            arrived(all_others, at)
            result = wide[turn, 0]
            for n in range(1, 16):
                result = result + wide[turn, n]
            return result

        return finish

    chip_weight = jnp.sum(both[3:4], axis=1, keepdims=True)
    finish = wide_sum(0, folded(sums, squares, jnp.broadcast_to(chip_weight, (1, 128))))
    arrived(head.at[xn, :, k], hx_recv)
    half_head = head.at[xn, pl.ds(0, 2), k]
    push(half_head, half_head, to_y, hxy_recv)
    arrived(head.at[yn, :, k], hy_recv)
    half_head = head.at[yn, pl.ds(2, 2), k]
    push(half_head, half_head, to_x, hyx_recv)
    for t in range(SIDE, TAPS):
        transpose_tap(t)
    inner = act_in[pl.ds(1, SIDE + 1)].reshape((SIDE + 1) * PITCH, per_chip, width)
    inner = inner[1 : 1 + SIDE * PITCH].reshape(SIDE * rows_c, width).astype(F32)
    row = lax.broadcasted_iota(jnp.int32, (SIDE * rows_c, 1), 0)
    inner = jnp.where(lax.rem(lax.div(row, per_chip), PITCH) < SIDE, inner - centre, 0.0)
    act_t[...] = inner.astype(BF16).T
    d_pad[pl.ds(0, FRONT)] = jnp.zeros((FRONT, per_chip, half), BF16)
    d_pad[pl.ds(FRONT + SIDE * PITCH, FRONT)] = jnp.zeros((FRONT, per_chip, half), BF16)
    arrived(head.at[dg, pl.ds(0, 2), k], hxy_recv)
    arrived(head.at[dg, pl.ds(2, 2), k], hyx_recv)
    hd_sib = new_recv()
    theirs = head.at[pl.ds(2 * (1 - k), 2), :, k]
    push(theirs, theirs, (i, sib), hd_sib)
    totals_two = finish()
    total = totals_two[4:5, 0:1]
    mean_two = unfolded(totals_two, 0) / count_all
    inv_two = lax.rsqrt(unfolded(totals_two, 1) / count_all - mean_two * mean_two + EPS)
    norms_two = jnp.where(k == 0, norm_two[:, :half], norm_two[:, half:])
    gain_two, bias_two = norms_two[0:1], norms_two[1:2]

    def second_act(h, pooled):
        hat = (z_two[h] - mean_two) * inv_two
        z_two[h] = hat
        value, grade = silu_pair(gain_two * hat + bias_two)
        slope[h] = grade
        return pooled + jnp.sum(value[:SIDE], axis=0)

    pooled = lax.fori_loop(0, SIDE, second_act, jnp.zeros((per_chip, half), F32)) / PIX
    pooled_low = pooled.astype(BF16)

    arrived(head.at[pl.ds(2 * k, 2), :, 1 - k], hd_sib)
    head_half = head[pl.ds(2 * k, 2)].reshape(half, head.shape[4])
    logit[0] = jnp.dot(pooled_low, head_half, preferred_element_type=F32)
    at = new_recv()
    push(logit.at[0], logit.at[1], (i, sib), at)
    image_id = per_chip * z + lax.broadcasted_iota(jnp.int32, (per_chip, group), 0)
    fills = place[...] == image_id
    label = jnp.sum(jnp.where(fills, slots[2:3, :group], 0.0), axis=1, keepdims=True).astype(jnp.int32)
    weight = jnp.sum(jnp.where(fills, slots[3:4, :group], 0.0), axis=1, keepdims=True)
    share = weight / total
    arrived(logit.at[1], at)
    logits = logit[0] + logit[1]
    klass = lax.broadcasted_iota(jnp.int32, logits.shape, 1)
    inside = klass < classes
    top = jnp.max(jnp.where(inside, logits, -jnp.inf), axis=1, keepdims=True)
    expd = jnp.where(inside, jnp.exp(jnp.where(inside, logits - top, 0.0)), 0.0)
    denom = jnp.sum(expd, axis=1, keepdims=True)
    onehot = klass == label
    picked = jnp.sum(jnp.where(onehot, logits, 0.0), axis=1, keepdims=True)
    partial = jnp.sum(share * (top + jnp.log(denom) - picked), axis=0, keepdims=True)
    d_logits = (share * (expd / denom - jnp.where(onehot, 1.0, 0.0))).astype(BF16)
    d_pooled = matmul_nt(d_logits, head_half) / PIX

    def second_back(h, carry):
        sums, products = carry
        d_y = d_pooled[None] * slope[h]
        slope[h] = d_y
        d_y = d_y[:SIDE].reshape(SIDE * per_chip, half)
        hat = z_two[h][:SIDE].reshape(SIDE * per_chip, half)
        return (
            sums + jnp.sum(d_y, axis=0, keepdims=True),
            products + jnp.sum(d_y * hat, axis=0, keepdims=True),
        )

    d_bias, d_gain = lax.fori_loop(0, SIDE, second_back, (zero_half, zero_half))

    finish = wide_sum(1, folded(d_gain, d_bias, jnp.broadcast_to(partial, (1, 128))))
    gh_swap = new_recv()
    gh_half[...] = matmul_tn(pooled_low, d_logits).astype(BF16).reshape(gh_half.shape)
    push(gh_half.at[:, :, 1 - k], gh.at[pl.ds(2 * k, 2)], (i, sib), gh_swap)
    gh[pl.ds(2 * k, 2)] = jnp.where(
        k == 0, gh_half[:, :, 0].astype(F32), gh_half[:, :, 1].astype(F32)
    ).astype(BF16)
    arrived(gh.at[pl.ds(2 * (1 - k), 2)], gh_swap)
    h_one, h_two, h_z = new_recv(4), new_recv(2), new_recv(4)
    for way, first in enumerate((xn, yn)):
        part = pl.ds(2 * way, 2)
        push(gh.at[dg, part], rh_one.at[way, 1], (first, c), h_one + 2 * way + 1)
        push(gh.at[first, part], rh_one.at[way, 0], (first, c), h_one + 2 * way)
    totals_back = finish()
    loss[...] = totals_back[4:5]
    wide_sib[0] = totals_back
    bn_at = new_recv()
    push(wide_sib.at[0], wide_sib.at[1], (i, sib), bn_at)
    scale = gain_two * inv_two
    shift_two, lean_two = unfolded(totals_back, 1) / count_all, unfolded(totals_back, 0) / count_all

    def second_grad(h, carry):
        grad = scale * (slope[h] - shift_two - z_two[h] * lean_two)
        pixel = lax.broadcasted_iota(jnp.int32, grad.shape, 0)
        grad = jnp.where(pixel < SIDE, grad, 0.0)
        d_pad[pl.ds(FRONT + PITCH * h, PITCH)] = grad.astype(BF16)
        return carry

    lax.fori_loop(0, SIDE, second_grad, 0)

    def shifted(t):
        at = FRONT + PITCH + 1 - PITCH * lax.div(t, 3) - lax.rem(t, 3)
        return d_pad[pl.ds(at, SIDE * PITCH)].reshape(SIDE * rows_c, half)

    def kernel_gradient(line):
        def granule(n, carry):
            at = 4 * chunk * line + 128 * n
            tap = lax.div(at, width)
            rows = act_t[pl.ds(pl.multiple_of(at - width * tap, 128), 128), :]
            gk[pl.ds(pl.multiple_of(at, 128), 128), :] = jnp.dot(
                rows, shifted(tap), preferred_element_type=F32
            ).astype(BF16)
            return carry

        lax.fori_loop(0, 4 * chunk // 128, granule, 0)

    def edge_sums():
        maps = d_pad[pl.ds(FRONT, SIDE * PITCH)].astype(F32).reshape(SIDE, PITCH, per_chip, half)
        across = jnp.sum(maps[:, :SIDE], axis=1)
        for left, rows in enumerate((across - maps[:, 0], across, across - maps[:, SIDE - 1])):
            down = jnp.sum(rows, axis=0)
            for up, part in enumerate((down - rows[0], down, down - rows[SIDE - 1])):
                t = 3 * up + left
                edge_rows[t : t + 1] = jnp.sum(part, axis=0, keepdims=True)

    sent.pop(0).wait_send()
    def gk_at(line, dz):
        return gk.at[pl.ds(pl.multiple_of(chunk * (line * 4 + chip(dz)), 32), chunk)]

    whole, first_half, second_half = (0, chunk), (0, block), (block, block)
    units = {
        3: ((whole, xn, yn),),
        2: ((whole, yn, xn),),
        1: ((first_half, xn, yn), (second_half, yn, xn)),
        0: ((first_half, xn, yn), (second_half, yn, xn)),
    }
    one_at = {dz: new_recv(2 * len(units[dz])) for dz in units}
    two_at = {dz: new_recv(len(units[dz])) for dz in units}
    z_at = new_recv(4)
    r_send = next(next_send)
    sent.append(size_wait(gk.at[pl.ds(0, 15 * chunk)], r_send, z_at))

    def rows_of(ref, part):
        return ref.at[pl.ds(part[0], part[1])]

    def gk_part(line, dz, part):
        at = chunk * (line * 4 + chip(dz)) + part[0]
        return gk.at[pl.ds(pl.multiple_of(at, 16), part[1])]

    def start_far(dz):
        for n, (part, first, second) in enumerate(units[dz]):
            into_part = rows_of(rk_one.at[dz, 1], part)
            start(r_send, one_at[dz] + 2 * n + 1, gk_part(dg, dz, part), into_part, (first, c))

    def start_near(dz):
        for n, (part, first, second) in enumerate(units[dz]):
            into_part = rows_of(rk_one.at[dz, 0], part)
            start(r_send, one_at[dz] + 2 * n, gk_part(first, dz, part), into_part, (first, c))

    def start_two(dz):
        for n, (part, first, second) in enumerate(units[dz]):
            came = rows_of(rk_one.at[dz, 1], part)
            arrived(came, one_at[dz] + 2 * n + 1)
            into_k = gk_part(second, dz, part)
            into_k[...] = (into_k[...].astype(F32) + came[...].astype(F32)).astype(BF16)
            start(r_send, two_at[dz] + n, into_k, rows_of(rk_two.at[dz], part), (second, c))

    def plane_done(dz):
        for n, (part, first, second) in enumerate(units[dz]):
            arrived(rows_of(rk_one.at[dz, 0], part), one_at[dz] + 2 * n)
            arrived(rows_of(rk_two.at[dz], part), two_at[dz] + n)
        into_k = gk_at(i, dz)
        sum_k = into_k[...].astype(F32) + rk_one[dz, 0].astype(F32) + rk_two[dz].astype(F32)
        if dz == 0:
            return sum_k
        into_k[...] = sum_k.astype(BF16)
        start(r_send, z_at + z, into_k, rk_z.at[z], to_z[dz - 1])
        return None

    def back_conv(h):
        rows = []
        for t in range(TAPS):
            up, left = tap_of(t)
            at = PITCH * h + FRONT + PITCH + 1 - PITCH * up - left
            rows.append(d_pad[pl.ds(at, PITCH)].reshape(rows_c, half))
        out = jnp.dot(jnp.concatenate(rows, axis=1), kern_t[...], preferred_element_type=F32)
        return out.reshape(PITCH, per_chip, width)[:SIDE]

    d_at, d_send_at = new_recv(), next(next_send)

    def back_theirs(r, carry):
        out = back_conv(h0_other + r)
        d_act[h0_other + r, pl.ds(0, SIDE)] = out
        d_send[r] = out.astype(BF16)
        start(d_send_at, d_at, d_send.at[r], d_recv.at[r], (i, sib))
        return carry

    def channels_of(r, dz):
        return d_recv.at[r, :, :, pl.ds(pl.multiple_of(chip_ch * chip(dz), 128), chip_ch)]

    def back_row(r, at, to):
        d_recv[r] = (d_act[h0 + r, pl.ds(0, SIDE)] + d_recv[r].astype(F32)).astype(BF16)
        for dz in (3, 2, 1):
            start(at, to, channels_of(r, dz), images_in_row(d_one, r, 0), to_z[dz - 1])

    h0_other = (SIDE - UPPER) * (1 - k)
    lax.fori_loop(0, UPPER, back_theirs, 0)
    kernel_gradient(dg)
    start_far(3)
    start_far(2)
    for way, second in enumerate((yn, xn)):
        part = pl.ds(2 * way, 2)
        arrived(rh_one.at[way, 1], h_one + 2 * way + 1)
        gh[second, part] = (gh[second, part].astype(F32) + rh_one[way, 1].astype(F32)).astype(BF16)
        push(gh.at[second, part], rh_two.at[way], (second, c), h_two + way)
    b_recv, b_more = new_recv(), new_recv()
    b_send, b_more_send = next(next_send), next(next_send)

    d_copy = size_wait(d_send, d_send_at, d_at)
    sent.append(d_copy)
    d_act[UPPER * k, pl.ds(0, SIDE)] = back_conv(UPPER * k)
    d_copy.wait_recv()

    def keep_back(r, n):
        return pltpu.make_async_copy(
            channels_of(r, 0), images_in_row(d_one, r, 0), local_sem.at[n]
        )

    @pl.when(k == 0)
    def _():
        back_row(common, b_more_send, b_more)
        keep_back(common, common).start()

    @pl.when(k == 1)
    def _():
        d_one[0] = jnp.zeros(d_one.shape[1:], BF16)

    for r in range(common):
        if r:
            d_act[UPPER * k + r, pl.ds(0, SIDE)] = back_conv(UPPER * k + r)
        back_row(r + k, b_send, b_recv)
    kept = [keep_back(r + k, r) for r in range(common)]
    for copy in kept:
        copy.start()
    back_copy = size_wait(d_one.at[pl.ds(0, 3), :, pl.ds(0, 3 * per_chip)], b_send, b_recv)
    back_more = size_wait(d_one.at[0, :, pl.ds(0, 3 * per_chip)], b_more_send, b_more)
    sent.append(back_copy)
    kernel_gradient(xn)
    start_near(3)
    kernel_gradient(yn)
    start_near(2)

    for way in (0, 1):
        part = pl.ds(2 * way, 2)
        arrived(rh_one.at[way, 0], h_one + 2 * way)
        arrived(rh_two.at[way], h_two + way)
        sum_h = gh[i, part].astype(F32) + rh_one[way, 0].astype(F32) + rh_two[way].astype(F32)
        h_sum[part] = sum_h
        gh[i, part] = sum_h.astype(BF16)
    for dz in (3, 2, 1):
        push(gh.at[i, chip(dz)], rh_z.at[z], (i, zdev(dz)), h_z + z)

    start_two(3)
    start_two(2)
    for dz in (1, 0):
        start_far(dz)
        start_near(dz)
    kernel_gradient(i)
    edge_rows[...] = jnp.zeros(edge_rows.shape, F32)
    edge_sums()
    for copy in kept:
        copy.wait()
    back_copy.wait_recv()

    @pl.when(k == 0)
    def _():
        keep_back(common, common).wait()
        back_more.wait_recv()
        back_more.wait_send()


    def first_back(r, carry):
        sums, products = carry
        at = pl.ds(pl.multiple_of(rows_a * r, 64), rows_a)
        hat = (z_one[at, :] - mean_one) * inv_one
        z_one[at, :] = hat
        _, grade = silu_pair(gain_one * hat + bias_one)
        d_y = d_one[r].reshape(rows_a, chip_ch).astype(F32) * grade
        counted = jnp.where((r == 0) & (k == 1), 0.0, 1.0)
        return (
            sums + counted * jnp.sum(d_y, axis=0, keepdims=True),
            products + counted * jnp.sum(d_y * hat, axis=0, keepdims=True),
        )

    d_bias, d_gain = lax.fori_loop(0, UPPER, first_back, (zero_row, zero_row))
    finish = small_sum(
        1, jnp.concatenate([d_gain, d_bias, jnp.zeros((6, 128), F32)], axis=0)
    )
    edge_at, edge_z_at = new_recv(), new_recv()
    edge_plane[i] = edge_rows[...]
    push_all(
        [(edge_plane.at[i], edge_plane.at[i], (line, c)) for line in lines],
        edge_plane.at[pl.ds(0, 3)],
        edge_at,
    )
    start_two(1)
    start_two(0)
    plane_done(3)
    plane_done(2)
    scale_one = gain_one * inv_one
    near_count = count_all / 8
    shift_near, lean_near = d_bias / near_count, d_gain / near_count

    def first_grad(r, carry):
        at = pl.ds(pl.multiple_of(rows_a * r, 64), rows_a)
        hat = z_one[at, :]
        _, grade = silu_pair(gain_one * hat + bias_one)
        d_y = d_one[r].reshape(rows_a, chip_ch).astype(F32) * grade
        counted = jnp.where((r == 0) & (k == 1), 0.0, 1.0)
        grad = (counted * scale_one) * (d_y - shift_near - hat * lean_near)
        act_out[r] = grad.astype(BF16).reshape(SIDE, group, chip_ch)
        return carry

    for copy in out_copies:
        copy.wait_send()
    sent[:] = [copy for copy in sent if all(copy is not done for done in out_copies)]
    lax.fori_loop(0, UPPER, first_grad, 0)

    grad_t[...] = act_out[...].reshape(UPPER * rows_a, chip_ch).T

    def first_weights(n, carry):
        at = pl.ds(pl.multiple_of(256 * n, 256), 256)
        rows = feats[:, :, at].reshape(UPPER * rows_a, 256)
        g_acc[:, at] = jnp.dot(grad_t[...], rows, preferred_element_type=F32)
        return carry

    part, columns = own_ch // 2, feats.shape[2] // 2
    upper, lower = pl.ds(0, part), pl.ds(part, part)
    sides = [slice(0, columns), slice(columns, 2 * columns)]
    g_at, first_at, second_at = new_recv(2), new_recv(4), new_recv(4)
    for n, side in enumerate(sides):
        lax.fori_loop(columns // 256 * n, columns // 256 * (n + 1), first_weights, 0)
        if n == 0:
            totals_one = finish()
            g_bn_one[...] = jnp.where(k == 0, totals_one[0:2, :own_ch], totals_one[0:2, own_ch:])
            shift_rest = scale_one * (totals_one[1:2] / count_all - shift_near)
            lean_rest = scale_one * (totals_one[0:1] / count_all - lean_near)
            rest = jnp.concatenate([shift_rest, lean_rest, jnp.zeros((6, chip_ch), F32)], axis=0).T
        g_all = (
            g_acc[:, side]
            - rest[:, 0:1] * m_two[chip_ch : chip_ch + 1, side]
            - rest[:, 1:2] * m_two[:chip_ch, side]
        )
        low, high = g_all[:own_ch], g_all[own_ch:]
        go_send[n] = jnp.where(k == 0, high, low).astype(BF16)
        push(go_send.at[n], go_recv.at[n], (i, sib), g_at + n)
        g_one[:, side] = jnp.where(k == 0, low, high)
    for n, side in enumerate(sides):
        arrived(go_recv.at[n], g_at + n)
        ga_send[n] = (g_one[:, side] + go_recv[n].astype(F32)).astype(BF16)
        push(ga_send.at[n, upper], ga_recv.at[n, upper], to_x, first_at + 2 * n)
        push(ga_send.at[n, lower], ga_recv.at[n, lower], to_y, first_at + 2 * n + 1)
    plane_done(1)
    arrived(edge_plane.at[pl.ds(0, 3)], edge_at)
    edge_z[z] = edge_plane[0] + edge_plane[1] + edge_plane[2] + edge_plane[3]
    push_all(
        [(edge_z.at[z], edge_z.at[z], device) for device in to_z], edge_z.at[pl.ds(0, 3)], edge_z_at
    )
    for n in (0, 1):
        arrived(ga_recv.at[n, upper], first_at + 2 * n)
        arrived(ga_recv.at[n, lower], first_at + 2 * n + 1)
        ga_send[2 + n] = (ga_send[n].astype(F32) + ga_recv[n].astype(F32)).astype(BF16)
        push(ga_send.at[2 + n, upper], ga_recv.at[2 + n, upper], to_y, second_at + 2 * n)
        push(ga_send.at[2 + n, lower], ga_recv.at[2 + n, lower], to_x, second_at + 2 * n + 1)

    arrived(edge_z.at[pl.ds(0, 3)], edge_z_at)
    edges = edge_z[0] + edge_z[1] + edge_z[2] + edge_z[3]
    sum_k = plane_done(0)

    for n, side in enumerate(sides):
        arrived(ga_recv.at[2 + n, upper], second_at + 2 * n)
        arrived(ga_recv.at[2 + n, lower], second_at + 2 * n + 1)
        g_one[:, side] = ga_send[2 + n].astype(F32) + ga_recv[2 + n].astype(F32)

    row_at = chunk * (i * 4 + z)
    tap = lax.div(row_at, width)
    edge_rows[...] = edges
    for step in range(2):
        ranked[pl.ds(width * step, width), :] = rank_one(
            centre, edge_rows[pl.ds(lax.rem(tap + step, TAPS), 1)]
        )
    offset = pl.multiple_of(row_at - width * tap, 32)
    sum_k = sum_k + ranked[pl.ds(offset, chunk), :]
    sum_h = h_sum[z]
    for dz in (1, 2, 3):
        arrived(rk_z.at[chip(dz)], z_at + chip(dz))
        arrived(rh_z.at[chip(dz)], h_z + chip(dz))
        sum_k = sum_k + rk_z[chip(dz)].astype(F32)
        sum_h = sum_h + rh_z[chip(dz)].astype(F32)
    head_flat[...] = sum_h
    g_head[...] = jnp.zeros(g_head.shape, F32)
    for r in range(head_rows):
        first, shift = divmod(classes * r, 128)
        rows = jnp.concatenate(
            [head_flat[r : r + 1, 128 * j : 128 * j + 128] for j in range(8)], axis=0
        )
        if shift:
            rows = pltpu.roll(rows, shift, 1)
        count = min(8, g_head.shape[0] - first)
        g_head[first : first + count, :] += jnp.where(lane >= shift, rows, 0.0)[:count]
        count = min(8, g_head.shape[0] - first - 1)
        if shift:
            g_head[first + 1 : first + 1 + count, :] += jnp.where(lane < shift, rows, 0.0)[:count]
    last_send[...] = sum_k
    l_at = new_recv()
    theirs = last_send.at[pl.ds(pl.multiple_of(block * (1 - k), 16), block)]
    push(theirs, last_recv, (i, sib), l_at)
    mine = last_send[pl.ds(pl.multiple_of(block * k, 16), block), :]
    arrived(last_recv, l_at)
    other = last_recv[...]
    for j in range(4):
        lanes = slice(128 * (j % 2), 128 * (j % 2) + 128)
        g_two[pl.ds(j, block, stride=4), :] = jnp.where(
            k == j // 2, mine[:, lanes], other[:, lanes]
        )

    arrived(wide_sib.at[1], bn_at)
    own_bn, other_bn = (
        jnp.concatenate([unfolded(wide_sib[n], 0), unfolded(wide_sib[n], 1)], axis=0) for n in (0, 1)
    )
    g_bn_two[...] = jnp.where(
        k == 0,
        jnp.concatenate([own_bn, other_bn], axis=1),
        jnp.concatenate([other_bn, own_bn], axis=1),
    )
    for copy in sent:
        copy.wait_send()


def update_kernel(rates, *refs):
    take, give = refs[:24], refs[24:]
    rate_one, rate_bn_one, rate_two, rate_bn_two, rate_head = rates
    w, g, m, v, mask, rank = (r[...] for r in take[:6])
    results = sparse_update(w, g * mask.astype(F32), m, v, mask, rank, rate_one)
    for ref, value in zip(give[:5], results):
        ref[...] = value
    w, g, m, v, mask, rank = (r[...] for r in take[6:12])
    results = sparse_update(w, g * mask.astype(F32), m, v, mask, rank, rate_two)
    for ref, value in zip(give[5:10], results):
        ref[...] = value

    @pl.when(pl.program_id(0) == 0)
    def _():
        for n, rate in enumerate((rate_bn_one, rate_bn_two, rate_head)):
            w, g, m, v = (r[...] for r in take[12 + 4 * n : 16 + 4 * n])
            results = dense_update(w, g, m, v, rate)
            for ref, value in zip(give[10 + 3 * n : 13 + 3 * n], results):
                ref[...] = value
        give[19][...] = results[0].astype(BF16)


def fast_shards(
    images_in, labels, loss_wt, placement,
    w_one, mom_one, avg_one, mask_one, rank_one_in, first_norm_params, mom_bn_one, avg_bn_one,
    w_two, mom_two, avg_two, mask_two, rank_two, second_norm_params, mom_bn_two, avg_bn_two,
    w_head, mom_head, avg_head,
):
    n_img, n_ch = lax.axis_size("img"), lax.axis_size("ch")
    group, cin = images_in.shape[0], images_in.shape[2]
    per_core = labels.shape[0]
    per_chip = 2 * per_core
    width = second_norm_params.shape[1]
    half = width // 2
    own_ch = w_one.shape[1]
    chip_ch = 2 * own_ch
    classes = w_head.shape[0] * n_img * n_ch // width
    images = per_core * n_img * n_ch
    head_rows = w_head.shape[0] // classes
    lanes = -(-classes // 512) * 512
    block = w_two.shape[0] // width
    chunk = 2 * block
    flat = (w_two.shape[0] // 128, 128)
    top = [a.reshape(-1, 128) for a in (w_head, mom_head, avg_head)]
    one = [a.T for a in (w_one, mom_one, avg_one, mask_one, rank_one_in)]
    two = [a.reshape(flat) for a in (w_two, mom_two, avg_two, mask_two, rank_two)]
    vmem = pl.BlockSpec(memory_space=pltpu.VMEM)
    hbm = pl.BlockSpec(memory_space=pltpu.HBM)
    v = pltpu.VMEM
    shape = jax.ShapeDtypeStruct
    g_one, g_two, g_head, g_bn_one, g_bn_two, loss = pl.pallas_call(
        functools.partial(step_kernel, (group, per_chip, classes, images)),
        out_shape=(
            shape((own_ch, cin), F32),
            shape(flat, F32),
            shape(top[0].shape, F32),
            shape((2, own_ch), F32),
            shape((2, width), F32),
            shape((1, 128), F32),
        ),
        in_specs=[hbm] * 11,
        out_specs=[vmem] * 6,
        scratch_shapes=[
            v((own_ch, cin), F32),
            v((own_ch, cin), jnp.int32),
            v(flat, F32),
            v(flat, jnp.int32),
            v(top[0].shape, F32),
            v((2, own_ch), F32),
            v((2, width), F32),
            v((1, group), jnp.int32),
            pltpu.SMEM((per_core,), jnp.int32),
            pltpu.SMEM((per_core,), jnp.int32),
            v((UPPER * SIDE, group, cin), BF16),
            v((chip_ch, cin), BF16),
            v((TAPS * width, half), BF16),
            v((4, 4, 2, head_rows, lanes), BF16),
            v((SIDE + 3, PITCH, per_chip, width), BF16),
            v((UPPER, SIDE, group, chip_ch), BF16),
            v((UPPER * SIDE * group, chip_ch), F32),
            v((SIDE, PITCH, per_chip, half), F32),
            v((SIDE, PITCH, per_chip, half), F32),
            v((2 * FRONT + SIDE * PITCH, per_chip, half), BF16),
            v((width, SIDE * PITCH * per_chip), BF16),
            v((SIDE, PITCH, per_chip, width), F32),
            v((UPPER, SIDE, per_chip, width), BF16),
            v((UPPER, SIDE, per_chip, width), BF16),
            v((UPPER, SIDE, group, chip_ch), BF16),
            v((2, 8, 128), F32),
            v((4, 8, 128), F32),
            v((2, 8, 8, 128), F32),
            v((2, 16, 8, 128), F32),
            v((2, 8, 128), F32),
            v((2, per_chip, lanes), F32),
            v((2, 4, 2, head_rows, lanes), BF16),
            v((TAPS * width, half), BF16),
            v((4, 4, head_rows, lanes), BF16),
            v((4, 2, chunk, half), BF16),
            v((2, 2, 2, head_rows, lanes), BF16),
            v((4, chunk, half), BF16),
            v((2, 2, head_rows, lanes), BF16),
            v((4, chunk, half), BF16),
            v((4, head_rows, lanes), BF16),
            v((4, head_rows, lanes), F32),
            v((head_rows, lanes), F32),
            v((chunk, half), F32),
            v((block, half), F32),
            v((16, half), F32),
            v((2 * width, half), F32),
            v((chip_ch, UPPER * SIDE * group), BF16),
            v((chip_ch, cin), F32),
            v((2, own_ch, cin // 2), BF16),
            v((2, own_ch, cin // 2), BF16),
            v((4, own_ch, cin // 2), BF16),
            v((4, own_ch, cin // 2), BF16),
            v((TAPS * half, width), BF16),
            v((chip_ch + 16, UPPER * SIDE * group), BF16),
            v((chip_ch + 16, cin), F32),
            v((4, 16, half), F32),
            v((4, 16, half), F32),
            pltpu.SemaphoreType.DMA((10,)),
            pltpu.SemaphoreType.DMA((UPPER,)),
            pltpu.SemaphoreType.DMA((UPPER + 1,)),
            pltpu.SemaphoreType.DMA((SENDS,)),
            pltpu.SemaphoreType.DMA((RECEIVES,)),
        ],
        compiler_params=pltpu.CompilerParams(
            collective_id=0, has_side_effects=True, vmem_limit_bytes=56 << 20
        ),
        name="step",
    )(
        images_in.transpose(1, 0, 2),
        placement,
        labels,
        loss_wt,
        one[0],
        one[3],
        first_norm_params,
        two[0],
        two[3],
        top[0],
        second_norm_params,
    )
    root = math.sqrt(images)
    steps = 2
    one_spec = pl.BlockSpec((own_ch // steps, cin), lambda n: (n, 0))
    two_spec = pl.BlockSpec((flat[0] // steps, 128), lambda n: (n, 0))
    bno_spec = pl.BlockSpec((2, own_ch), lambda n: (0, 0))
    bnt_spec = pl.BlockSpec((2, width), lambda n: (0, 0))
    top_spec = pl.BlockSpec(top[0].shape, lambda n: (0, 0))
    f_one, f_two = shape(one[0].shape, F32), shape(flat, F32)
    new = pl.pallas_call(
        functools.partial(update_kernel, (1.3 * root, 8.0 * root, 0.25 * root, root, 40.0)),
        grid=(steps,),
        in_specs=[one_spec] * 6 + [two_spec] * 6 + [bno_spec] * 4 + [bnt_spec] * 4 + [top_spec] * 4,
        out_specs=[one_spec] * 5 + [two_spec] * 5 + [bno_spec] * 3 + [bnt_spec] * 3 + [top_spec] * 4,
        out_shape=[f_one] * 3 + [shape(f_one.shape, jnp.int32), shape(f_one.shape, BF16)]
        + [f_two] * 3 + [shape(flat, jnp.int32), shape(flat, BF16)]
        + [shape((2, own_ch), F32)] * 3 + [shape((2, width), F32)] * 3
        + [shape(top[0].shape, F32)] * 3 + [shape(top[0].shape, BF16)],
        compiler_params=pltpu.CompilerParams(vmem_limit_bytes=56 << 20),
        name="update",
    )(
        one[0], g_one, one[1], one[2], one[3], one[4],
        two[0], g_two, two[1], two[2], two[3], two[4],
        first_norm_params, g_bn_one, mom_bn_one, avg_bn_one,
        second_norm_params, g_bn_two, mom_bn_two, avg_bn_two,
        top[0], g_head, top[1], top[2],
    )
    return (
        loss[0, 0],
        *(a.T for a in new[:5]),
        *new[10:13],
        *(a.reshape(-1) for a in new[5:10]),
        *new[13:16],
        *(a.reshape(-1) for a in new[16:20]),
    )


def solution(mesh):
    in_specs = (
        P("img", None, None),
        P(("img", "ch")),
        P(("img", "ch")),
        P("img", None),
        P(None, "ch"),
        P(None, "ch"),
        P(None, "ch"),
        P(None, "ch"),
        P(None, "ch"),
        P(None, "ch"),
        P(None, "ch"),
        P(None, "ch"),
        P(("img", "ch")),
        P(("img", "ch")),
        P(("img", "ch")),
        P(("img", "ch")),
        P(("img", "ch")),
        P(),
        P(),
        P(),
        P(("img", "ch")),
        P(("img", "ch")),
        P(("img", "ch")),
    )
    out_specs = (
        P(),
        P(None, "ch"),
        P(None, "ch"),
        P(None, "ch"),
        P(None, "ch"),
        P(None, "ch"),
        P(None, "ch"),
        P(None, "ch"),
        P(None, "ch"),
        P(("img", "ch")),
        P(("img", "ch")),
        P(("img", "ch")),
        P(("img", "ch")),
        P(("img", "ch")),
        P(),
        P(),
        P(),
        P(("img", "ch")),
        P(("img", "ch")),
        P(("img", "ch")),
        P(("img", "ch")),
    )
    fast = mesh.shape["img"] == 4 and mesh.shape["ch"] == 8
    return jax.shard_map(fast_shards if fast else shards, mesh=mesh, in_specs=in_specs, out_specs=out_specs, check_vma=False)
```

```python
import functools
import itertools
import math

import jax
import jax.numpy as jnp
from jax import lax
from jax.experimental import pallas as pl
from jax.experimental.pallas import tpu as pltpu
from jax.sharding import PartitionSpec as P

SIDE = 7
PIX = 49
DROP = 10
GROW = 10


EPS = 1e-05
MOMENTUM = 0.5


def advance(weight, grad, velocity, rate):
    velocity = MOMENTUM * velocity + grad
    return (weight - rate * (grad + MOMENTUM * velocity), velocity)


def dense_update(weight, grad, velocity, average, rate):
    moved, velocity = advance(weight, grad, velocity, rate)
    return (moved, velocity, 0.5 * average + 0.5 * moved)


def sparse_update(weight, grad, velocity, average, mask, rank, rate):
    moved, velocity = advance(weight, grad, velocity, rate)
    kept = (mask == 1) & (rank >= DROP)
    grown = (mask == 0) & (rank < GROW)
    new_mask = jnp.where(kept | grown, 1, 0).astype(jnp.int32)
    weight = jnp.where(kept, moved, 0.0)
    velocity = jnp.where(kept, velocity, 0.0)
    average = 0.5 * average + 0.5 * weight
    return (weight, velocity, average, new_mask, weight.astype(jnp.bfloat16))


def silu_slope(value):
    sigma = jax.nn.sigmoid(value)
    return sigma * (1.0 + value * (1.0 - sigma))


def apply_batch_norm(z, sums, squares, element_count):
    mean = sums / element_count
    inverse_deviation = lax.rsqrt(squares / element_count - mean * mean + EPS)
    return ((z - mean) * inverse_deviation, inverse_deviation)


def batch_norm_backward(
    norm_gain,
    inverse_deviation,
    output_gradient,
    standardized_input,
    bias_gradient_sum,
    gain_gradient_sum,
    element_count,
):
    return (
        norm_gain
        * inverse_deviation
        * (
            output_gradient
            - bias_gradient_sum / element_count
            - standardized_input * gain_gradient_sum / element_count
        )
    )


def contract_rows(left, right):
    return jnp.einsum("pk,pc->kc", left, right, preferred_element_type=jnp.float32)


def shards(
    images_in,
    labels,
    loss_wt,
    placement,
    w_one,
    mom_one,
    avg_one,
    mask_one,
    rank_one,
    first_norm_params,
    mom_bn_one,
    avg_bn_one,
    w_two,
    mom_two,
    avg_two,
    mask_two,
    rank_two,
    second_norm_params,
    mom_bn_two,
    avg_bn_two,
    w_head,
    mom_head,
    avg_head,
):
    n_img = lax.axis_size("img")
    n_ch = lax.axis_size("ch")
    group = images_in.shape[0]
    element_count = labels.shape[0]
    width = second_norm_params.shape[1]
    classes = w_head.shape[0] * n_img * n_ch // width
    images = element_count * n_img * n_ch
    slot_info = jnp.stack([labels.astype(jnp.float32), loss_wt.astype(jnp.float32)])
    slot_info = lax.all_gather(slot_info, "ch", axis=1, tiled=True)
    own = lax.axis_index("ch") * element_count + jnp.arange(element_count, dtype=jnp.int32)
    fills = placement[0][None, :] == own[:, None]
    labels_f, weights = jnp.sum(jnp.where(fills[None], slot_info[:, None, :], 0.0), axis=2)
    labels = labels_f.astype(jnp.int32)
    kernel_part = (w_two * mask_two.astype(jnp.float32)).astype(jnp.bfloat16)
    kernel = lax.all_gather(kernel_part, ("img", "ch"), axis=0, tiled=True)
    head = lax.all_gather(w_head.astype(jnp.bfloat16), ("img", "ch"), axis=0, tiled=True)
    kernel = kernel.reshape(9 * width, width)
    head = head.reshape(width, classes)
    rows = images_in.transpose(1, 0, 2).reshape(PIX * group, images_in.shape[2])
    filt_one = (w_one * mask_one.astype(jnp.float32)).astype(jnp.bfloat16)
    first_conv_output = jnp.dot(rows, filt_one, preferred_element_type=jnp.float32)
    first_feature_sum, first_squares_sum, total = lax.psum(
        (
            jnp.sum(first_conv_output, axis=0),
            jnp.sum(first_conv_output * first_conv_output, axis=0),
            jnp.sum(slot_info[1]),
        ),
        "img",
    )
    first_element_count = group * PIX * n_img
    first_standardized_input, first_inverse_deviation = apply_batch_norm(
        first_conv_output, first_feature_sum, first_squares_sum, first_element_count
    )
    first_norm_output = first_norm_params[0] * first_standardized_input + first_norm_params[1]
    act = jax.nn.silu(first_norm_output).astype(jnp.bfloat16).reshape(PIX, group, -1)
    act_in = lax.all_to_all(act, "ch", split_axis=1, concat_axis=2, tiled=True)
    padded = jnp.pad(
        act_in.reshape(SIDE, SIDE, element_count, width), ((1, 1), (1, 1), (0, 0), (0, 0))
    )
    patches = jnp.concatenate(
        [
            padded[tap // 3 : tap // 3 + SIDE, tap % 3 : tap % 3 + SIDE].reshape(
                PIX * element_count, width
            )
            for tap in range(9)
        ],
        axis=1,
    )
    second_conv_output = jnp.dot(patches, kernel, preferred_element_type=jnp.float32)
    second_feature_sum, second_squares_sum = lax.psum(
        (
            jnp.sum(second_conv_output, axis=0),
            jnp.sum(second_conv_output * second_conv_output, axis=0),
        ),
        ("img", "ch"),
    )
    second_element_count = images * PIX
    second_standardized_input, second_inverse_deviation = apply_batch_norm(
        second_conv_output, second_feature_sum, second_squares_sum, second_element_count
    )
    second_norm_output = second_norm_params[0] * second_standardized_input + second_norm_params[1]
    pooled = jnp.mean(jax.nn.silu(second_norm_output).reshape(PIX, element_count, width), axis=0)
    pooled_low = pooled.astype(jnp.bfloat16)
    logits = jnp.dot(pooled_low, head, preferred_element_type=jnp.float32)
    top = jnp.max(logits, axis=1, keepdims=True)
    expd = jnp.exp(logits - top)
    denom = jnp.sum(expd, axis=1, keepdims=True)
    lse = top[:, 0] + jnp.log(denom[:, 0])
    onehot = labels[:, None] == jnp.arange(classes, dtype=jnp.int32)[None, :]
    picked = jnp.sum(jnp.where(onehot, logits, 0.0), axis=1)
    share = weights / total
    partial_loss_value = jnp.sum(share * (lse - picked))
    d_logits = (share[:, None] * (expd / denom - onehot.astype(jnp.float32))).astype(jnp.bfloat16)
    g_head = contract_rows(pooled_low, d_logits)
    d_pooled = jnp.einsum("ic,kc->ik", d_logits, head, preferred_element_type=jnp.float32)
    d_act = jnp.broadcast_to(d_pooled[None] / PIX, (PIX, element_count, width)).reshape(
        PIX * element_count, width
    )
    second_output_gradient = d_act * silu_slope(second_norm_output)
    second_shift_bias, second_norm_gain, loss = lax.psum(
        (
            jnp.sum(second_output_gradient, axis=0),
            jnp.sum(second_output_gradient * second_standardized_input, axis=0),
            partial_loss_value,
        ),
        ("img", "ch"),
    )
    second_preact_gradient = batch_norm_backward(
        second_norm_params[0],
        second_inverse_deviation,
        second_output_gradient,
        second_standardized_input,
        second_shift_bias,
        second_norm_gain,
        second_element_count,
    ).astype(jnp.bfloat16)
    d_patches = jnp.einsum(
        "pc,kc->pk", second_preact_gradient, kernel, preferred_element_type=jnp.float32
    )
    d_pad = 0.0
    for tap in range(9):
        piece = d_patches[:, tap * width : (tap + 1) * width].reshape(
            SIDE, SIDE, element_count, width
        )
        up, left = tap // 3, tap % 3
        d_pad = d_pad + jnp.pad(piece, ((up, 2 - up), (left, 2 - left), (0, 0), (0, 0)))
    d_act_in = d_pad[1:-1, 1:-1].astype(jnp.bfloat16).reshape(PIX, element_count, width)
    d_act_one = lax.all_to_all(d_act_in, "ch", split_axis=2, concat_axis=1, tiled=True)
    g_kernel = contract_rows(patches, second_preact_gradient)
    d_act_one = d_act_one.reshape(PIX * group, -1).astype(jnp.float32)
    first_output_gradient = d_act_one * silu_slope(first_norm_output)
    first_shift_bias, first_norm_gain = lax.psum(
        (
            jnp.sum(first_output_gradient, axis=0),
            jnp.sum(first_output_gradient * first_standardized_input, axis=0),
        ),
        "img",
    )
    first_preact_gradient = batch_norm_backward(
        first_norm_params[0],
        first_inverse_deviation,
        first_output_gradient,
        first_standardized_input,
        first_shift_bias,
        first_norm_gain,
        first_element_count,
    ).astype(jnp.bfloat16)
    g_filt = lax.psum(
        contract_rows(rows, first_preact_gradient).astype(jnp.bfloat16), "img"
    ).astype(jnp.float32)
    g_one = g_filt * mask_one.astype(jnp.float32)
    part_two = lax.psum_scatter(
        g_kernel.reshape(-1), ("img", "ch"), tiled=True
    )
    part_head = lax.psum_scatter(
        g_head.reshape(-1), ("img", "ch"), tiled=True
    )
    g_two = part_two * mask_two.astype(jnp.float32)
    root = math.sqrt(images)
    one = sparse_update(w_one, g_one, mom_one, avg_one, mask_one, rank_one, 1.3 * root)
    bno = dense_update(
        first_norm_params,
        jnp.stack([first_norm_gain, first_shift_bias]),
        mom_bn_one,
        avg_bn_one,
        8.0 * root,
    )
    two = sparse_update(w_two, g_two, mom_two, avg_two, mask_two, rank_two, 0.25 * root)
    bnt = dense_update(
        second_norm_params,
        jnp.stack([second_norm_gain, second_shift_bias]),
        mom_bn_two,
        avg_bn_two,
        root,
    )
    top_head = dense_update(w_head, part_head, mom_head, avg_head, 40.0)
    return (
        loss,
        one[0],
        one[1],
        one[2],
        one[3],
        one[4],
        bno[0],
        bno[1],
        bno[2],
        two[0],
        two[1],
        two[2],
        two[3],
        two[4],
        bnt[0],
        bnt[1],
        bnt[2],
        top_head[0],
        top_head[1],
        top_head[2],
        top_head[0].astype(jnp.bfloat16),
    )


F32, BF16 = jnp.float32, jnp.bfloat16
MESH = pl.DeviceIdType.MESH
TAPS = 9
UPPER = (SIDE + 1) // 2
PITCH = SIDE + 1
FRONT = 2 * PITCH
SENDS, RECEIVES = 48, 102


def silu_pair(value):
    sigma = 1.0 / (1.0 + jnp.exp(-value))
    return value * sigma, sigma * (1.0 + value * (1.0 - sigma))


def matmul_nt(left, right):
    return lax.dot_general(left, right, (((1,), (1,)), ((), ())), preferred_element_type=F32)


def matmul_tn(left, right):
    return lax.dot_general(left, right, (((0,), (0,)), ((), ())), preferred_element_type=F32)


def rank_one(row, other):
    first = other.astype(BF16)
    rest = other - first.astype(F32)
    second = rest.astype(BF16)
    third = (rest - second.astype(F32)).astype(BF16)
    place = lax.broadcasted_iota(jnp.int32, (16, other.shape[1]), 0)
    parts = jnp.where(place == 0, first.astype(F32), 0.0)
    parts = jnp.where(place == 1, second.astype(F32), parts)
    parts = jnp.where(place == 2, third.astype(F32), parts)
    rows = jnp.broadcast_to(row, (16, row.shape[1])).astype(BF16)
    return matmul_tn(rows, parts.astype(BF16))


def step_kernel(
    sizes,
    images,
    place_in,
    labels_in,
    loss_wt_in,
    w_one_in,
    mask_one_in,
    norm_one_in,
    w_two_in,
    mask_two_in,
    w_head_in,
    norm_two_in,
    g_one,
    g_two,
    g_head,
    g_bn_one,
    g_bn_two,
    loss,
    w_one,
    mask_one,
    w_two,
    mask_two,
    w_head,
    norm_one,
    norm_two,
    place,
    labels,
    loss_wt,
    feats,
    filt,
    kern,
    head,
    act_in,
    act_out,
    z_one,
    z_two,
    slope,
    d_pad,
    act_t,
    d_act,
    d_send,
    d_recv,
    d_one,
    early,
    info,
    tiles,
    wide,
    wide_sib,
    logit,
    gh_half,
    gk,
    gh,
    rk_one,
    rh_one,
    rk_two,
    rh_two,
    rk_z,
    rh_z,
    h_sum,
    head_flat,
    last_send,
    last_recv,
    edge_rows,
    ranked,
    grad_t,
    g_acc,
    go_send,
    go_recv,
    ga_send,
    ga_recv,
    kern_t,
    hat_t,
    m_two,
    edge_plane,
    edge_z,
    load_sem,
    image_sem,
    local_sem,
    send,
    recv,
):
    group, per_chip, classes, images_in_all = sizes
    width = norm_two.shape[1]
    half = width // 2
    own_ch = w_one.shape[0]
    chip_ch = 2 * own_ch
    block = w_two.shape[0] * 128 // width
    chunk = 2 * block
    head_rows = head.shape[3]
    rows_a = SIDE * group
    rows_c = PITCH * per_chip
    count_all = float(images_in_all * PIX)

    i, c = lax.axis_index("img"), lax.axis_index("ch")
    z, k = lax.div(c, 2), lax.rem(c, 2)
    sib = c + 1 - 2 * k
    xn, yn, dg = i + 1 - 2 * lax.rem(i, 2), lax.rem(i + 2, 4), 3 - i
    lines = (xn, yn, dg)
    near = (z, z + 1 - 2 * lax.rem(z, 2), 2 - lax.div(z, 2), 3 - 3 * lax.div(z, 2))
    h0 = (SIDE - UPPER) * k

    def chip(dz):
        return near[dz]

    def zdev(dz):
        return 2 * chip(dz) + k

    next_send, next_recv = itertools.count(), itertools.count()
    sent = []

    def new_recv(n=1):
        first = next(next_recv)
        for _ in range(n - 1):
            next(next_recv)
        return first

    def push(src, dst, device, to):
        copy = pltpu.make_async_remote_copy(
            src_ref=src,
            dst_ref=dst,
            send_sem=send.at[next(next_send)],
            recv_sem=recv.at[to],
            device_id=device,
            device_id_type=MESH,
        )
        copy.start()
        sent.append(copy)
        return copy

    def push_all(copies, size_of, to):
        at = next(next_send)
        for src, dst, device in copies:
            pltpu.make_async_remote_copy(
                src_ref=src,
                dst_ref=dst,
                send_sem=send.at[at],
                recv_sem=recv.at[to],
                device_id=device,
                device_id_type=MESH,
            ).start()
        group_copy = pltpu.make_async_remote_copy(
            src_ref=size_of,
            dst_ref=size_of,
            send_sem=send.at[at],
            recv_sem=recv.at[to],
            device_id=(i, sib),
            device_id_type=MESH,
        )
        sent.append(group_copy)
        return group_copy

    def start(at, to, src, dst, device):
        pltpu.make_async_remote_copy(
            src_ref=src,
            dst_ref=dst,
            send_sem=send.at[at],
            recv_sem=recv.at[to],
            device_id=device,
            device_id_type=MESH,
        ).start()

    def size_wait(ref, at, to):
        return pltpu.make_async_remote_copy(
            src_ref=ref,
            dst_ref=ref,
            send_sem=send.at[at],
            recv_sem=recv.at[to],
            device_id=(i, sib),
            device_id_type=MESH,
        )

    def arrived(dst, at):
        pltpu.make_async_remote_copy(
            src_ref=dst,
            dst_ref=dst,
            send_sem=send.at[0],
            recv_sem=recv.at[at],
            device_id=(i, sib),
            device_id_type=MESH,
        ).wait_recv()

    def image_copy(r):
        return pltpu.make_async_copy(
            images.at[pl.ds(SIDE * (h0 + r), SIDE)], feats.at[pl.ds(SIDE * r, SIDE)], image_sem.at[r]
        )

    barrier = pltpu.get_barrier_semaphore()
    same_core = [(o, zdev(dz)) for o in (i, *lines) for dz in (0, 1, 2, 3)][1:]
    plane = [(i, sib)] + [(o, d) for o in lines for d in (c, sib)]
    others = plane + same_core[:3]
    for device in others:
        pl.semaphore_signal(barrier, inc=1, device_id=device, device_id_type=MESH)
    loads = [
        pltpu.make_async_copy(src, dst, load_sem.at[n])
        for n, (src, dst) in enumerate(
            (
                (w_two_in, w_two),
                (mask_two_in, mask_two),
                (w_one_in, w_one),
                (mask_one_in, mask_one),
                (norm_one_in, norm_one),
                (labels_in, labels),
                (loss_wt_in, loss_wt),
                (w_head_in, w_head),
                (norm_two_in, norm_two),
                (place_in, place),
            )
        )
    ]
    for copy in loads:
        copy.start()
    for r in range(UPPER):
        image_copy(r).start()

    loads[0].wait()
    loads[1].wait()
    chunk_at = pl.multiple_of(chunk * (i * 4 + z), 32)
    block_at = pl.multiple_of(chunk_at + block * k, 16)
    parts = [
        w_two[pl.ds(j, block, stride=4), :] * mask_two[pl.ds(j, block, stride=4), :].astype(F32)
        for j in range(4)
    ]
    low = jnp.concatenate(parts[:2], axis=1).astype(BF16)
    high = jnp.concatenate(parts[2:], axis=1).astype(BF16)
    kern[pl.ds(block_at, block), :] = jnp.where(k == 0, low.astype(F32), high.astype(F32)).astype(BF16)
    gk[pl.ds(0, block), :] = jnp.where(k == 0, high.astype(F32), low.astype(F32)).astype(BF16)
    for copy in loads[2:7]:
        copy.wait()
    own_at = pl.multiple_of(own_ch * k, 16)
    filt[pl.ds(own_at, own_ch), :] = (w_one[...] * mask_one[...].astype(F32)).astype(BF16)
    lane = lax.broadcasted_iota(jnp.int32, (1, 128), 1)
    norms = norm_one[...]
    nothing = jnp.zeros_like(norms)
    placed = jnp.where(
        k == 0, jnp.concatenate([norms, nothing], axis=1), jnp.concatenate([nothing, norms], axis=1)
    )
    label_row, weight_row = jnp.zeros((1, 128), F32), jnp.zeros((1, 128), F32)
    for j in range(labels.shape[0]):
        here = lane == labels.shape[0] * c + j
        label_row = jnp.where(here, labels[j].astype(F32), label_row)
        weight_row = jnp.where(here, loss_wt[j].astype(F32), weight_row)
    early[0] = jnp.concatenate(
        [placed, label_row, weight_row, jnp.zeros((4, 128), F32)], axis=0
    )

    pl.semaphore_wait(barrier, len(others))

    k_sib, f_sib, e_sib = new_recv(), new_recv(), new_recv()
    push(gk.at[pl.ds(0, block)], kern.at[pl.ds(block_at, block)], (i, sib), k_sib)
    push(filt.at[pl.ds(own_at, own_ch)], filt.at[pl.ds(own_at, own_ch)], (i, sib), f_sib)
    push(early.at[0], early.at[1], (i, sib), e_sib)

    k_recv = new_recv(32)

    def kern_at(line, dz, u):
        at = chunk * (line * 4 + chip(dz)) + block * (k if u == 0 else 1 - k)
        return kern.at[pl.ds(pl.multiple_of(at, 16), block)]

    k_send, k_count = next(next_send), itertools.count(1)

    def forward(line, dz, u, *devices):
        for device in devices:
            at = k_recv + 2 * (line * 4 + chip(dz)) + u
            start(k_send, at, kern_at(line, dz, u), kern_at(line, dz, u), device)
            next(k_count)

    def landed(line, dz, u):
        arrived(kern_at(line, dz, u), k_recv + 2 * (line * 4 + chip(dz)) + u)

    def relay(line, dz, u, *devices):
        landed(line, dz, u)
        forward(line, dz, u, *devices)

    to_x, to_y = (xn, c), (yn, c)
    to_z = [(i, zdev(dz)) for dz in (1, 2, 3)]
    forward(i, 0, 0, to_x, to_y, *to_z[::-1])
    act_in[0] = jnp.zeros(act_in.shape[1:], BF16)
    for r in range(SIDE + 1, act_in.shape[0]):
        act_in[r] = jnp.zeros(act_in.shape[1:], BF16)
    for r in range(1, SIDE + 1):
        act_in[r, 0] = jnp.zeros(act_in.shape[2:], BF16)
    other_block_at = pl.multiple_of(chunk_at + block * (1 - k), 16)
    arrived(kern.at[pl.ds(other_block_at, block)], k_sib)
    forward(i, 0, 1, to_x, to_y, *to_z[::-1])
    arrived(early.at[1], e_sib)
    both = early[0] + early[1]
    info[z] = both
    i_recv = new_recv()
    push_all([(info.at[z], info.at[z], device) for device in to_z], info.at[pl.ds(0, 3)], i_recv)
    other_at = pl.multiple_of(own_ch * (1 - k), 16)
    arrived(filt.at[pl.ds(other_at, own_ch)], f_sib)

    def first_conv(r, carry):
        sums, squares = carry
        image_copy(r).wait()
        rows = feats[pl.ds(SIDE * r, SIDE)].reshape(rows_a, feats.shape[2])
        out = matmul_nt(rows, filt[...])
        z_one[pl.ds(pl.multiple_of(rows_a * r, 64), rows_a), :] = out
        counted = jnp.where((r == 0) & (k == 1), 0.0, 1.0)
        return (
            sums + counted * jnp.sum(out, axis=0, keepdims=True),
            squares + counted * jnp.sum(out * out, axis=0, keepdims=True),
        )

    zero_row = jnp.zeros((1, chip_ch), F32)
    so_far = lax.fori_loop(0, UPPER // 2, first_conv, (zero_row, zero_row))
    relay(i, 1, 0, to_x, to_y)
    relay(xn, 0, 0, to_y)
    sums, squares = lax.fori_loop(UPPER // 2, UPPER, first_conv, so_far)

    def small_sum(turn, rows):
        own = 2 * i + k
        tiles[turn, own] = rows
        at = new_recv()
        tile, all_others = tiles.at[turn, own], tiles.at[turn, pl.ds(0, 7)]
        push_all([(tile, tile, device) for device in plane], all_others, at)

        def finish():
            arrived(all_others, at)
            result = tiles[turn, 0]
            for n in range(1, 8):
                result = result + tiles[turn, n]
            return result

        return finish

    finish = small_sum(0, jnp.concatenate([sums, squares, jnp.zeros((6, 128), F32)], axis=0))
    for copy in loads[7:]:
        copy.wait()
    for r in range(head_rows):
        first, shift = divmod(classes * r, 128)
        taken = -(-(shift + classes) // 128)
        rows = w_head[first : first + taken, :]
        if taken < 9:
            rows = jnp.concatenate([rows, jnp.zeros((9 - taken, 128), F32)], axis=0)
        if shift:
            rows = pltpu.roll(rows, 128 - shift, 1)
            rows = jnp.where(lane < 128 - shift, rows[:8], rows[1:9])
        for j in range(8):
            head_flat[r : r + 1, 128 * j : 128 * j + 128] = rows[j : j + 1]
    head_lane = lax.broadcasted_iota(jnp.int32, (head_rows, 1024), 1)
    head[i, z, k] = jnp.where(head_lane < classes, head_flat[...], 0.0).astype(BF16)
    relay(xn, 0, 1, to_y)
    relay(i, 2, 0, to_x, to_y)
    relay(i, 1, 1, to_x, to_y)
    relay(xn, 1, 0, to_y)
    totals = finish()
    mean_one = totals[0:1] / count_all
    inv_one = lax.rsqrt(totals[1:2] / count_all - mean_one * mean_one + EPS)
    gain_one, bias_one = both[0:1], both[1:2]

    def first_act(r):
        at = slice(rows_a * r, rows_a * r + rows_a)
        hat = (z_one[at, :] - mean_one) * inv_one
        value, grade = silu_pair(gain_one * hat + bias_one)
        act_out[r] = value.astype(BF16).reshape(SIDE, group, chip_ch)
        counted = jnp.where(k == 1, 0.0, 1.0) if r == 0 else 1.0
        d_one[r] = (counted * hat).astype(BF16).reshape(SIDE, group, chip_ch)

    def hat_products(first, last):
        def step(n, carry):
            at = pl.ds(pl.multiple_of(256 * n, 256), 256)
            rows = feats[:, :, at].reshape(UPPER * rows_a, 256)
            m_two[:, at] = jnp.dot(hat_t[...], rows, preferred_element_type=F32)
            return carry

        lax.fori_loop(first, last, step, 0)

    def into(row, chip_id):
        return act_in.at[
            1 + row, pl.ds(1, SIDE), :, pl.ds(pl.multiple_of(chip_ch * chip_id, 128), chip_ch)
        ]

    def images_of(ref, dz):
        return ref.at[:, :, pl.ds(pl.multiple_of(per_chip * chip(dz), 16), per_chip), :]

    def images_in_row(ref, r, dz):
        return ref.at[r, :, pl.ds(pl.multiple_of(per_chip * chip(dz), 16), per_chip), :]

    def row_copies(r):
        return [
            (images_in_row(act_out, r + k, dz), into(UPPER * k + r, z), to_z[dz - 1])
            for dz in (3, 2, 1)
        ]

    def keep_row(r, n):
        return pltpu.make_async_copy(
            images_in_row(act_out, r, 0), into(h0 + r, z), local_sem.at[n]
        )

    for r in range(UPPER):
        first_act(r)
    a_recv, a_more = new_recv(), new_recv()
    common = SIDE - UPPER
    out_copies = [
        push_all(
            [copy for r in range(common) for copy in row_copies(r)],
            act_out.at[pl.ds(0, 3), :, pl.ds(0, 3 * per_chip)],
            a_recv,
        )
    ]
    more_send = next(next_send)

    def more_copy(dz):
        return pltpu.make_async_remote_copy(
            src_ref=images_in_row(act_out, common, dz),
            dst_ref=into(common, z),
            send_sem=send.at[more_send],
            recv_sem=recv.at[a_more],
            device_id=to_z[dz - 1],
            device_id_type=MESH,
        )

    more_size = act_out.at[0, :, pl.ds(0, 3 * per_chip)]
    more_wait = pltpu.make_async_remote_copy(
        src_ref=more_size,
        dst_ref=more_size,
        send_sem=send.at[more_send],
        recv_sem=recv.at[a_more],
        device_id=(i, sib),
        device_id_type=MESH,
    )

    @pl.when(k == 0)
    def _():
        for dz in (3, 2, 1):
            more_copy(dz).start()
        keep_row(common, common).start()

    kept = [keep_row(r + k, r) for r in range(common)]
    for copy in kept:
        copy.start()
    steps = feats.shape[2] // 256
    relay(i, 3, 0, to_x, to_y)
    relay(i, 2, 1, to_x, to_y)
    relay(xn, 1, 1, to_y)
    hat_t[pl.ds(0, chip_ch), :] = d_one[...].reshape(UPPER * rows_a, chip_ch).T
    place_of = lax.broadcasted_iota(jnp.int32, (16, UPPER * rows_a), 1)
    hat_t[pl.ds(chip_ch, 16), :] = jnp.where(
        place_of < jnp.where(k == 1, rows_a, 0), 0.0, 1.0
    ).astype(BF16)
    relay(yn, 2, 0, to_x)
    hat_products(0, steps // 4)
    relay(yn, 3, 0, to_x)
    relay(i, 3, 1, to_x, to_y)
    hat_products(steps // 4, steps // 2)
    relay(yn, 2, 1, to_x)
    relay(yn, 3, 1, to_x)
    hz_recv = new_recv()
    own_head, line_head = head.at[i, z, k], head.at[i, :, k]
    push_all([(own_head, own_head, device) for device in to_z], head.at[i, pl.ds(0, 3), k], hz_recv)
    hat_products(steps // 2, steps)

    for copy in kept:
        copy.wait()
    arrived(act_out.at[pl.ds(0, 3), :, pl.ds(0, 3 * per_chip)], a_recv)
    a_sib, m_sib = new_recv(), new_recv()
    mine = act_in.at[pl.ds(1 + UPPER * k, common), pl.ds(1, SIDE)]
    push(mine, mine, (i, sib), a_sib)
    m_send = next(next_send)
    middle = pltpu.make_async_remote_copy(
        src_ref=act_in.at[1 + common, pl.ds(1, SIDE)],
        dst_ref=act_in.at[1 + common, pl.ds(1, SIDE)],
        send_sem=send.at[m_send],
        recv_sem=recv.at[m_sib],
        device_id=(i, sib),
        device_id_type=MESH,
    )

    @pl.when(k == 0)
    def _():
        keep_row(common, common).wait()
        more_wait.wait_recv()
        middle.start()

    for line, dz in ((yn, 0), (yn, 1), (xn, 2), (xn, 3), (dg, 0), (dg, 1), (dg, 2), (dg, 3)):
        landed(line, dz, 0)
        landed(line, dz, 1)
    sent.append(size_wait(kern.at[pl.ds(0, block * (next(k_count) - 1))], k_send, k_recv))
    arrived(act_in.at[pl.ds(1 + UPPER * (1 - k), common), pl.ds(1, SIDE)], a_sib)

    @pl.when(k == 1)
    def _():
        middle.wait_recv()

    @pl.when(k == 0)
    def _():
        middle.wait_send()
        more_wait.wait_send()

    hx_recv, hy_recv, hxy_recv, hyx_recv = new_recv(), new_recv(), new_recv(), new_recv()
    arrived(head.at[i, pl.ds(0, 3), k], hz_recv)
    push(line_head, line_head, to_x, hx_recv)
    push(line_head, line_head, to_y, hy_recv)

    arrived(info.at[pl.ds(0, 3)], i_recv)
    slots = info[0] + info[1] + info[2] + info[3]
    gains = jnp.concatenate([info[n, 0:1] for n in range(4)], axis=1)
    biases = jnp.concatenate([info[n, 1:2] for n in range(4)], axis=1)
    spread = math.sqrt(3.0) * gains
    centre = 2.0 / 3.0 * silu_pair(biases)[0] + 1.0 / 6.0 * (
        silu_pair(biases + spread)[0] + silu_pair(biases - spread)[0]
    )
    centre = centre.astype(BF16).astype(F32)

    def tap_of(t):
        return t // 3, t % 3

    def transpose_tap(t):
        kern_t[pl.ds(pl.multiple_of(half * t, 256), half), :] = kern[
            pl.ds(pl.multiple_of(width * t, 512), width), :
        ].T

    def second_conv(h, carry):
        sums, squares = carry
        transpose_tap(h)
        rows = []
        for t in range(TAPS):
            up, left = tap_of(t)
            wide_rows = act_in[pl.ds(h + up, 2)].reshape(2 * PITCH, per_chip, width)
            rows.append(wide_rows[left : left + PITCH].reshape(rows_c, width))
        out = jnp.dot(jnp.concatenate(rows, axis=1), kern[...], preferred_element_type=F32)
        z_two[h] = out.reshape(PITCH, per_chip, half)
        real = out[: SIDE * per_chip]
        return (
            sums + jnp.sum(real, axis=0, keepdims=True),
            squares + jnp.sum(real * real, axis=0, keepdims=True),
        )

    zero_half = jnp.zeros((1, half), F32)
    sums, squares = lax.fori_loop(0, SIDE, second_conv, (zero_half, zero_half))

    def folded(*rows):
        parts = [row[:, n : n + 128] for row in rows for n in range(0, row.shape[1], 128)]
        parts.append(jnp.zeros((8 - len(parts), 128), F32))
        return jnp.concatenate(parts, axis=0)

    def unfolded(tile, n):
        return jnp.concatenate([tile[2 * n : 2 * n + 1], tile[2 * n + 1 : 2 * n + 2]], axis=1)

    def wide_sum(turn, rows):
        own = 4 * i + z
        wide[turn, own] = rows
        at = new_recv()
        tile, all_others = wide.at[turn, own], wide.at[turn, pl.ds(0, 15)]
        push_all([(tile, tile, device) for device in same_core[::-1]], all_others, at)

        def finish():
            arrived(all_others, at)
            result = wide[turn, 0]
            for n in range(1, 16):
                result = result + wide[turn, n]
            return result

        return finish

    chip_weight = jnp.sum(both[3:4], axis=1, keepdims=True)
    finish = wide_sum(0, folded(sums, squares, jnp.broadcast_to(chip_weight, (1, 128))))
    arrived(head.at[xn, :, k], hx_recv)
    half_head = head.at[xn, pl.ds(0, 2), k]
    push(half_head, half_head, to_y, hxy_recv)
    arrived(head.at[yn, :, k], hy_recv)
    half_head = head.at[yn, pl.ds(2, 2), k]
    push(half_head, half_head, to_x, hyx_recv)
    for t in range(SIDE, TAPS):
        transpose_tap(t)
    inner = act_in[pl.ds(1, SIDE + 1)].reshape((SIDE + 1) * PITCH, per_chip, width)
    inner = inner[1 : 1 + SIDE * PITCH].reshape(SIDE * rows_c, width).astype(F32)
    row = lax.broadcasted_iota(jnp.int32, (SIDE * rows_c, 1), 0)
    inner = jnp.where(lax.rem(lax.div(row, per_chip), PITCH) < SIDE, inner - centre, 0.0)
    act_t[...] = inner.astype(BF16).T
    d_pad[pl.ds(0, FRONT)] = jnp.zeros((FRONT, per_chip, half), BF16)
    d_pad[pl.ds(FRONT + SIDE * PITCH, FRONT)] = jnp.zeros((FRONT, per_chip, half), BF16)
    arrived(head.at[dg, pl.ds(0, 2), k], hxy_recv)
    arrived(head.at[dg, pl.ds(2, 2), k], hyx_recv)
    hd_sib = new_recv()
    theirs = head.at[pl.ds(2 * (1 - k), 2), :, k]
    push(theirs, theirs, (i, sib), hd_sib)
    totals_two = finish()
    total = totals_two[4:5, 0:1]
    mean_two = unfolded(totals_two, 0) / count_all
    inv_two = lax.rsqrt(unfolded(totals_two, 1) / count_all - mean_two * mean_two + EPS)
    norms_two = jnp.where(k == 0, norm_two[:, :half], norm_two[:, half:])
    gain_two, bias_two = norms_two[0:1], norms_two[1:2]

    def second_act(h, pooled):
        hat = (z_two[h] - mean_two) * inv_two
        z_two[h] = hat
        value, grade = silu_pair(gain_two * hat + bias_two)
        slope[h] = grade
        return pooled + jnp.sum(value[:SIDE], axis=0)

    pooled = lax.fori_loop(0, SIDE, second_act, jnp.zeros((per_chip, half), F32)) / PIX
    pooled_low = pooled.astype(BF16)

    arrived(head.at[pl.ds(2 * k, 2), :, 1 - k], hd_sib)
    head_half = head[pl.ds(2 * k, 2)].reshape(half, head.shape[4])
    logit[0] = jnp.dot(pooled_low, head_half, preferred_element_type=F32)
    at = new_recv()
    push(logit.at[0], logit.at[1], (i, sib), at)
    image_id = per_chip * z + lax.broadcasted_iota(jnp.int32, (per_chip, group), 0)
    fills = place[...] == image_id
    label = jnp.sum(jnp.where(fills, slots[2:3, :group], 0.0), axis=1, keepdims=True).astype(jnp.int32)
    weight = jnp.sum(jnp.where(fills, slots[3:4, :group], 0.0), axis=1, keepdims=True)
    share = weight / total
    arrived(logit.at[1], at)
    logits = logit[0] + logit[1]
    klass = lax.broadcasted_iota(jnp.int32, logits.shape, 1)
    inside = klass < classes
    top = jnp.max(jnp.where(inside, logits, -jnp.inf), axis=1, keepdims=True)
    expd = jnp.where(inside, jnp.exp(jnp.where(inside, logits - top, 0.0)), 0.0)
    denom = jnp.sum(expd, axis=1, keepdims=True)
    onehot = klass == label
    picked = jnp.sum(jnp.where(onehot, logits, 0.0), axis=1, keepdims=True)
    partial = jnp.sum(share * (top + jnp.log(denom) - picked), axis=0, keepdims=True)
    d_logits = (share * (expd / denom - jnp.where(onehot, 1.0, 0.0))).astype(BF16)
    d_pooled = matmul_nt(d_logits, head_half) / PIX

    def second_back(h, carry):
        sums, products = carry
        d_y = d_pooled[None] * slope[h]
        slope[h] = d_y
        d_y = d_y[:SIDE].reshape(SIDE * per_chip, half)
        hat = z_two[h][:SIDE].reshape(SIDE * per_chip, half)
        return (
            sums + jnp.sum(d_y, axis=0, keepdims=True),
            products + jnp.sum(d_y * hat, axis=0, keepdims=True),
        )

    d_bias, d_gain = lax.fori_loop(0, SIDE, second_back, (zero_half, zero_half))

    finish = wide_sum(1, folded(d_gain, d_bias, jnp.broadcast_to(partial, (1, 128))))
    gh_swap = new_recv()
    gh_half[...] = matmul_tn(pooled_low, d_logits).astype(BF16).reshape(gh_half.shape)
    push(gh_half.at[:, :, 1 - k], gh.at[pl.ds(2 * k, 2)], (i, sib), gh_swap)
    gh[pl.ds(2 * k, 2)] = jnp.where(
        k == 0, gh_half[:, :, 0].astype(F32), gh_half[:, :, 1].astype(F32)
    ).astype(BF16)
    arrived(gh.at[pl.ds(2 * (1 - k), 2)], gh_swap)
    h_one, h_two, h_z = new_recv(4), new_recv(2), new_recv(4)
    for way, first in enumerate((xn, yn)):
        part = pl.ds(2 * way, 2)
        push(gh.at[dg, part], rh_one.at[way, 1], (first, c), h_one + 2 * way + 1)
        push(gh.at[first, part], rh_one.at[way, 0], (first, c), h_one + 2 * way)
    totals_back = finish()
    loss[...] = totals_back[4:5]
    wide_sib[0] = totals_back
    bn_at = new_recv()
    push(wide_sib.at[0], wide_sib.at[1], (i, sib), bn_at)
    scale = gain_two * inv_two
    shift_two, lean_two = unfolded(totals_back, 1) / count_all, unfolded(totals_back, 0) / count_all

    def second_grad(h, carry):
        grad = scale * (slope[h] - shift_two - z_two[h] * lean_two)
        pixel = lax.broadcasted_iota(jnp.int32, grad.shape, 0)
        grad = jnp.where(pixel < SIDE, grad, 0.0)
        d_pad[pl.ds(FRONT + PITCH * h, PITCH)] = grad.astype(BF16)
        return carry

    lax.fori_loop(0, SIDE, second_grad, 0)

    def shifted(t):
        at = FRONT + PITCH + 1 - PITCH * lax.div(t, 3) - lax.rem(t, 3)
        return d_pad[pl.ds(at, SIDE * PITCH)].reshape(SIDE * rows_c, half)

    def kernel_gradient(line):
        def granule(n, carry):
            at = 4 * chunk * line + 128 * n
            tap = lax.div(at, width)
            rows = act_t[pl.ds(pl.multiple_of(at - width * tap, 128), 128), :]
            gk[pl.ds(pl.multiple_of(at, 128), 128), :] = jnp.dot(
                rows, shifted(tap), preferred_element_type=F32
            ).astype(BF16)
            return carry

        lax.fori_loop(0, 4 * chunk // 128, granule, 0, unroll=3)

    def edge_sums():
        maps = d_pad[pl.ds(FRONT, SIDE * PITCH)].astype(F32).reshape(SIDE, PITCH, per_chip, half)
        across = jnp.sum(maps[:, :SIDE], axis=1)
        for left, rows in enumerate((across - maps[:, 0], across, across - maps[:, SIDE - 1])):
            down = jnp.sum(rows, axis=0)
            for up, part in enumerate((down - rows[0], down, down - rows[SIDE - 1])):
                t = 3 * up + left
                edge_rows[t : t + 1] = jnp.sum(part, axis=0, keepdims=True)

    sent.pop(0).wait_send()
    def gk_at(line, dz):
        return gk.at[pl.ds(pl.multiple_of(chunk * (line * 4 + chip(dz)), 32), chunk)]

    whole, first_half, second_half = (0, chunk), (0, block), (block, block)
    units = {
        3: ((whole, xn, yn),),
        2: ((whole, yn, xn),),
        1: ((first_half, xn, yn), (second_half, yn, xn)),
        0: ((first_half, xn, yn), (second_half, yn, xn)),
    }
    one_at = {dz: new_recv(2 * len(units[dz])) for dz in units}
    two_at = {dz: new_recv(len(units[dz])) for dz in units}
    z_at = new_recv(4)
    r_send = next(next_send)
    sent.append(size_wait(gk.at[pl.ds(0, 15 * chunk)], r_send, z_at))

    def rows_of(ref, part):
        return ref.at[pl.ds(part[0], part[1])]

    def gk_part(line, dz, part):
        at = chunk * (line * 4 + chip(dz)) + part[0]
        return gk.at[pl.ds(pl.multiple_of(at, 16), part[1])]

    def start_far(dz):
        for n, (part, first, second) in enumerate(units[dz]):
            into_part = rows_of(rk_one.at[dz, 1], part)
            start(r_send, one_at[dz] + 2 * n + 1, gk_part(dg, dz, part), into_part, (first, c))

    def start_near(dz):
        for n, (part, first, second) in enumerate(units[dz]):
            into_part = rows_of(rk_one.at[dz, 0], part)
            start(r_send, one_at[dz] + 2 * n, gk_part(first, dz, part), into_part, (first, c))

    def start_two(dz):
        for n, (part, first, second) in enumerate(units[dz]):
            came = rows_of(rk_one.at[dz, 1], part)
            arrived(came, one_at[dz] + 2 * n + 1)
            into_k = gk_part(second, dz, part)
            into_k[...] = (into_k[...].astype(F32) + came[...].astype(F32)).astype(BF16)
            start(r_send, two_at[dz] + n, into_k, rows_of(rk_two.at[dz], part), (second, c))

    def plane_done(dz):
        for n, (part, first, second) in enumerate(units[dz]):
            arrived(rows_of(rk_one.at[dz, 0], part), one_at[dz] + 2 * n)
            arrived(rows_of(rk_two.at[dz], part), two_at[dz] + n)
        into_k = gk_at(i, dz)
        sum_k = into_k[...].astype(F32) + rk_one[dz, 0].astype(F32) + rk_two[dz].astype(F32)
        if dz == 0:
            return sum_k
        into_k[...] = sum_k.astype(BF16)
        start(r_send, z_at + z, into_k, rk_z.at[z], to_z[dz - 1])
        return None

    def back_conv(h, count):
        lines_in = []
        for n in range(count):
            rows = []
            for t in range(TAPS):
                up, left = tap_of(t)
                at = PITCH * (h + n) + FRONT + PITCH + 1 - PITCH * up - left
                rows.append(d_pad[pl.ds(at, PITCH)].reshape(rows_c, half))
            lines_in.append(jnp.concatenate(rows, axis=1))
        out = jnp.dot(jnp.concatenate(lines_in, axis=0), kern_t[...], preferred_element_type=F32)
        return out.reshape(count, PITCH, per_chip, width)[:, :SIDE]

    d_at, d_send_at = new_recv(), next(next_send)

    def back_theirs(n, carry):
        at = pl.ds(2 * n, 2)
        out = back_conv(h0_other + 2 * n, 2)
        d_act[pl.ds(h0_other + 2 * n, 2), pl.ds(0, SIDE)] = out
        d_send[at] = out.astype(BF16)
        start(d_send_at, d_at, d_send.at[at], d_recv.at[at], (i, sib))
        return carry

    def channels_of(r, dz):
        return d_recv.at[r, :, :, pl.ds(pl.multiple_of(chip_ch * chip(dz), 128), chip_ch)]

    def back_row(r, at, to):
        d_recv[r] = (d_act[h0 + r, pl.ds(0, SIDE)] + d_recv[r].astype(F32)).astype(BF16)
        for dz in (3, 2, 1):
            start(at, to, channels_of(r, dz), images_in_row(d_one, r, 0), to_z[dz - 1])

    h0_other = (SIDE - UPPER) * (1 - k)
    lax.fori_loop(0, UPPER // 2, back_theirs, 0)
    kernel_gradient(dg)
    start_far(3)
    start_far(2)
    for way, second in enumerate((yn, xn)):
        part = pl.ds(2 * way, 2)
        arrived(rh_one.at[way, 1], h_one + 2 * way + 1)
        gh[second, part] = (gh[second, part].astype(F32) + rh_one[way, 1].astype(F32)).astype(BF16)
        push(gh.at[second, part], rh_two.at[way], (second, c), h_two + way)
    b_recv, b_more = new_recv(), new_recv()
    b_send, b_more_send = next(next_send), next(next_send)

    d_copy = size_wait(d_send, d_send_at, d_at)
    sent.append(d_copy)
    d_act[pl.ds(UPPER * k, 2), pl.ds(0, SIDE)] = back_conv(UPPER * k, 2)
    d_copy.wait_recv()

    def keep_back(r, n):
        return pltpu.make_async_copy(
            channels_of(r, 0), images_in_row(d_one, r, 0), local_sem.at[n]
        )

    @pl.when(k == 0)
    def _():
        back_row(common, b_more_send, b_more)
        keep_back(common, common).start()

    @pl.when(k == 1)
    def _():
        d_one[0] = jnp.zeros(d_one.shape[1:], BF16)

    for r in range(common):
        if r == 2:
            d_act[UPPER * k + r, pl.ds(0, SIDE)] = back_conv(UPPER * k + r, 1)[0]
        back_row(r + k, b_send, b_recv)
    kept = [keep_back(r + k, r) for r in range(common)]
    for copy in kept:
        copy.start()
    back_copy = size_wait(d_one.at[pl.ds(0, 3), :, pl.ds(0, 3 * per_chip)], b_send, b_recv)
    back_more = size_wait(d_one.at[0, :, pl.ds(0, 3 * per_chip)], b_more_send, b_more)
    sent.append(back_copy)
    kernel_gradient(xn)
    start_near(3)
    kernel_gradient(yn)
    start_near(2)

    for way in (0, 1):
        part = pl.ds(2 * way, 2)
        arrived(rh_one.at[way, 0], h_one + 2 * way)
        arrived(rh_two.at[way], h_two + way)
        sum_h = gh[i, part].astype(F32) + rh_one[way, 0].astype(F32) + rh_two[way].astype(F32)
        h_sum[part] = sum_h
        gh[i, part] = sum_h.astype(BF16)
    for dz in (3, 2, 1):
        push(gh.at[i, chip(dz)], rh_z.at[z], (i, zdev(dz)), h_z + z)

    start_two(3)
    start_two(2)
    for dz in (1, 0):
        start_far(dz)
        start_near(dz)
    kernel_gradient(i)
    edge_rows[...] = jnp.zeros(edge_rows.shape, F32)
    edge_sums()
    for copy in kept:
        copy.wait()
    back_copy.wait_recv()

    @pl.when(k == 0)
    def _():
        keep_back(common, common).wait()
        back_more.wait_recv()
        back_more.wait_send()


    def first_back(r, carry):
        sums, products = carry
        at = pl.ds(pl.multiple_of(rows_a * r, 64), rows_a)
        hat = (z_one[at, :] - mean_one) * inv_one
        z_one[at, :] = hat
        _, grade = silu_pair(gain_one * hat + bias_one)
        d_y = d_one[r].reshape(rows_a, chip_ch).astype(F32) * grade
        counted = jnp.where((r == 0) & (k == 1), 0.0, 1.0)
        return (
            sums + counted * jnp.sum(d_y, axis=0, keepdims=True),
            products + counted * jnp.sum(d_y * hat, axis=0, keepdims=True),
        )

    d_bias, d_gain = lax.fori_loop(0, UPPER, first_back, (zero_row, zero_row))
    finish = small_sum(
        1, jnp.concatenate([d_gain, d_bias, jnp.zeros((6, 128), F32)], axis=0)
    )
    edge_at, edge_z_at = new_recv(), new_recv()
    edge_plane[i] = edge_rows[...]
    push_all(
        [(edge_plane.at[i], edge_plane.at[i], (line, c)) for line in lines],
        edge_plane.at[pl.ds(0, 3)],
        edge_at,
    )
    start_two(1)
    start_two(0)
    plane_done(3)
    plane_done(2)
    scale_one = gain_one * inv_one
    near_count = count_all / 8
    shift_near, lean_near = d_bias / near_count, d_gain / near_count

    def first_grad(r, carry):
        at = pl.ds(pl.multiple_of(rows_a * r, 64), rows_a)
        hat = z_one[at, :]
        _, grade = silu_pair(gain_one * hat + bias_one)
        d_y = d_one[r].reshape(rows_a, chip_ch).astype(F32) * grade
        counted = jnp.where((r == 0) & (k == 1), 0.0, 1.0)
        grad = (counted * scale_one) * (d_y - shift_near - hat * lean_near)
        act_out[r] = grad.astype(BF16).reshape(SIDE, group, chip_ch)
        return carry

    for copy in out_copies:
        copy.wait_send()
    sent[:] = [copy for copy in sent if all(copy is not done for done in out_copies)]
    lax.fori_loop(0, UPPER, first_grad, 0)

    grad_t[...] = act_out[...].reshape(UPPER * rows_a, chip_ch).T

    def first_weights(n, carry):
        at = pl.ds(pl.multiple_of(256 * n, 256), 256)
        rows = feats[:, :, at].reshape(UPPER * rows_a, 256)
        g_acc[:, at] = jnp.dot(grad_t[...], rows, preferred_element_type=F32)
        return carry

    part, columns = own_ch // 2, feats.shape[2] // 2
    upper, lower = pl.ds(0, part), pl.ds(part, part)
    sides = [slice(0, columns), slice(columns, 2 * columns)]
    g_at, first_at, second_at = new_recv(2), new_recv(4), new_recv(4)
    for n, side in enumerate(sides):
        lax.fori_loop(columns // 256 * n, columns // 256 * (n + 1), first_weights, 0)
        if n == 0:
            totals_one = finish()
            g_bn_one[...] = jnp.where(k == 0, totals_one[0:2, :own_ch], totals_one[0:2, own_ch:])
            shift_rest = scale_one * (totals_one[1:2] / count_all - shift_near)
            lean_rest = scale_one * (totals_one[0:1] / count_all - lean_near)
            rest = jnp.concatenate([shift_rest, lean_rest, jnp.zeros((6, chip_ch), F32)], axis=0).T
        g_all = (
            g_acc[:, side]
            - rest[:, 0:1] * m_two[chip_ch : chip_ch + 1, side]
            - rest[:, 1:2] * m_two[:chip_ch, side]
        )
        low, high = g_all[:own_ch], g_all[own_ch:]
        go_send[n] = jnp.where(k == 0, high, low).astype(BF16)
        push(go_send.at[n], go_recv.at[n], (i, sib), g_at + n)
        g_one[:, side] = jnp.where(k == 0, low, high)
    for n, side in enumerate(sides):
        arrived(go_recv.at[n], g_at + n)
        ga_send[n] = (g_one[:, side] + go_recv[n].astype(F32)).astype(BF16)
        push(ga_send.at[n, upper], ga_recv.at[n, upper], to_x, first_at + 2 * n)
        push(ga_send.at[n, lower], ga_recv.at[n, lower], to_y, first_at + 2 * n + 1)
    plane_done(1)
    arrived(edge_plane.at[pl.ds(0, 3)], edge_at)
    edge_z[z] = edge_plane[0] + edge_plane[1] + edge_plane[2] + edge_plane[3]
    push_all(
        [(edge_z.at[z], edge_z.at[z], device) for device in to_z], edge_z.at[pl.ds(0, 3)], edge_z_at
    )
    for n in (0, 1):
        arrived(ga_recv.at[n, upper], first_at + 2 * n)
        arrived(ga_recv.at[n, lower], first_at + 2 * n + 1)
        ga_send[2 + n] = (ga_send[n].astype(F32) + ga_recv[n].astype(F32)).astype(BF16)
        push(ga_send.at[2 + n, upper], ga_recv.at[2 + n, upper], to_y, second_at + 2 * n)
        push(ga_send.at[2 + n, lower], ga_recv.at[2 + n, lower], to_x, second_at + 2 * n + 1)

    arrived(edge_z.at[pl.ds(0, 3)], edge_z_at)
    edges = edge_z[0] + edge_z[1] + edge_z[2] + edge_z[3]
    sum_k = plane_done(0)

    for n, side in enumerate(sides):
        arrived(ga_recv.at[2 + n, upper], second_at + 2 * n)
        arrived(ga_recv.at[2 + n, lower], second_at + 2 * n + 1)
        g_one[:, side] = ga_send[2 + n].astype(F32) + ga_recv[2 + n].astype(F32)

    row_at = chunk * (i * 4 + z)
    tap = lax.div(row_at, width)
    edge_rows[...] = edges
    for step in range(2):
        ranked[pl.ds(width * step, width), :] = rank_one(
            centre, edge_rows[pl.ds(lax.rem(tap + step, TAPS), 1)]
        )
    offset = pl.multiple_of(row_at - width * tap, 32)
    sum_k = sum_k + ranked[pl.ds(offset, chunk), :]
    sum_h = h_sum[z]
    for dz in (1, 2, 3):
        arrived(rk_z.at[chip(dz)], z_at + chip(dz))
        arrived(rh_z.at[chip(dz)], h_z + chip(dz))
        sum_k = sum_k + rk_z[chip(dz)].astype(F32)
        sum_h = sum_h + rh_z[chip(dz)].astype(F32)
    head_flat[...] = sum_h
    g_head[...] = jnp.zeros(g_head.shape, F32)
    for r in range(head_rows):
        first, shift = divmod(classes * r, 128)
        rows = jnp.concatenate(
            [head_flat[r : r + 1, 128 * j : 128 * j + 128] for j in range(8)], axis=0
        )
        if shift:
            rows = pltpu.roll(rows, shift, 1)
        count = min(8, g_head.shape[0] - first)
        g_head[first : first + count, :] += jnp.where(lane >= shift, rows, 0.0)[:count]
        count = min(8, g_head.shape[0] - first - 1)
        if shift:
            g_head[first + 1 : first + 1 + count, :] += jnp.where(lane < shift, rows, 0.0)[:count]
    last_send[...] = sum_k
    l_at = new_recv()
    theirs = last_send.at[pl.ds(pl.multiple_of(block * (1 - k), 16), block)]
    push(theirs, last_recv, (i, sib), l_at)
    mine = last_send[pl.ds(pl.multiple_of(block * k, 16), block), :]
    arrived(last_recv, l_at)
    other = last_recv[...]
    for j in range(4):
        lanes = slice(128 * (j % 2), 128 * (j % 2) + 128)
        g_two[pl.ds(j, block, stride=4), :] = jnp.where(
            k == j // 2, mine[:, lanes], other[:, lanes]
        )

    arrived(wide_sib.at[1], bn_at)
    own_bn, other_bn = (
        jnp.concatenate([unfolded(wide_sib[n], 0), unfolded(wide_sib[n], 1)], axis=0) for n in (0, 1)
    )
    g_bn_two[...] = jnp.where(
        k == 0,
        jnp.concatenate([own_bn, other_bn], axis=1),
        jnp.concatenate([other_bn, own_bn], axis=1),
    )
    for copy in sent:
        copy.wait_send()


def update_kernel(rates, *refs):
    take, give = refs[:24], refs[24:]
    rate_one, rate_bn_one, rate_two, rate_bn_two, rate_head = rates
    w, g, m, v, mask, rank = (r[...] for r in take[:6])
    results = sparse_update(w, g * mask.astype(F32), m, v, mask, rank, rate_one)
    for ref, value in zip(give[:5], results):
        ref[...] = value
    w, g, m, v, mask, rank = (r[...] for r in take[6:12])
    results = sparse_update(w, g * mask.astype(F32), m, v, mask, rank, rate_two)
    for ref, value in zip(give[5:10], results):
        ref[...] = value

    @pl.when(pl.program_id(0) == 0)
    def _():
        for n, rate in enumerate((rate_bn_one, rate_bn_two, rate_head)):
            w, g, m, v = (r[...] for r in take[12 + 4 * n : 16 + 4 * n])
            results = dense_update(w, g, m, v, rate)
            for ref, value in zip(give[10 + 3 * n : 13 + 3 * n], results):
                ref[...] = value
        give[19][...] = results[0].astype(BF16)


def fast_shards(
    images_in, labels, loss_wt, placement,
    w_one, mom_one, avg_one, mask_one, rank_one_in, first_norm_params, mom_bn_one, avg_bn_one,
    w_two, mom_two, avg_two, mask_two, rank_two, second_norm_params, mom_bn_two, avg_bn_two,
    w_head, mom_head, avg_head,
):
    n_img, n_ch = lax.axis_size("img"), lax.axis_size("ch")
    group, cin = images_in.shape[0], images_in.shape[2]
    per_core = labels.shape[0]
    per_chip = 2 * per_core
    width = second_norm_params.shape[1]
    half = width // 2
    own_ch = w_one.shape[1]
    chip_ch = 2 * own_ch
    classes = w_head.shape[0] * n_img * n_ch // width
    images = per_core * n_img * n_ch
    head_rows = w_head.shape[0] // classes
    lanes = -(-classes // 512) * 512
    block = w_two.shape[0] // width
    chunk = 2 * block
    flat = (w_two.shape[0] // 128, 128)
    top = [a.reshape(-1, 128) for a in (w_head, mom_head, avg_head)]
    one = [a.T for a in (w_one, mom_one, avg_one, mask_one, rank_one_in)]
    two = [a.reshape(flat) for a in (w_two, mom_two, avg_two, mask_two, rank_two)]
    vmem = pl.BlockSpec(memory_space=pltpu.VMEM)
    hbm = pl.BlockSpec(memory_space=pltpu.HBM)
    v = pltpu.VMEM
    shape = jax.ShapeDtypeStruct
    g_one, g_two, g_head, g_bn_one, g_bn_two, loss = pl.pallas_call(
        functools.partial(step_kernel, (group, per_chip, classes, images)),
        out_shape=(
            shape((own_ch, cin), F32),
            shape(flat, F32),
            shape(top[0].shape, F32),
            shape((2, own_ch), F32),
            shape((2, width), F32),
            shape((1, 128), F32),
        ),
        in_specs=[hbm] * 11,
        out_specs=[vmem] * 6,
        scratch_shapes=[
            v((own_ch, cin), F32),
            v((own_ch, cin), jnp.int32),
            v(flat, F32),
            v(flat, jnp.int32),
            v(top[0].shape, F32),
            v((2, own_ch), F32),
            v((2, width), F32),
            v((1, group), jnp.int32),
            pltpu.SMEM((per_core,), jnp.int32),
            pltpu.SMEM((per_core,), jnp.int32),
            v((UPPER * SIDE, group, cin), BF16),
            v((chip_ch, cin), BF16),
            v((TAPS * width, half), BF16),
            v((4, 4, 2, head_rows, lanes), BF16),
            v((SIDE + 3, PITCH, per_chip, width), BF16),
            v((UPPER, SIDE, group, chip_ch), BF16),
            v((UPPER * SIDE * group, chip_ch), F32),
            v((SIDE, PITCH, per_chip, half), F32),
            v((SIDE, PITCH, per_chip, half), F32),
            v((2 * FRONT + SIDE * PITCH, per_chip, half), BF16),
            v((width, SIDE * PITCH * per_chip), BF16),
            v((SIDE, PITCH, per_chip, width), F32),
            v((UPPER, SIDE, per_chip, width), BF16),
            v((UPPER, SIDE, per_chip, width), BF16),
            v((UPPER, SIDE, group, chip_ch), BF16),
            v((2, 8, 128), F32),
            v((4, 8, 128), F32),
            v((2, 8, 8, 128), F32),
            v((2, 16, 8, 128), F32),
            v((2, 8, 128), F32),
            v((2, per_chip, lanes), F32),
            v((2, 4, 2, head_rows, lanes), BF16),
            v((TAPS * width, half), BF16),
            v((4, 4, head_rows, lanes), BF16),
            v((4, 2, chunk, half), BF16),
            v((2, 2, 2, head_rows, lanes), BF16),
            v((4, chunk, half), BF16),
            v((2, 2, head_rows, lanes), BF16),
            v((4, chunk, half), BF16),
            v((4, head_rows, lanes), BF16),
            v((4, head_rows, lanes), F32),
            v((head_rows, lanes), F32),
            v((chunk, half), F32),
            v((block, half), F32),
            v((16, half), F32),
            v((2 * width, half), F32),
            v((chip_ch, UPPER * SIDE * group), BF16),
            v((chip_ch, cin), F32),
            v((2, own_ch, cin // 2), BF16),
            v((2, own_ch, cin // 2), BF16),
            v((4, own_ch, cin // 2), BF16),
            v((4, own_ch, cin // 2), BF16),
            v((TAPS * half, width), BF16),
            v((chip_ch + 16, UPPER * SIDE * group), BF16),
            v((chip_ch + 16, cin), F32),
            v((4, 16, half), F32),
            v((4, 16, half), F32),
            pltpu.SemaphoreType.DMA((10,)),
            pltpu.SemaphoreType.DMA((UPPER,)),
            pltpu.SemaphoreType.DMA((UPPER + 1,)),
            pltpu.SemaphoreType.DMA((SENDS,)),
            pltpu.SemaphoreType.DMA((RECEIVES,)),
        ],
        compiler_params=pltpu.CompilerParams(
            collective_id=0, has_side_effects=True, vmem_limit_bytes=56 << 20
        ),
        name="step",
    )(
        images_in.transpose(1, 0, 2),
        placement,
        labels,
        loss_wt,
        one[0],
        one[3],
        first_norm_params,
        two[0],
        two[3],
        top[0],
        second_norm_params,
    )
    root = math.sqrt(images)
    steps = 2
    one_spec = pl.BlockSpec((own_ch // steps, cin), lambda n: (n, 0))
    two_spec = pl.BlockSpec((flat[0] // steps, 128), lambda n: (n, 0))
    bno_spec = pl.BlockSpec((2, own_ch), lambda n: (0, 0))
    bnt_spec = pl.BlockSpec((2, width), lambda n: (0, 0))
    top_spec = pl.BlockSpec(top[0].shape, lambda n: (0, 0))
    f_one, f_two = shape(one[0].shape, F32), shape(flat, F32)
    new = pl.pallas_call(
        functools.partial(update_kernel, (1.3 * root, 8.0 * root, 0.25 * root, root, 40.0)),
        grid=(steps,),
        in_specs=[one_spec] * 6 + [two_spec] * 6 + [bno_spec] * 4 + [bnt_spec] * 4 + [top_spec] * 4,
        out_specs=[one_spec] * 5 + [two_spec] * 5 + [bno_spec] * 3 + [bnt_spec] * 3 + [top_spec] * 4,
        out_shape=[f_one] * 3 + [shape(f_one.shape, jnp.int32), shape(f_one.shape, BF16)]
        + [f_two] * 3 + [shape(flat, jnp.int32), shape(flat, BF16)]
        + [shape((2, own_ch), F32)] * 3 + [shape((2, width), F32)] * 3
        + [shape(top[0].shape, F32)] * 3 + [shape(top[0].shape, BF16)],
        compiler_params=pltpu.CompilerParams(vmem_limit_bytes=56 << 20),
        name="update",
    )(
        one[0], g_one, one[1], one[2], one[3], one[4],
        two[0], g_two, two[1], two[2], two[3], two[4],
        first_norm_params, g_bn_one, mom_bn_one, avg_bn_one,
        second_norm_params, g_bn_two, mom_bn_two, avg_bn_two,
        top[0], g_head, top[1], top[2],
    )
    return (
        loss[0, 0],
        *(a.T for a in new[:5]),
        *new[10:13],
        *(a.reshape(-1) for a in new[5:10]),
        *new[13:16],
        *(a.reshape(-1) for a in new[16:20]),
    )


def solution(mesh):
    in_specs = (
        P("img", None, None),
        P(("img", "ch")),
        P(("img", "ch")),
        P("img", None),
        P(None, "ch"),
        P(None, "ch"),
        P(None, "ch"),
        P(None, "ch"),
        P(None, "ch"),
        P(None, "ch"),
        P(None, "ch"),
        P(None, "ch"),
        P(("img", "ch")),
        P(("img", "ch")),
        P(("img", "ch")),
        P(("img", "ch")),
        P(("img", "ch")),
        P(),
        P(),
        P(),
        P(("img", "ch")),
        P(("img", "ch")),
        P(("img", "ch")),
    )
    out_specs = (
        P(),
        P(None, "ch"),
        P(None, "ch"),
        P(None, "ch"),
        P(None, "ch"),
        P(None, "ch"),
        P(None, "ch"),
        P(None, "ch"),
        P(None, "ch"),
        P(("img", "ch")),
        P(("img", "ch")),
        P(("img", "ch")),
        P(("img", "ch")),
        P(("img", "ch")),
        P(),
        P(),
        P(),
        P(("img", "ch")),
        P(("img", "ch")),
        P(("img", "ch")),
        P(("img", "ch")),
    )
    fast = mesh.shape["img"] == 4 and mesh.shape["ch"] == 8
    return jax.shard_map(fast_shards if fast else shards, mesh=mesh, in_specs=in_specs, out_specs=out_specs, check_vma=False)
```
